128 devices in a mesh: group: 2 (over y_lo), replica: 64 (over y_hi, x, z, core).
Axes of the slice: x: 4, y: 4 (y_hi: 2, y_lo: 2; y = y_hi * 2 + y_lo), z: 4, core: 2. Of those that a mesh axis runs over, the one named last changes fastest.
Arguments:
- block_input: bfloat16 [16384, 1024], P(('group', 'replica')), may hold values from -6 to 6
- segment_ids: int32 [128, 128], P(('group', 'replica')), may hold values from 0 to 2, as said below
- ln1_gain: bfloat16 [1024], P('group'), may hold values from 0.5 to 1.5
- ln1_bias: bfloat16 [1024], P('group'), may hold values from -1.75 to 1.75
- w_qkv: bfloat16 [1024, 3072], P('group'), may hold values from -0.1875 to 0.1875
- b_query: bfloat16 [1024], P('group'), may hold values from -1.75 to 1.75
- b_value: bfloat16 [1024], P('group'), may hold values from -1.75 to 1.75
- w_out: bfloat16 [1024, 1024], P('group'), may hold values from -0.75 to 0.75
- b_out: bfloat16 [1024], P('group'), may hold values from -1.75 to 1.75
- ln2_gain: bfloat16 [1024], P('group'), may hold values from 0.5 to 1.5
- ln2_bias: bfloat16 [1024], P('group'), may hold values from -1.75 to 1.75
- w_fc: bfloat16 [1024, 4096], P('group'), may hold values from -0.1875 to 0.1875
- b_fc: bfloat16 [4096], P('group'), may hold values from -1.75 to 1.75
- w_proj: bfloat16 [4096, 1024], P('group'), may hold values from -0.09375 to 0.09375
- b_proj: bfloat16 [1024], P('group'), may hold values from -1.75 to 1.75
- cotangent: bfloat16 [16384, 1024], P(('group', 'replica')), may hold values from -6 to 6
Outputs:
- layer_output: bfloat16 [16384, 1024], P(('group', 'replica'))
- input_grad: float32 [16384, 1024], P(('group', 'replica'))
- ln1_gain_grad: float32 [1024], P('group')
- ln1_bias_grad: float32 [1024], P('group')
- w_qkv_grad: float32 [1024, 3072], P('group')
- b_query_grad: float32 [1024], P('group')
- b_value_grad: float32 [1024], P('group')
- w_out_grad: float32 [1024, 1024], P('group')
- b_out_grad: float32 [1024], P('group')
- ln2_gain_grad: float32 [1024], P('group')
- ln2_bias_grad: float32 [1024], P('group')
- w_fc_grad: float32 [1024, 4096], P('group')
- b_fc_grad: float32 [4096], P('group')
- w_proj_grad: float32 [4096, 1024], P('group')
- b_proj_grad: float32 [1024], P('group')
The draws below stay inside these ranges and needn't reach their ends.
Inputs may be any that keep to these rules, and one draw needn't show every extreme that they name: Each row of segment_ids (one sequence) holds three documents numbered 0, 1, 2 in order, each of 25 tokens or more.
All inputs are finite; a program needn't handle non-finite values.
Results may differ from the reference program's by a relative error of at most 0.014.
Values may be sent and summed in bfloat16 or wider, within the bound.
No kernel may reach another device: no remote copies, remote signals or barrier semaphores. Data moves between devices by JAX's collectives and lax.ppermute only.
A program may use at most 256 MiB of HBM per device.

```python
import math
import jax
import jax.numpy as jnp
from jax import lax

D = 1024
HEADS = 16
FF = 4096
TOK_DEV = 128
HEAD_DIM = 64
SEQS = 128
TOKENS = 16384


def draw_segment_ids(key, part):
    key = jax.random.fold_in(key, 7)
    first_key, second_key = jax.random.split(key)
    smallest = TOK_DEV // 5
    first_length = jax.random.randint(first_key, (SEQS, 1), smallest, TOK_DEV // 2 + 1)
    room = TOK_DEV - first_length - smallest - smallest + 1
    spread_bits = jax.random.randint(second_key, (SEQS, 1), 0, 1048576)
    second_length = smallest + spread_bits % room
    positions = jnp.arange(TOK_DEV, dtype=jnp.int32)[None, :]
    first_end = first_length.astype(jnp.int32)
    second_end = (first_length + second_length).astype(jnp.int32)
    return (positions >= first_end).astype(jnp.int32) + (positions >= second_end).astype(jnp.int32)


def shard_levels(key, dims, cuts, low, top_value):
    def one(dim, blocks):
        heights = jax.random.uniform(jax.random.fold_in(jax.random.fold_in(key, 6), dim), (blocks,), jnp.float32, low / len(cuts), top_value / len(cuts))
        return jnp.repeat(jnp.exp(heights), dims[dim] // blocks).reshape((-1,) + (1,) * (len(dims) - dim - 1))

    loudness = one(*cuts[0])
    for cut in cuts[1:]:
        loudness = loudness * one(*cut)
    return loudness


def noise(key, dims, spread, reach, cuts=(), kind=jnp.bfloat16):
    gain = shard_levels(key, dims, cuts, -0.22, 0.18) if cuts else 1.0
    drawn = jax.random.normal(key, dims, jnp.float32) * spread * gain
    return jnp.minimum(jnp.maximum(drawn, -reach), reach).astype(kind)


def setup_inputs(seed: int = 0) -> dict:
    streams_of = jax.random.split(jax.random.key(seed), 17)
    block_input = noise(streams_of[0], (TOKENS, D), 1.0, 6.0, ((0, 128),))
    segment_ids = draw_segment_ids(jax.random.fold_in(streams_of[16], 71), 0)
    ln1_gain = jnp.clip(1.0 + 0.1 * jax.random.normal(streams_of[2], (D,), jnp.float32), 0.5, 1.5).astype(jnp.bfloat16)
    ln1_bias = noise(streams_of[3], (D,), 0.3, 1.75, ((0, 2),))
    w_qkv = noise(streams_of[4], (D, 3 * D), D ** -0.5, 0.1875, ((0, 2),))
    b_query = noise(streams_of[5], (D,), 0.3, 1.75, ((0, 2),))
    b_value = noise(streams_of[6], (D,), 0.3, 1.75, ((0, 2),))
    w_out = noise(streams_of[7], (D, D), (D // 16) ** -0.5, 0.75, ((0, 2),))
    b_out = noise(streams_of[8], (D,), 0.3, 1.75, ((0, 2),))
    ln2_gain = jnp.clip(1.0 + 0.1 * jax.random.normal(streams_of[9], (D,), jnp.float32), 0.5, 1.5).astype(jnp.bfloat16)
    ln2_bias = noise(streams_of[10], (D,), 0.3, 1.75, ((0, 2),))
    w_fc = noise(streams_of[11], (D, FF), D ** -0.5, 0.1875, ((0, 2),))
    b_fc = noise(streams_of[12], (FF,), 0.3, 1.75, ((0, 2),))
    w_proj = noise(streams_of[13], (FF, D), FF ** -0.5, 0.09375, ((0, 2),))
    b_proj = noise(streams_of[14], (D,), 0.3, 1.75, ((0, 2),))
    cotangent = noise(streams_of[15], (TOKENS, D), 1.0, 6.0, ((0, 128),))
    return {"block_input": block_input, "segment_ids": segment_ids, "ln1_gain": ln1_gain, "ln1_bias": ln1_bias, "w_qkv": w_qkv, "b_query": b_query, "b_value": b_value, "w_out": w_out, "b_out": b_out, "ln2_gain": ln2_gain, "ln2_bias": ln2_bias, "w_fc": w_fc, "b_fc": b_fc, "w_proj": w_proj, "b_proj": b_proj, "cotangent": cotangent}


@jax.custom_vjp
def low(v):
    return lax.optimization_barrier(v.astype(jnp.bfloat16)).astype(jnp.float32)

@jax.custom_vjp
def low_back(v):
    return v

def low_keep(v):
    return (low(v), None)

def low_pass(kept, grad):
    return (grad,)

def back_keep(v):
    return (v, None)

def back_low(kept, grad):
    return (low(grad),)
low.defvjp(low_keep, low_pass)
low_back.defvjp(back_keep, back_low)
norm_epsilon = 1e-05
masked_score = -1e+30
gelu_factor = 0.7978845608028654

def precise_dot(left_matrix, right_matrix):
    return jnp.dot(left_matrix, right_matrix, precision=lax.Precision.HIGHEST)

def layer_norm(values, norm_gain, norm_shift):
    center = lax.optimization_barrier(jnp.mean(values, axis=-1, keepdims=True))
    centered = values - center
    variance = lax.optimization_barrier(jnp.mean(centered * centered, axis=-1, keepdims=True))
    return centered * lax.rsqrt(variance + norm_epsilon) * norm_gain + norm_shift

def gelu_tanh(values):
    return 0.5 * values * (1.0 + jnp.tanh(gelu_factor * (values + 0.044715 * values * values * values)))

def attention(projected, segments):
    seq_count = projected.shape[0]
    seq_length = projected.shape[1]
    head_shape = (seq_count, seq_length, HEADS, HEAD_DIM)
    queries = projected[..., :D].reshape(head_shape)
    key_heads = projected[..., D:2 * D].reshape(head_shape)
    value_heads = projected[..., 2 * D:].reshape(head_shape)
    scores = jnp.einsum('bqhd,bkhd->bhqk', queries, key_heads, precision=lax.Precision.HIGHEST) * (1.0 / math.sqrt(HEAD_DIM))
    scores = low_back(scores)
    positions = jnp.arange(seq_length)
    causal = (positions[:, None] >= positions[None, :])[None, None]
    allowed = causal & (segments[:, None, :, None] == segments[:, None, None, :])
    scores = jnp.where(allowed, scores, masked_score)
    largest = lax.optimization_barrier(jnp.max(scores, axis=-1, keepdims=True))
    weights = jnp.exp(scores - largest)
    softmax_weights = weights / lax.optimization_barrier(jnp.sum(weights, axis=-1, keepdims=True))
    mixture = jnp.einsum('bhqk,bkhd->bqhd', low(softmax_weights), value_heads, precision=lax.Precision.HIGHEST)
    return mixture.reshape(seq_count, seq_length, D)

def forward(inputs, parameters, segments):
    gain_one, shift_one, qkv_weight, query_bias, value_bias, out_weight, out_bias, gain_two, shift_two, fc_weight, fc_bias, proj_weight, proj_bias = parameters
    normed_one = low(layer_norm(inputs, gain_one, shift_one))
    bias_full = jnp.concatenate([query_bias, jnp.zeros_like(query_bias), value_bias])
    projected = low(low_back(precise_dot(normed_one, qkv_weight) + bias_full))
    mixture = low(low_back(attention(projected, segments)))
    residual = inputs + low_back(precise_dot(mixture, out_weight)) + out_bias
    normed_two = low(layer_norm(residual, gain_two, shift_two))
    hidden_pre = low_back(precise_dot(normed_two, fc_weight) + fc_bias)
    hidden = low(gelu_tanh(hidden_pre))
    return residual + low_back(precise_dot(hidden, proj_weight)) + proj_bias

def reference(block_input, segment_ids, ln1_gain, ln1_bias, w_qkv, b_query, b_value, w_out, b_out, ln2_gain, ln2_bias, w_fc, b_fc, w_proj, b_proj, cotangent):
    parameters = tuple((array.astype(jnp.float32) for array in (ln1_gain, ln1_bias, w_qkv, b_query, b_value, w_out, b_out, ln2_gain, ln2_bias, w_fc, b_fc, w_proj, b_proj)))
    per_step = math.gcd(SEQS, max(1, 2048 // TOK_DEV))
    step_count = SEQS // per_step
    inputs = block_input.astype(jnp.float32).reshape(step_count, per_step, TOK_DEV, D)
    segments = segment_ids.reshape(step_count, per_step, TOK_DEV)
    cotangents = cotangent.astype(jnp.float32).reshape(step_count, per_step, TOK_DEV, D)

    def one_step(totals, block):
        block_rows, block_segments, block_cotangent = block

        def local_forward(layer_in, layer_parameters):
            return forward(layer_in, layer_parameters, block_segments)
        result, pullback = jax.vjp(local_forward, block_rows, parameters)
        grad_in, grad_parameters = pullback(block_cotangent)
        totals = jax.tree.map(jnp.add, totals, grad_parameters)
        return (totals, (result.astype(jnp.bfloat16), grad_in))
    zeros_start = jax.tree.map(jnp.zeros_like, parameters)
    totals, (outputs, grad_inputs) = lax.scan(one_step, zeros_start, (inputs, segments, cotangents))
    return (outputs.reshape(TOKENS, D), grad_inputs.reshape(TOKENS, D), totals[0], totals[1], totals[2], totals[3], totals[4], totals[5], totals[6], totals[7], totals[8], totals[9], totals[10], totals[11], totals[12])
```

```python
import math

import jax
import jax.numpy as jnp
from jax import lax
from jax.experimental import pallas as pl
from jax.experimental.pallas import tpu as pltpu
from jax.sharding import PartitionSpec as P

D = 1024
HEADS = 16
HEAD_DIM = 64
FF = 4096
ROWS = 128

norm_epsilon = 1e-05
masked_score = -1e30
gelu_factor = 0.7978845608028654

f32 = jnp.float32
bf16 = jnp.bfloat16
AXES = ("group", "replica")


def flat(g, yh, x, z, c):
    return (((g * 2 + yh) * 4 + x) * 4 + z) * 2 + c


def exchange(move):
    pairs = []
    for g in range(2):
        for yh in range(2):
            for x in range(4):
                for z in range(4):
                    for c in range(2):
                        pairs.append((flat(g, yh, x, z, c), move(2 * yh + g, x, z, c)))
    return pairs


def at(y, x, z, c):
    return flat(y % 2, y // 2, x, z, c)


FIRST = {
    "g": exchange(lambda y, x, z, c: at(y ^ (1, 3)[c], x, z, c)),
    "x": exchange(lambda y, x, z, c: at(y, x ^ (1, 3)[c], z, c)),
    "z": exchange(lambda y, x, z, c: at(y, x, z ^ (1, 3)[c], c)),
}
SECOND = {
    "x": exchange(lambda y, x, z, c: at(y, x ^ (3, 1)[c], z, c)),
    "z": exchange(lambda y, x, z, c: at(y, x, z ^ (3, 1)[c], c)),
}
FAR = exchange(lambda y, x, z, c: at(y ^ 2, x, z, c))
CORE = exchange(lambda y, x, z, c: at(y, x, z, c ^ 1))


def swap(array, pairs):
    return lax.ppermute(array, AXES, pairs)


class Place:
    def __init__(self):
        self.g = lax.axis_index("group")
        replica = lax.axis_index("replica")
        self.c = replica % 2
        x = (replica // 8) % 4
        z = (replica // 2) % 4
        x_bits = ((x % 2) ^ (x // 2), x // 2)
        z_bits = ((z % 2) ^ (z // 2), z // 2)
        first = self.c == 0

        def order(bits):
            return jnp.where(first, bits[0], bits[1]), jnp.where(first, bits[1], bits[0])

        self.ux, self.vx = order(x_bits)
        self.uz, self.vz = order(z_bits)

    def block(self, gx, bx, bz):
        return ((gx ^ self.g) * 2 + (bx ^ self.ux)) * 2 + (bz ^ self.uz)


def grad_blocks(pairs, columns, block, received):
    count = columns.shape[0]
    tokens = pairs[0][0].shape[0]
    widths = [right.shape[1] for _, right in pairs]
    width = sum(widths)
    n = len(pairs)

    def kernel(columns_ref, *refs):
        out_ref = refs[-1]
        extra = refs[2 * n : -1]
        offset = 0
        for k in range(n):
            term = lax.dot_general(
                refs[2 * k][...], refs[2 * k + 1][...], (((0,), (0,)), ((), ())), preferred_element_type=f32
            )
            span = slice(offset, offset + widths[k])
            for ref in extra:
                term = term + ref[:, span].astype(f32)
            out_ref[:, span] = term.astype(bf16)
            offset += widths[k]

    def shifted(first):
        return lambda j, cols: (first + j, 0)

    in_specs = []
    operands = []
    for left, right in pairs:
        in_specs.append(pl.BlockSpec((tokens, block), lambda j, cols: (0, cols[j])))
        in_specs.append(pl.BlockSpec(right.shape, lambda j, cols: (0, 0)))
        operands += [left, right]
    for array, first in received:
        in_specs.append(pl.BlockSpec((block, width), shifted(first)))
        operands.append(array)
    rows = count * block
    return pl.pallas_call(
        kernel,
        grid_spec=pltpu.PrefetchScalarGridSpec(
            num_scalar_prefetch=1,
            grid=(count,),
            in_specs=in_specs,
            out_specs=pl.BlockSpec((block, width), lambda j, cols: (j, 0)),
        ),
        out_shape=jax.ShapeDtypeStruct((rows, width), bf16),
        compiler_params=pltpu.CompilerParams(vmem_limit_bytes=40 * 2**20),
        cost_estimate=pl.CostEstimate(
            flops=2 * tokens * rows * width,
            bytes_accessed=2 * rows * width * (1 + len(received)) + 4 * tokens * width,
            transcendentals=0,
        ),
    )(columns, *operands)


def reduce_part(place, pairs, order, block):
    def columns(*steps):
        rows = []
        for step in steps:
            away = dict(zip(order, step))
            rows.append(place.block(away["g"], away["x"], away["z"]))
        return jnp.stack(rows).astype(jnp.int32)

    first = swap(
        grad_blocks(pairs, columns((1, 0, 0), (1, 0, 1), (1, 1, 0), (1, 1, 1)), block, []), FIRST[order[0]]
    )
    second = swap(
        grad_blocks(pairs, columns((0, 1, 0), (0, 1, 1)), block, [(first, 2)]), FIRST[order[1]]
    )
    third = swap(
        grad_blocks(pairs, columns((0, 0, 1)), block, [(first, 1), (second, 1)]), FIRST[order[2]]
    )
    total = grad_blocks(pairs, columns((0, 0, 0)), block, [(first, 0), (second, 0), (third, 0)])
    late = [name for name in order if name != "g"]
    own = {"x": place.vx, "z": place.vz}
    for name in late:
        half = total.shape[0] // 2
        sent = lax.dynamic_slice_in_dim(total, (1 - own[name]) * half, half, 0)
        kept = lax.dynamic_slice_in_dim(total, own[name] * half, half, 0)
        total = (kept.astype(f32) + swap(sent, SECOND[name]).astype(f32)).astype(bf16)
    total = (total.astype(f32) + swap(total, FAR).astype(f32)).astype(bf16)
    return total


def gather_part(place, total, order):
    late = [name for name in order if name != "g"]
    own = {"x": place.vx, "z": place.vz}
    for name in reversed(late):
        other = swap(total, SECOND[name])
        total = jnp.where(
            own[name] == 0, jnp.concatenate([total, other], 0), jnp.concatenate([other, total], 0)
        )
    for name in reversed(late):
        total = jnp.concatenate([total, swap(total, FIRST[name])], 0)
    return total


def source_blocks(place, order, core):
    same = core == place.c
    ux = jnp.where(same, place.ux, place.vx)
    uz = jnp.where(same, place.uz, place.vz)
    late = [name for name in order if name != "g"]
    rows = []
    for bx in range(2):
        for bz in range(2):
            away = {"x": bx ^ ux, "z": bz ^ uz}
            rows.append(away[late[0]] * 2 + away[late[1]])
    return rows


def unpack_rows(place, mine, theirs, order, block):
    width = mine.shape[1]
    first = place.c == 0
    own = source_blocks(place, order, place.c)
    other = source_blocks(place, order, 1 - place.c)
    mine_at = [jnp.where(first, a, b) for a, b in zip(own + [own[3]] * 4, [own[0]] * 4 + own)]
    theirs_at = [jnp.where(first, a, b) for a, b in zip([other[0]] * 4 + other, other + [other[3]] * 4)]
    from_mine = [jnp.where(first, 1, 0)] * 4 + [jnp.where(first, 0, 1)] * 4
    table = jnp.stack([jnp.stack(mine_at), jnp.stack(theirs_at), jnp.stack(from_mine)]).astype(jnp.int32)

    def kernel(table_ref, mine_ref, theirs_ref, out_ref):
        j = pl.program_id(0)

        @pl.when(table_ref[2, j] == 1)
        def _():
            out_ref[...] = mine_ref[...].astype(f32)

        @pl.when(table_ref[2, j] == 0)
        def _():
            out_ref[...] = theirs_ref[...].astype(f32)

    return pl.pallas_call(
        kernel,
        grid_spec=pltpu.PrefetchScalarGridSpec(
            num_scalar_prefetch=1,
            grid=(8,),
            in_specs=[
                pl.BlockSpec((block, width), lambda j, t: (t[0, j], 0)),
                pl.BlockSpec((block, width), lambda j, t: (t[1, j], 0)),
            ],
            out_specs=pl.BlockSpec((block, width), lambda j, t: (j, 0)),
        ),
        out_shape=jax.ShapeDtypeStruct((8 * block, width), f32),
        compiler_params=pltpu.CompilerParams(vmem_limit_bytes=40 * 2**20),
        cost_estimate=pl.CostEstimate(flops=0, bytes_accessed=8 * block * width * 6, transcendentals=0),
    )(table, mine, theirs)


def unpack_columns(place, mine, theirs, order, block, spans):
    width = mine.shape[1]
    outs = 1 + max(span[0] for span in spans)
    widths = [2 * sum(span[4] for span in spans if span[0] == k) for k in range(outs)]
    own = source_blocks(place, order, place.c)
    other = source_blocks(place, order, 1 - place.c)
    table = jnp.stack([jnp.stack(own), jnp.stack(other), jnp.stack([place.c] * 4)]).astype(jnp.int32)

    def kernel(table_ref, mine_ref, theirs_ref, *out_refs):
        for core in range(2):

            @pl.when(table_ref[2, 0] == core)
            def _():
                for out, start0, start1, start, length in spans:
                    starts = (start0, start1)
                    out_refs[out][:, pl.ds(starts[core], length)] = mine_ref[:, pl.ds(start, length)].astype(f32)
                    out_refs[out][:, pl.ds(starts[1 - core], length)] = theirs_ref[:, pl.ds(start, length)].astype(
                        f32
                    )

    return pl.pallas_call(
        kernel,
        grid_spec=pltpu.PrefetchScalarGridSpec(
            num_scalar_prefetch=1,
            grid=(4,),
            in_specs=[
                pl.BlockSpec((block, width), lambda j, t: (t[0, j], 0)),
                pl.BlockSpec((block, width), lambda j, t: (t[1, j], 0)),
            ],
            out_specs=[pl.BlockSpec((block, w), lambda j, t: (j, 0)) for w in widths],
        ),
        out_shape=[jax.ShapeDtypeStruct((4 * block, w), f32) for w in widths],
        compiler_params=pltpu.CompilerParams(vmem_limit_bytes=40 * 2**20),
        cost_estimate=pl.CostEstimate(flops=0, bytes_accessed=4 * block * sum(widths) * 6, transcendentals=0),
    )(table, mine, theirs)


def dot(left, right):
    return jnp.dot(left, right, preferred_element_type=f32)


def times_transpose(left, right):
    return lax.dot_general(left, right, (((1,), (1,)), ((), ())), preferred_element_type=f32)


def cut(array, start, size, axis):
    return lax.dynamic_slice_in_dim(array, start, size, axis)


def norm_parts(values):
    center = jnp.mean(values, axis=-1, keepdims=True)
    centered = values - center
    variance = jnp.mean(centered * centered, axis=-1, keepdims=True)
    scale = lax.rsqrt(variance + norm_epsilon)
    return centered * scale, scale


def norm_back(normal, scale, grad):
    return scale * (
        grad
        - jnp.mean(grad, axis=-1, keepdims=True)
        - normal * jnp.mean(grad * normal, axis=-1, keepdims=True)
    )


def gelu_parts(values):
    square = values * values
    inner = jnp.tanh(gelu_factor * values * (1.0 + 0.044715 * square))
    value = 0.5 * values * (1.0 + inner)
    slope = 0.5 * (1.0 + inner) + 0.5 * values * (1.0 - inner * inner) * gelu_factor * (
        1.0 + 3.0 * 0.044715 * square
    )
    return value, slope


def shards(
    block_input,
    segment_ids,
    ln1_gain,
    ln1_bias,
    w_qkv,
    b_query,
    b_value,
    w_out,
    b_out,
    ln2_gain,
    ln2_bias,
    w_fc,
    b_fc,
    w_proj,
    b_proj,
    cotangent,
):
    place = Place()
    g, c = place.g, place.c
    far = 1 - g

    vectors = jnp.stack([ln1_gain, ln1_bias, b_query, b_value, b_out, ln2_gain, ln2_bias, b_proj])
    vectors = jnp.concatenate([vectors, b_fc.reshape(4, 512)], 0)
    vectors_other = swap(vectors, FIRST["g"])
    qkv_near = swap(cut(w_qkv, c * 256, 256, 0), FIRST["g"])
    out_near = swap(cut(w_out, c * 256, 256, 0), FIRST["g"])
    fc_own = jnp.concatenate([cut(w_fc, c * 1024, 1024, 1), cut(w_fc, 2048 + c * 1024, 1024, 1)], 1)
    fc_other = swap(fc_own, FIRST["g"])
    proj_own = cut(w_proj, c * 1024, 1024, 0)
    proj_other = swap(proj_own, FIRST["g"])
    qkv_far = swap(qkv_near, CORE)
    out_far = swap(out_near, CORE)
    cotangent_two = jnp.concatenate([cotangent, swap(cotangent, CORE)], 0)

    low = jnp.where(g == 0, vectors, vectors_other).astype(f32)
    high = jnp.where(g == 0, vectors_other, vectors).astype(f32)
    full = jnp.concatenate([low[:8], high[:8]], 1)
    gain_one, shift_one, query_bias, value_bias, out_bias, gain_two, shift_two, proj_bias = [
        full[k : k + 1] for k in range(8)
    ]
    fc_bias = jnp.concatenate(
        [cut(low[8:].reshape(1, 2048), c * 1024, 1024, 1), cut(high[8:].reshape(1, 2048), c * 1024, 1024, 1)], 1
    )

    def split_rows(activation):
        return (
            cut(activation, g * 512, 512, 1),
            cut(activation, far * 512 + c * 256, 256, 1),
            cut(activation, far * 512 + (1 - c) * 256, 256, 1),
        )

    inputs = block_input.astype(f32)
    normal_one, scale_one = norm_parts(inputs)
    normed_one = (normal_one * gain_one + shift_one).astype(bf16)
    normed_one_two = jnp.concatenate([normed_one, swap(normed_one, CORE)], 0)
    pieces = split_rows(normed_one)
    bias_full = jnp.concatenate([query_bias, jnp.zeros((1, D), f32), value_bias], 1)
    projected = (
        dot(pieces[0], w_qkv) + dot(pieces[1], qkv_near) + dot(pieces[2], qkv_far) + bias_full
    ).astype(bf16)
    head_shape = (ROWS, HEADS, HEAD_DIM)
    queries = projected[:, :D].reshape(head_shape)
    keys = projected[:, D : 2 * D].reshape(head_shape)
    values = projected[:, 2 * D :].reshape(head_shape)
    positions = jnp.arange(ROWS)
    segments = segment_ids[0]
    allowed = (positions[:, None] >= positions[None, :]) & (segments[:, None] == segments[None, :])
    score_scale = 1.0 / math.sqrt(HEAD_DIM)
    scores = jnp.einsum("qhd,khd->hqk", queries, keys, preferred_element_type=f32) * score_scale
    scores = jnp.where(allowed[None], scores, masked_score)
    weights = jnp.exp(scores - jnp.max(scores, axis=-1, keepdims=True))
    probs = weights / jnp.sum(weights, axis=-1, keepdims=True)
    probs_low = probs.astype(bf16)
    mixture = (
        jnp.einsum("hqk,khd->qhd", probs_low, values, preferred_element_type=f32).reshape(ROWS, D).astype(bf16)
    )
    mixture_two = jnp.concatenate([mixture, swap(mixture, CORE)], 0)
    pieces = split_rows(mixture)
    residual = inputs + (dot(pieces[0], w_out) + dot(pieces[1], out_near) + dot(pieces[2], out_far) + out_bias)
    normal_two, scale_two = norm_parts(residual)
    normed_two = (normal_two * gain_two + shift_two).astype(bf16)

    normed_both = jnp.concatenate([normed_two, swap(normed_two, CORE)], 0)
    hidden_pre = (
        dot(cut(normed_both, g * 512, 512, 1), fc_own) + dot(cut(normed_both, far * 512, 512, 1), fc_other) + fc_bias
    )
    hidden_value, hidden_slope = gelu_parts(hidden_pre)
    hidden = hidden_value.astype(bf16)
    proj_part = reduce_part(place, [(hidden, cotangent_two)], ("x", "z", "g"), 256)
    output_part = dot(cut(hidden, g * 1024, 1024, 1), proj_own) + dot(cut(hidden, far * 1024, 1024, 1), proj_other)
    result = (residual + (output_part[:ROWS] + swap(output_part[ROWS:], CORE) + proj_bias)).astype(bf16)
    grad_own = times_transpose(cotangent_two, proj_own)
    grad_other = times_transpose(cotangent_two, proj_other)
    grad_hidden = jnp.concatenate(
        [jnp.where(g == 0, grad_own, grad_other), jnp.where(g == 0, grad_other, grad_own)], 1
    )
    grad_pre = (grad_hidden * hidden_slope).astype(bf16)
    fc_part = reduce_part(place, [(normed_both, grad_pre)], ("z", "g", "x"), 128)
    back_own = times_transpose(grad_pre, fc_own)
    back_other = times_transpose(grad_pre, fc_other)
    back = jnp.concatenate([jnp.where(g == 0, back_own, back_other), jnp.where(g == 0, back_other, back_own)], 1)
    grad_normed_two = back[:ROWS] + swap(back[ROWS:], CORE)
    grad_output = cotangent.astype(f32)
    grad_residual = grad_output + norm_back(normal_two, scale_two, grad_normed_two * gain_two)

    residual_low = grad_residual.astype(bf16)
    residual_both = jnp.concatenate(
        [cut(residual_low, c * 512, 512, 1), swap(cut(residual_low, (1 - c) * 512, 512, 1), CORE)], 0
    )
    back_pieces = [times_transpose(residual_low, w) for w in (w_out, out_near, out_far)]

    def join_rows(own, near, other):
        rest = jnp.where(c == 0, jnp.concatenate([near, other], 1), jnp.concatenate([other, near], 1))
        return jnp.where(g == 0, jnp.concatenate([own, rest], 1), jnp.concatenate([rest, own], 1))

    grad_mixture = join_rows(*back_pieces).astype(bf16).reshape(head_shape)
    value_grad = jnp.einsum("hqk,qhd->khd", probs_low, grad_mixture, preferred_element_type=f32)
    grad_probs = jnp.einsum("qhd,khd->hqk", grad_mixture, values, preferred_element_type=f32)
    centre = jnp.sum(probs * grad_probs, axis=-1, keepdims=True)
    grad_scores = (probs * (grad_probs - centre)).astype(bf16)
    query_grad = jnp.einsum("hqk,khd->qhd", grad_scores, keys, preferred_element_type=f32) * score_scale
    key_grad = jnp.einsum("hqk,qhd->khd", grad_scores, queries, preferred_element_type=f32) * score_scale
    grad_projected = jnp.concatenate(
        [query_grad.reshape(ROWS, D), key_grad.reshape(ROWS, D), value_grad.reshape(ROWS, D)], 1
    ).astype(bf16)
    projected_both = jnp.concatenate(
        [cut(grad_projected, c * 1536, 1536, 1), swap(cut(grad_projected, (1 - c) * 1536, 1536, 1), CORE)], 0
    )
    attention_part = reduce_part(
        place, [(normed_one_two, projected_both), (mixture_two, residual_both)], ("g", "x", "z"), 128
    )
    grad_normed_one = join_rows(*[times_transpose(grad_projected, w) for w in (w_qkv, qkv_near, qkv_far)])
    input_grad = grad_residual + norm_back(normal_one, scale_one, grad_normed_one * gain_one)

    def over(values):
        return jnp.sum(values, axis=0, keepdims=True)

    projected_float = grad_projected.astype(f32)
    fc_sums = over(grad_pre.astype(f32)).reshape(2, 1, 1024)
    nothing = jnp.zeros_like(fc_sums)
    fc_sums = jnp.where(
        c == 0, jnp.concatenate([fc_sums, nothing], 1), jnp.concatenate([nothing, fc_sums], 1)
    ).reshape(4, 1024)
    sums = jnp.concatenate(
        [
            over(grad_normed_one * normal_one),
            over(grad_normed_one),
            over(projected_float[:, :D]),
            over(projected_float[:, 2 * D :]),
            over(grad_residual),
            over(grad_normed_two * normal_two),
            over(grad_normed_two),
            over(grad_output),
            fc_sums,
        ],
        0,
    )
    sums = lax.psum(sums, AXES)
    owned = cut(sums[:8], g * 512, 512, 1)
    fc_owned = cut(sums[8:].reshape(-1), g * 2048, 2048, 0)

    proj_mine = gather_part(place, proj_part, ("x", "z", "g"))
    proj_theirs = swap(proj_mine, CORE)
    proj_grad = unpack_rows(place, proj_mine, proj_theirs, ("x", "z", "g"), 256)
    fc_mine = gather_part(place, fc_part, ("z", "g", "x"))
    fc_theirs = swap(fc_mine, CORE)
    (fc_grad,) = unpack_columns(
        place, fc_mine, fc_theirs, ("z", "g", "x"), 128, [(0, 0, 1024, 0, 1024), (0, 2048, 3072, 1024, 1024)]
    )
    attention_mine = gather_part(place, attention_part, ("g", "x", "z"))
    attention_theirs = swap(attention_mine, CORE)
    qkv_grad, out_grad = unpack_columns(
        place, attention_mine, attention_theirs, ("g", "x", "z"), 128, [(0, 0, 1536, 0, 1536), (1, 0, 512, 1536, 512)]
    )
    return (
        result,
        input_grad,
        owned[0],
        owned[1],
        qkv_grad,
        owned[2],
        owned[3],
        out_grad,
        owned[4],
        owned[5],
        owned[6],
        fc_grad,
        fc_owned,
        proj_grad,
        owned[7],
    )


def solution(mesh):
    rows = P(("group", "replica"), None)
    vector = P("group")
    matrix = P("group", None)
    placed = (
        rows,
        rows,
        vector,
        vector,
        matrix,
        vector,
        vector,
        matrix,
        vector,
        vector,
        vector,
        matrix,
        vector,
        matrix,
        vector,
        rows,
    )
    results = (
        rows,
        rows,
        vector,
        vector,
        matrix,
        vector,
        vector,
        matrix,
        vector,
        vector,
        vector,
        matrix,
        vector,
        matrix,
        vector,
    )
    return jax.shard_map(shards, mesh=mesh, in_specs=placed, out_specs=results, check_vma=False)
```

```python
import math

import jax
import jax.numpy as jnp
import numpy as np
from jax import lax
from jax.experimental import pallas as pl
from jax.experimental.pallas import tpu as pltpu
from jax.sharding import PartitionSpec as P

D = 1024
HEADS = 16
HEAD_DIM = 64
ROWS = 128
BOTH = 2 * ROWS
EXTRA = 16

norm_epsilon = 1e-05
masked_score = -1e30
gelu_factor = 0.7978845608028654
score_scale = 1.0 / math.sqrt(HEAD_DIM)

f32 = jnp.float32
bf16 = jnp.bfloat16
AXES = ("group", "replica")
MIB = 2**20


def flat(g, yh, x, z, c):
    return (((g * 2 + yh) * 4 + x) * 4 + z) * 2 + c


def at(y, x, z, c):
    return flat(y % 2, y // 2, x, z, c)


def everywhere():
    return [(g, yh, x, z, c) for g in range(2) for yh in range(2) for x in range(4) for z in range(4) for c in range(2)]


def exchange(move):
    return [(flat(g, yh, x, z, c), move(2 * yh + g, x, z, c)) for g, yh, x, z, c in everywhere()]


FIRST = {
    "g": exchange(lambda y, x, z, c: at(y ^ (1, 3)[c], x, z, c)),
    "x": exchange(lambda y, x, z, c: at(y, x ^ (1, 3)[c], z, c)),
    "z": exchange(lambda y, x, z, c: at(y, x, z ^ (1, 3)[c], c)),
    "xz": exchange(lambda y, x, z, c: at(y, x ^ (1, 3)[c], z ^ (1, 3)[c], c)),
}
SECOND = {
    "x": exchange(lambda y, x, z, c: at(y, x ^ (3, 1)[c], z, c)),
    "z": exchange(lambda y, x, z, c: at(y, x, z ^ (3, 1)[c], c)),
    "xz": exchange(lambda y, x, z, c: at(y, x ^ (3, 1)[c], z ^ (3, 1)[c], c)),
}
FAR = exchange(lambda y, x, z, c: at(y ^ 2, x, z, c))
CORE = exchange(lambda y, x, z, c: at(y, x, z, c ^ 1))
PLANES = [
    [flat(g, yh, x, z, c) for x in range(4) for z in range(4)] for g in range(2) for yh in range(2) for c in range(2)
]


def swap(array, pairs):
    return lax.ppermute(array, AXES, pairs)


def after(value, *others):
    return lax.optimization_barrier((value, others))[0]


G, C, UX, UZ, VX, VZ = range(6)
PIECE = 6
QUARTER = 9
NUMBERS = 16


def numbers():
    rows = []
    for g, yh, x, z, c in everywhere():
        xs = ((x % 2) ^ (x // 2), x // 2)
        zs = ((z % 2) ^ (z // 2), z // 2)
        ux, vx, uz, vz = xs[c], xs[1 - c], zs[c], zs[1 - c]
        base = (1 - g) * 512
        row = [g, c, ux, uz, vx, vz, g * 512, base + c * 256, base + (1 - c) * 256]
        row += [base + ((ux ^ rx) * 2 + (uz ^ rz)) * 128 for rx in range(2) for rz in range(2)]
        rows.append(row + [0] * (NUMBERS - len(row)))
    return np.array(rows, np.int32)


def cost(us):
    return pl.CostEstimate(flops=0, bytes_accessed=int(us * 3.69e6), transcendentals=0)


def shape(dims, dtype):
    return jax.ShapeDtypeStruct(dims, dtype)


def dot(left, right):
    return jnp.dot(left, right, preferred_element_type=f32)


def rows_dot(left, right):
    return lax.dot_general(left, right, (((0,), (0,)), ((), ())), preferred_element_type=f32)


def dot_rows(left, right):
    return lax.dot_general(left, right, (((1,), (1,)), ((), ())), preferred_element_type=f32)


def span(start, size):
    return pl.ds(pl.multiple_of(start, size), size)


def norm_parts(values):
    center = jnp.mean(values, axis=-1, keepdims=True)
    centered = values - center
    variance = jnp.mean(centered * centered, axis=-1, keepdims=True)
    scale = lax.rsqrt(variance + norm_epsilon)
    return centered * scale, scale


def norm_back(normal, scale, grad):
    return scale * (
        grad
        - jnp.mean(grad, axis=-1, keepdims=True)
        - normal * jnp.mean(grad * normal, axis=-1, keepdims=True)
    )


def over(values):
    return jnp.sum(values, axis=0, keepdims=True)


MADE = []


def stepped(body, steps, table, operands, in_specs, outputs, out_specs, estimate, scratch=(), limit=32, near=False):
    operands = [
        pltpu.with_memory_space_constraint(array, pltpu.HBM)
        if not near and array.size >= 32768 and not any(array is made for made in MADE)
        else array
        for array in operands
    ]
    results = pl.pallas_call(
        body,
        grid_spec=pltpu.PrefetchScalarGridSpec(
            num_scalar_prefetch=1,
            grid=(steps,),
            in_specs=in_specs,
            out_specs=out_specs,
            scratch_shapes=list(scratch),
        ),
        out_shape=outputs,
        compiler_params=pltpu.CompilerParams(vmem_limit_bytes=limit * MIB),
        cost_estimate=estimate,
    )(table, *operands)
    MADE.extend(jax.tree.leaves(results))
    return results


def block(dims, place):
    return pl.BlockSpec(dims, place)


def fixed(dims, row=0, column=0):
    place = (row, column) if len(dims) == 2 else (0,) * len(dims)
    return pl.BlockSpec(dims, lambda j, t: place)


def pack(table, inputs, w_out, w_fc, vectors):
    def body(t, in_ref, out_ref, low_ref, high_ref, *refs):
        first, out_part, fc_part = refs[9:]
        first[:ROWS, :] = in_ref[...]
        first[ROWS:, :] = jnp.zeros((EXTRA, D), bf16)
        for k in range(8):
            first[ROWS + k // 2 : ROWS + k // 2 + 1, 512 * (k % 2) : 512 * (k % 2) + 512] = refs[k][...].reshape(1, 512)
        for k in range(2):
            first[ROWS + 4 + k : ROWS + 5 + k, :] = refs[8][pl.ds(1024 * k, 1024)].reshape(1, 1024)
        out_part[...] = out_ref[...]
        fc_part[:, :1024] = low_ref[...]
        fc_part[:, 1024:] = high_ref[...]

    outputs = [shape((ROWS + EXTRA, D), bf16), shape((256, D), bf16), shape((128, 2048), bf16)]
    return stepped(
        body,
        1,
        table,
        (inputs, w_out, w_fc, w_fc, *vectors),
        [
            fixed((ROWS, D)),
            block((256, D), lambda j, t: (t[C], 0)),
            block((128, 1024), lambda j, t: (t[UX] * 2 + t[UZ], t[C])),
            block((128, 1024), lambda j, t: (t[UX] * 2 + t[UZ], 2 + t[C])),
        ]
        + [pl.BlockSpec(v.shape, lambda j, t: (0,)) for v in vectors],
        outputs,
        [fixed(o.shape) for o in outputs],
        cost(3.6),
        limit=60,
    )


def spread(table, own, other):
    def body(t, own_ref, other_ref, full_ref, bias_ref, normed_ref):
        first = t[G] == 0
        mine = own_ref[ROWS : ROWS + 8, :].astype(f32)
        theirs = other_ref[...].astype(f32)[:8]
        low = jnp.where(first, mine, theirs)
        high = jnp.where(first, theirs, mine)
        for k in range(8):
            half = slice(512 * (k % 2), 512 * (k % 2) + 512)
            full_ref[k : k + 1, :512] = low[k // 2 : k // 2 + 1, half]
            full_ref[k : k + 1, 512:] = high[k // 2 : k // 2 + 1, half]
        second = t[C] == 1
        bias_ref[:, :1024] = jnp.where(second, low[5:6], low[4:5])
        bias_ref[:, 1024:] = jnp.where(second, high[5:6], high[4:5])
        normal, _ = norm_parts(own_ref[:ROWS, :].astype(f32))
        normed_ref[...] = (normal * full_ref[0:1, :] + full_ref[1:2, :]).astype(bf16)

    return stepped(
        body,
        1,
        table,
        (own, other),
        [fixed((ROWS + EXTRA, D)), fixed((EXTRA, D), ROWS // EXTRA)],
        [shape((8, D), f32), shape((1, 2048), f32), shape((ROWS, D), bf16)],
        [fixed((8, D)), fixed((1, 2048)), fixed((ROWS, D))],
        cost(1.8),
    )


def project(table, own, other, gain, shift, w_qkv):
    width = 512

    def body(t, own_ref, other_ref, gain_ref, shift_ref, w_ref, mine_ref, theirs_ref, normed_ref):
        @pl.when(pl.program_id(0) == 0)
        def _():
            half = span(t[PIECE], 512)
            scale = gain_ref[...].astype(f32).reshape(1, 512)
            offset = shift_ref[...].astype(f32).reshape(1, 512)
            for k, ref in enumerate((own_ref, other_ref)):
                values = ref[...].astype(f32)
                center = jnp.mean(values, axis=-1, keepdims=True)
                centered = values - center
                variance = jnp.mean(centered * centered, axis=-1, keepdims=True)
                part = (ref[:, half].astype(f32) - center) * lax.rsqrt(variance + norm_epsilon)
                normed_ref[k * ROWS : (k + 1) * ROWS, :] = (part * scale + offset).astype(bf16)

        total = dot(normed_ref[...], w_ref[...])
        mine_ref[...] = total[:ROWS]
        theirs_ref[...] = total[ROWS:].astype(bf16)

    step = lambda j, t: (0, j)
    vector = pl.BlockSpec((512,), lambda j, t: (0,))
    return stepped(
        body,
        6,
        table,
        (own, other, gain, shift, w_qkv),
        [fixed((ROWS, D)), fixed((ROWS, D)), vector, vector, block((512, width), step)],
        [shape((ROWS, 3 * D), f32), shape((ROWS, 3 * D), bf16)],
        [block((ROWS, width), step), block((ROWS, width), step)],
        cost(8),
        [pltpu.VMEM((BOTH, 512), bf16)],
    )


def admitted(segments_ref):
    across = jnp.broadcast_to(segments_ref[...], (ROWS, ROWS))
    down = across.T
    row = lax.broadcasted_iota(jnp.int32, (ROWS, ROWS), 0)
    column = lax.broadcasted_iota(jnp.int32, (ROWS, ROWS), 1)
    return (row >= column) & (across == down)


def head_probs(projected_ref, head, allowed):
    queries = projected_ref[:, head * HEAD_DIM : (head + 1) * HEAD_DIM]
    keys = projected_ref[:, D + head * HEAD_DIM : D + (head + 1) * HEAD_DIM]
    values = projected_ref[:, 2 * D + head * HEAD_DIM : 2 * D + (head + 1) * HEAD_DIM]
    scores = jnp.where(allowed, dot_rows(queries, keys) * score_scale, masked_score)
    weights = jnp.exp(scores - jnp.max(scores, axis=-1, keepdims=True))
    return queries, keys, values, weights / jnp.sum(weights, axis=-1, keepdims=True)


def mix(table, mine, theirs, full, segments):
    def body(t, mine_ref, theirs_ref, full_ref, seg_ref, p_ref, mixture_ref):
        for k, row in ((0, 2), (1, None), (2, 3)):
            columns = slice(k * D, (k + 1) * D)
            total = mine_ref[:, columns] + theirs_ref[:, columns].astype(f32)
            if row is not None:
                total += full_ref[row : row + 1, :]
            p_ref[:, columns] = total.astype(bf16)
        allowed = admitted(seg_ref)
        for head in range(HEADS):
            _, _, values, probs = head_probs(p_ref, head, allowed)
            mixture_ref[:, head * HEAD_DIM : (head + 1) * HEAD_DIM] = dot(probs.astype(bf16), values).astype(bf16)

    return stepped(
        body,
        1,
        table,
        (mine, theirs, full, segments),
        [fixed((ROWS, 3 * D)), fixed((ROWS, 3 * D)), fixed((8, D)), fixed((1, ROWS))],
        [shape((ROWS, 3 * D), bf16), shape((ROWS, D), bf16)],
        [fixed((ROWS, 3 * D)), fixed((ROWS, D))],
        cost(8.1),
    )


def settle(table, mixture, inputs, full, w_out, near, far):
    def body(t, mixture_ref, in_ref, full_ref, own, a, b, side_ref, residual_ref):
        total = dot(mixture_ref[:, span(t[PIECE], 512)], own[...])
        for k, ref in enumerate((a, b)):
            total += dot(mixture_ref[:, span(t[PIECE + 1 + k], 256)], ref[...])
        residual = in_ref[...].astype(f32) + (total + full_ref[4:5, :])
        residual_ref[...] = residual
        normal, _ = norm_parts(residual)
        side_ref[:, :D] = (normal * full_ref[5:6, :] + full_ref[6:7, :]).astype(bf16)
        side_ref[:, D:] = mixture_ref[...]

    return stepped(
        body,
        1,
        table,
        (mixture, inputs, full, w_out, near, far),
        [fixed((ROWS, D)), fixed((ROWS, D)), fixed((8, D)), fixed((512, D)), fixed((256, D)), fixed((256, D))],
        [shape((ROWS, 2 * D), bf16), shape((ROWS, D), f32)],
        [fixed((ROWS, 2 * D)), fixed((ROWS, D))],
        cost(3),
    )


QUARTERS = [(0, 0), (1, 0), (2, 0), (2, 1)]


def expand(table, normed, w_fc, quarters, bias):
    width = 512

    def body(t, normed_ref, own_ref, a, b, c, d, bias_ref, hidden_ref, slope_ref):
        values = dot(normed_ref[:, span(t[PIECE], 512)], own_ref[...])
        for k, ref in enumerate((a, b, c, d)):
            values += dot(normed_ref[:, span(t[QUARTER + k], 128)], ref[...])
        values += bias_ref[...]
        square = values * values
        inner = jnp.tanh(gelu_factor * values * (1.0 + 0.044715 * square))
        outer = 0.5 * (1.0 + inner)
        hidden_ref[...] = (values * outer).astype(bf16)
        slope_ref[...] = outer + values * outer * (1.0 - inner) * gelu_factor * (1.0 + 3.0 * 0.044715 * square)

    step = lambda j, t: (0, j)
    return stepped(
        body,
        4,
        table,
        (normed, w_fc, *[quarters[k] for k, _ in QUARTERS], bias),
        [fixed((BOTH, D)), block((512, width), lambda j, t: (0, (j // 2) * 4 + t[C] * 2 + j % 2))]
        + [block((128, width), lambda j, t, row=row: (row, j)) for _, row in QUARTERS]
        + [block((1, width), step)],
        [shape((BOTH, 2048), bf16), shape((BOTH, 2048), f32)],
        [block((BOTH, width), step), block((BOTH, width), step)],
        cost(6),
    )


def unit_block(j, t):
    other = (1 - t[G]) * 2 + jnp.where(j == 2, t[UX], 1 - t[UX])
    return (0, jnp.where(j < 2, t[G] * 2 + j, other))


def whole_block(j, t):
    return (0, jnp.where(j < 2, t[G], 1 - t[G]) * 2 + j % 2)


def unit_weights(j, t):
    return (t[C] * 2 + jnp.minimum(j, 1), 0)


def with_weights(refs, use):
    j = pl.program_id(0)
    for ref, here in zip(refs, (j < 2, j == 2, j == 3)):

        @pl.when(here)
        def _():
            use(ref[...])


def contract(table, hidden, w_proj, others):
    def body(t, hidden_ref, own, a, b, mine_ref, theirs_ref):
        @pl.when(pl.program_id(0) == 0)
        def _():
            mine_ref[...] = jnp.zeros((ROWS, D), f32)
            theirs_ref[...] = jnp.zeros((ROWS, D), f32)

        def use(weights):
            total = dot(hidden_ref[...], weights)
            mine_ref[...] += total[:ROWS]
            theirs_ref[...] += total[ROWS:]

        with_weights((own, a, b), use)

    return stepped(
        body,
        4,
        table,
        (hidden, w_proj, *others),
        [block((BOTH, 512), whole_block), block((512, D), unit_weights)] + [fixed((512, D))] * 2,
        [shape((ROWS, D), f32), shape((ROWS, D), f32)],
        [fixed((ROWS, D)), fixed((ROWS, D))],
        cost(0.5),
    )


def hidden_back(table, cotangents, slope, w_proj, others):
    def body(t, cot_ref, slope_ref, own, a, b, grad_ref, sums_ref):
        def use(weights):
            grad = (dot_rows(cot_ref[...], weights) * slope_ref[...]).astype(bf16)
            grad_ref[...] = grad
            sums_ref[...] = over(grad.astype(f32))

        with_weights((own, a, b), use)

    return stepped(
        body,
        4,
        table,
        (cotangents, slope, w_proj, *others),
        [fixed((BOTH, D)), block((BOTH, 512), whole_block), block((512, D), unit_weights)] + [fixed((512, D))] * 2,
        [shape((BOTH, 2048), bf16), shape((1, 2048), f32)],
        [block((BOTH, 512), whole_block), block((1, 512), whole_block)],
        cost(8),
    )


def normed_back(table, grad_pre, w_fc, quarters):
    def body(t, grad_ref, low_ref, high_ref, a, b, c, d, mine_ref, theirs_ref):
        j = pl.program_id(0)

        def use(low, high, columns):
            total = dot_rows(grad_ref[:, :1024], low) + dot_rows(grad_ref[:, 1024:], high)
            mine_ref[:, columns] = total[:ROWS]
            theirs_ref[:, columns] = total[ROWS:]

        @pl.when(j < 2)
        def _():
            use(low_ref[...], high_ref[...], slice(0, 256))

        for step, near, far in ((2, a, b), (3, c, d)):

            @pl.when(j == step)
            def _():
                use(near[:, :1024], near[:, 1024:], span(t[UZ] * 128, 128))
                use(far[:, :1024], far[:, 1024:], span((1 - t[UZ]) * 128, 128))

    return stepped(
        body,
        4,
        table,
        (grad_pre, w_fc, w_fc, *[quarters[k] for k, _ in QUARTERS]),
        [
            fixed((BOTH, 2048)),
            block((256, 1024), lambda j, t: (jnp.minimum(j, 1), t[C])),
            block((256, 1024), lambda j, t: (jnp.minimum(j, 1), 2 + t[C])),
        ]
        + [fixed((128, 2048), row) for _, row in QUARTERS],
        [shape((ROWS, D), f32), shape((ROWS, D), f32)],
        [block((ROWS, 256), unit_block), block((ROWS, 256), unit_block)],
        cost(8),
    )


def attend_back(table, mine, theirs, residual, cotangent, full, projected, segments, w_out, near, far):
    def body(
        t, mine_ref, theirs_ref, res_ref, cot_ref, full_ref, p_ref, seg_ref, own, a, b,
        grad_ref, dealt_ref, sums_ref, mix_ref,
    ):
        normal, scale = norm_parts(res_ref[...])
        grad_normed = mine_ref[...] + theirs_ref[...]
        grad_output = cot_ref[...].astype(f32)
        grad = grad_output + norm_back(normal, scale, grad_normed * full_ref[5:6, :])
        grad_ref[...] = grad
        low = grad.astype(bf16)
        for k in range(8):
            dealt_ref[k // 4, :, 512 * (k % 4) + 384 : 512 * (k % 4) + 512] = low[:, 128 * k : 128 * (k + 1)]
        sums_ref[0:1, :] = over(grad)
        sums_ref[1:2, :] = over(grad_normed * normal)
        sums_ref[2:3, :] = over(grad_normed)
        sums_ref[3:4, :] = over(grad_output)
        sums_ref[4:, :] = jnp.zeros((4, D), f32)
        mix_ref[:, span(t[PIECE], 512)] = dot_rows(low, own[...]).astype(bf16)
        for k, ref in enumerate((a, b)):
            mix_ref[:, span(t[PIECE + 1 + k], 256)] = dot_rows(low, ref[...]).astype(bf16)
        allowed = admitted(seg_ref)

        def store(number, values):
            column = 512 * (number % 24 // 6) + HEAD_DIM * (number % 6)
            dealt_ref[number // 24, :, column : column + HEAD_DIM] = values.astype(bf16)

        for head in range(HEADS):
            queries, keys, values, probs = head_probs(p_ref, head, allowed)
            grad_mix = mix_ref[:, head * HEAD_DIM : (head + 1) * HEAD_DIM]
            grad_probs = dot_rows(grad_mix, values)
            centre = jnp.sum(probs * grad_probs, axis=-1, keepdims=True)
            grad_scores = (probs * (grad_probs - centre)).astype(bf16)
            store(head, dot(grad_scores, keys) * score_scale)
            store(HEADS + head, rows_dot(grad_scores, queries) * score_scale)
            store(2 * HEADS + head, rows_dot(probs.astype(bf16), grad_mix))

    square = fixed((ROWS, D))
    return stepped(
        body,
        1,
        table,
        (mine, theirs, residual, cotangent, full, projected, segments, w_out, near, far),
        [square] * 4 + [fixed((8, D)), fixed((ROWS, 3 * D)), fixed((1, ROWS))]
        + [fixed((512, D)), fixed((256, D)), fixed((256, D))],
        [shape((ROWS, D), f32), shape((2, ROWS, 2048), bf16), shape((8, D), f32)],
        [square, fixed((2, ROWS, 2048)), fixed((8, D))],
        cost(11.5),
        [pltpu.VMEM((ROWS, D), bf16)],
    )


def input_back(table, dealt, w_qkv, near, far, inputs, grad_residual, full, sums, fc_sums):
    width = 384

    def body(t, grad_ref, own, a, b, in_ref, res_ref, full_ref, early_ref, fc_ref, out_ref, sums_ref, total_ref, bias_ref):
        j = pl.program_id(0)
        grad = grad_ref[0, :, :width]

        @pl.when(j == 0)
        def _():
            total_ref[...] = jnp.zeros((ROWS, D), f32)

        offset = 0
        for ref in (own, a, b):
            size = ref.shape[0]
            total_ref[:, offset : offset + size] += dot_rows(grad, ref[...])
            offset += size
        bias_ref[:, span(j * width, width)] = over(grad.astype(f32))

        @pl.when(j == 7)
        def _():
            offset = 0
            for k, size in enumerate((512, 256, 256)):
                out_ref[:, span(t[PIECE + k], size)] = total_ref[:, offset : offset + size]
                offset += size
            grad_normed = out_ref[...]
            normal, scale = norm_parts(in_ref[...].astype(f32))
            gain_sums = over(grad_normed * normal)
            shift_sums = over(grad_normed)
            out_ref[...] = res_ref[...] + norm_back(normal, scale, grad_normed * full_ref[0:1, :])
            row = lax.broadcasted_iota(jnp.int32, (4, 512), 0)
            for g in range(2):
                half = slice(512 * g, 512 * (g + 1))
                sums_ref[16 * g : 16 * g + 1, :] = gain_sums[:, half]
                sums_ref[16 * g + 1 : 16 * g + 2, :] = shift_sums[:, half]
                sums_ref[16 * g + 2 : 16 * g + 3, :] = bias_ref[:, 512 * g : 512 * (g + 1)]
                sums_ref[16 * g + 3 : 16 * g + 4, :] = bias_ref[:, 2048 + 512 * g : 2048 + 512 * (g + 1)]
                sums_ref[16 * g + 4 : 16 * g + 8, :] = early_ref[0:4, half]
                units = [fc_ref[:, 1024 * g + 512 * (k % 2) : 1024 * g + 512 * (k % 2) + 512] for k in range(4)]
                sums_ref[16 * g + 8 : 16 * g + 12, :] = jnp.where(row // 2 == t[C], jnp.concatenate(units, 0), 0.0)
                sums_ref[16 * g + 12 : 16 * g + 16, :] = jnp.zeros((4, 512), f32)

    step = lambda j, t: (0, j)
    return stepped(
        body,
        8,
        table,
        (dealt, w_qkv, near, far, inputs, grad_residual, full, sums, fc_sums),
        [pl.BlockSpec((1, ROWS, 512), lambda j, t: (j // 4, 0, j % 4)), block((512, width), step)]
        + [block((256, width), step)] * 2
        + [fixed((ROWS, D)), fixed((ROWS, D)), fixed((8, D)), fixed((8, D)), fixed((1, 2048))],
        [shape((ROWS, D), f32), shape((2 * EXTRA, 512), f32)],
        [fixed((ROWS, D)), fixed((2 * EXTRA, 512))],
        cost(9.2),
        [pltpu.VMEM((ROWS, D), f32), pltpu.VMEM((1, 3 * D), f32)],
    )


def piece_specs(pieces, width, number):
    specs, operands = [], []
    for array, row, column in pieces:
        specs.append(
            pl.BlockSpec(
                (BOTH, width),
                lambda j, t, row=row, column=column: (row // BOTH, column(t) + number(j, t)),
            )
        )
        operands.append(array)
    return specs, operands


def sum_dots(lefts, rights, columns=slice(None)):
    total = rows_dot(lefts[0][...], rights[0][:, columns])
    for left, right in zip(lefts[1:], rights[1:]):
        total += rows_dot(left[...], right[:, columns])
    return total


def deal_feed(table, hidden, grad_pre):
    def body(t, hidden_ref, grad_ref, *outs):
        for j, out in enumerate(outs):
            away = 3 - j
            bx, bz = (away // 2) ^ t[UX], (away % 2) ^ t[UZ]
            for g in range(2):
                out[:, 256 * g : 256 * (g + 1)] = hidden_ref[:, span(g * 1024 + (bx * 2 + bz) * 256, 256)]
            out[:, 512:] = grad_ref[:, span((bx * 2 + bz) * 512, 512)]

    return stepped(
        body, 1, table, (hidden, grad_pre), [fixed((BOTH, 2048))] * 2, [shape((BOTH, D), bf16)] * 4,
        [fixed((BOTH, D))] * 4, cost(0.8), near=True,
    )


def deal_attention(table, mine, theirs):
    def body(t, mine_ref, theirs_ref, *outs):
        for j, out in enumerate(outs):
            away = 3 - j
            columns = span((((away // 2) ^ t[UX]) * 2 + ((away % 2) ^ t[UZ])) * 512, 512)
            out[:ROWS, :] = mine_ref[0, :, columns]
            out[ROWS:, :] = theirs_ref[:, columns]

    return stepped(
        body, 1, table, (mine, theirs),
        [pl.BlockSpec((1, ROWS, 2048), lambda j, t: (t[C], 0, 0)), fixed((ROWS, 2048))],
        [shape((BOTH, 512), bf16)] * 4, [fixed((BOTH, 512))] * 4, cost(0.7), near=True,
    )


def quarter(j, t):
    away = 3 - j
    return ((away // 2) ^ t[VX]) * 2 + ((away % 2) ^ t[VZ])


def half_rows(j, t):
    return jnp.where(j == 0, 1 - t[VX], t[VX])


def feed_specs(normeds, grads, hiddens, cotangents, rows, width, features, units, columns):
    specs, operands = [], []
    for pieces, size, number in (
        (normeds, rows, features),
        (grads, 512, lambda j, t: 1),
        (hiddens, 256, units),
        (cotangents, width, columns),
    ):
        more, arrays = piece_specs(pieces, size, number)
        specs += more
        operands += arrays
    return specs, operands


def feed_sent(table, normeds, grads, hiddens, cotangents):
    specs, operands = feed_specs(
        normeds, grads, hiddens, cotangents, 256, 512,
        lambda j, t: (1 - t[G]) * 2 + j, lambda j, t: 1 - t[G], lambda j, t: j,
    )

    def body(t, *refs):
        out = refs[-1]
        out[:, :512] = sum_dots(refs[:4], refs[4:8]).astype(bf16)
        units = sum_dots(refs[8:12], refs[12:16]).astype(bf16)
        for q in range(2):
            rows, columns = slice(128 * q, 128 * (q + 1)), slice(256 * q, 256 * (q + 1))
            out[rows, 512:768] = units[:128, columns]
            out[rows, 768:] = units[128:, columns]

    return stepped(
        body, 2, table, operands, specs, shape((512, D), bf16), block((256, D), lambda j, t: (j, 0)), cost(4.3),
    )


def feed_total(table, normeds, grads, hiddens, cotangents, received):
    specs, operands = feed_specs(
        normeds, grads, hiddens, cotangents, 128, 256,
        lambda j, t: t[G] * 4 + quarter(j, t), lambda j, t: t[G], quarter,
    )

    def body(t, *refs):
        received_ref = refs[16]
        outs = refs[17:]
        j = pl.program_id(0)
        got = received_ref[...].astype(f32)
        left = sum_dots(refs[:4], refs[4:8]) + got[:, :512]
        right = sum_dots(refs[8:12], refs[12:16])
        top = right[:128] + got[:, 512:768]
        low = right[128:] + got[:, 768:]
        for k, out in enumerate(outs):

            @pl.when(j == k)
            def _():
                out[:, :512] = left.astype(out.dtype)
                out[:, 512:768] = top.astype(out.dtype)
                out[:, 768:] = low.astype(out.dtype)

    return stepped(
        body,
        4,
        table,
        operands + [received],
        specs + [block((128, D), lambda j, t: (quarter(j, t), 0))],
        [shape((128, D), bf16)] * 3 + [shape((128, D), f32)],
        [fixed((128, D))] * 4,
        cost(5),
    )


def attention_sent(table, normeds, mixtures, grads, sums):
    specs, operands = [], []
    for pieces in (normeds, mixtures):
        more, arrays = piece_specs(pieces, 512, lambda j, t: 1 - t[G])
        specs += more
        operands += arrays
    more, arrays = piece_specs(grads, 512, lambda j, t: 0)

    def body(t, *refs):
        sums_ref, out_ref = refs[12:]
        out_ref[:512, :384] = sum_dots(refs[:4], refs[8:12], slice(0, 384)).astype(bf16)
        out_ref[:512, 384:] = sum_dots(refs[4:8], refs[8:12], slice(384, 512)).astype(bf16)
        out_ref[512:, :] = sums_ref[...].astype(bf16)

    return stepped(
        body,
        1,
        table,
        operands + arrays + [sums],
        specs + more + [block((EXTRA, 512), lambda j, t: (1 - t[G], 0))],
        shape((512 + EXTRA, 512), bf16),
        fixed((512 + EXTRA, 512)),
        cost(3.3),
    )


def attention_total(table, normeds, mixtures, grads, received, sums):
    specs, operands = [], []
    for pieces in (normeds, mixtures):
        more, arrays = piece_specs(pieces, 256, lambda j, t: t[G] * 2 + half_rows(j, t))
        specs += more
        operands += arrays
    more, arrays = piece_specs(grads, 512, lambda j, t: 0)

    def body(t, *refs):
        received_ref, tail_ref, sums_ref, sent_ref, kept_ref, total_ref = refs[12:]
        j = pl.program_id(0)
        got = received_ref[...].astype(f32)
        left = sum_dots(refs[:4], refs[8:12], slice(0, 384)) + got[:, :384]
        right = sum_dots(refs[4:8], refs[8:12], slice(384, 512)) + got[:, 384:]

        @pl.when(j == 0)
        def _():
            sent_ref[:256, :384] = left.astype(bf16)
            sent_ref[:256, 384:] = right.astype(bf16)
            total = sums_ref[...] + tail_ref[...].astype(f32)
            total_ref[...] = total
            sent_ref[256:, :] = total.astype(bf16)

        @pl.when(j == 1)
        def _():
            kept_ref[:, :384] = left
            kept_ref[:, 384:] = right

    return stepped(
        body,
        2,
        table,
        operands + arrays + [received, received, sums],
        specs
        + more
        + [
            block((256, 512), lambda j, t: (half_rows(j, t), 0)),
            fixed((EXTRA, 512), 512 // EXTRA),
            block((EXTRA, 512), lambda j, t: (t[G], 0)),
        ],
        [shape((256 + EXTRA, 512), bf16), shape((256, 512), f32), shape((EXTRA, 512), f32)],
        [fixed((256 + EXTRA, 512)), fixed((256, 512)), fixed((EXTRA, 512))],
        cost(3.9),
    )


def add_up(table, kept, received):
    def body(t, kept_ref, *refs):
        total = kept_ref[...].astype(f32)
        for ref in refs[:-1]:
            total += ref[...].astype(f32)
        refs[-1][...] = total.astype(bf16)

    operands = [kept, *received]
    return stepped(
        body, 1, table, operands, [fixed(a.shape) for a in operands], shape(kept.shape, bf16), fixed(kept.shape),
        cost(0.7),
        near=True,
    )


def place_quarters(table, mine, others):
    width = mine.shape[1]
    extra = mine.shape[0] - 128

    def body(t, *refs):
        out = refs[-1]
        for j, ref in enumerate(refs[:-1]):
            out[span(quarter(j, t) * 128, 128), :] = ref[:128, :]
        if extra:
            out[512:, :] = refs[3][128:, :]

    operands = [*others, mine]
    return stepped(
        body, 1, table, operands, [fixed(a.shape) for a in operands], shape((512 + extra, width), bf16),
        fixed((512 + extra, width)), cost(0.7),
        near=True,
    )


def add_split(table, kept, received, sums):
    rows, width = kept.shape
    half, extra = rows // 2, received.shape[0] - rows

    def body(t, kept_ref, received_ref, *refs):
        sent_ref, left_ref = refs[-3:-1] if extra else refs
        for bit, out in ((1 - t[VZ], sent_ref), (t[VZ], left_ref)):
            lines = span(bit * half, half)
            total = kept_ref[lines, :] + received_ref[lines, :].astype(f32)
            out[:half, :] = total.astype(out.dtype)
        if extra:
            total = refs[0][...] + received_ref[rows:, :].astype(f32)
            refs[-1][...] = total
            sent_ref[half:, :] = total.astype(bf16)

    outputs = [shape((half + extra, width), bf16), shape((half, width), f32)]
    if extra:
        outputs.append(shape((extra, width), f32))
    operands = [kept, received] + ([sums] if extra else [])
    return stepped(
        body, 1, table, operands, [fixed(a.shape) for a in operands], outputs, [fixed(o.shape) for o in outputs],
        cost(0.7),
        near=True,
    )


def add_low(table, kept, received, sums):
    rows, width = kept.shape
    extra = received.shape[0] - rows

    def body(t, kept_ref, received_ref, *refs):
        out = refs[-1]
        out[:rows, :] = (kept_ref[...] + received_ref[:rows, :].astype(f32)).astype(bf16)
        if extra:
            out[rows:, :] = (refs[0][...] + received_ref[rows:, :].astype(f32)).astype(bf16)

    operands = [kept, received] + ([sums] if extra else [])
    return stepped(
        body, 1, table, operands, [fixed(a.shape) for a in operands], shape(received.shape, bf16),
        fixed(received.shape), cost(0.6),
        near=True,
    )


def add_far(table, low, received, extra):
    rows, width = low.shape[0] - extra, low.shape[1]

    def body(t, low_ref, received_ref, *outs):
        total = low_ref[...].astype(f32) + received_ref[...].astype(f32)
        outs[0][...] = total[:rows].astype(bf16)
        if extra:
            outs[1][...] = total[rows:].astype(bf16)

    outputs = [shape((rows, width), bf16)] + ([shape((extra, width), bf16)] if extra else [])
    return stepped(
        body, 1, table, (low, received), [fixed(low.shape)] * 2, outputs, [fixed(o.shape) for o in outputs],
        cost(0.6),
        near=True,
    )


def place(table, bit, mine, other, sums=None):
    rows, width = mine.shape
    extra = 0 if sums is None else EXTRA

    def body(t, mine_ref, other_ref, *refs):
        out = refs[-1]
        out[span(t[bit] * rows, rows), :] = mine_ref[...]
        out[span((1 - t[bit]) * rows, rows), :] = other_ref[...]
        if extra:
            out[2 * rows :, :] = refs[0][...]

    operands = [mine, other] + ([sums] if extra else [])
    return stepped(
        body, 1, table, operands, [fixed(a.shape) for a in operands], shape((2 * rows + extra, width), bf16),
        fixed((2 * rows + extra, width)), cost(0.6),
        near=True,
    )


def sources(t):
    found = []
    for core in range(2):
        mine = t[C] == core
        ux = jnp.where(mine, t[UX], t[VX])
        uz = jnp.where(mine, t[UZ], t[VZ])
        for number in range(4):
            away = ((number // 2) ^ ux) * 2 + ((number % 2) ^ uz)
            found.append((core, number, jnp.where(mine, 0, 4) + away))
    return found


def unpack_feed(table, arrays):
    def body(t, *refs):
        fc_ref, proj_ref = refs[8:]
        j = pl.program_id(0)
        rows = span(j * 64, 64)
        for core, number, source in sources(t):
            column = (number // 2) * 2048 + core * 1024 + (number % 2) * 512
            for k in range(8):

                @pl.when(source == k)
                def _():
                    fc_ref[:, column : column + 512] = refs[k][rows, :512].astype(f32)

                    @pl.when(j == core * 4 + number)
                    def _():
                        for q in range(4):
                            part = slice(128 * q, 128 * (q + 1))
                            columns = slice(256 * q, 256 * (q + 1))
                            proj_ref[:128, columns] = refs[k][part, 512:768].astype(f32)
                            proj_ref[128:, columns] = refs[k][part, 768:].astype(f32)

    return stepped(
        body,
        8,
        table,
        arrays,
        [pl.BlockSpec(memory_space=pltpu.VMEM)] * 8,
        [shape((512, 4096), f32), shape((2048, D), f32)],
        [block((64, 4096), lambda j, t: (j, 0)), block((256, D), lambda j, t: (j, 0))],
        cost(0.5),
        near=True,
    )


def unpack_attention(table, arrays):
    def body(t, *refs):
        arrays, qkv_ref, out_ref, vectors = refs[:8], refs[8], refs[9], refs[10:]
        rows = span(pl.program_id(0) * 64, 64)
        for core, number, source in sources(t):
            number += core * 4
            for k in range(8):

                @pl.when(source == k)
                def _():
                    qkv_ref[:, 384 * number : 384 * (number + 1)] = arrays[k][rows, :384].astype(f32)
                    out_ref[:, 128 * number : 128 * (number + 1)] = arrays[k][rows, 384:].astype(f32)

        @pl.when(pl.program_id(0) == 0)
        def _():
            sums = arrays[0][512:, :].astype(f32)
            for ref in arrays[1:]:
                sums += ref[512:, :].astype(f32)
            for k in range(8):
                vectors[k][...] = sums[k : k + 1, :].reshape(512)
            for k in range(4):
                vectors[8][pl.ds(512 * k, 512)] = sums[8 + k : 9 + k, :].reshape(512)

    vector = pl.BlockSpec((512,), lambda j, t: (0,))
    return stepped(
        body,
        8,
        table,
        arrays,
        [pl.BlockSpec(memory_space=pltpu.VMEM)] * 8,
        [shape((512, 3 * D), f32), shape((512, D), f32)] + [shape((512,), f32)] * 8 + [shape((2048,), f32)],
        [block((64, 3 * D), lambda j, t: (j, 0)), block((64, D), lambda j, t: (j, 0))]
        + [vector] * 8
        + [pl.BlockSpec((2048,), lambda j, t: (0,))],
        cost(0.5),
        near=True,
    )


def cut(array, start, size, axis):
    return lax.dynamic_slice_in_dim(array, start, size, axis)


def both(upper, lower):
    return jnp.concatenate([upper, lower], 0)


def zero(t):
    return 0


ROUND = ("z", "x", "xz")
DEALT = ("xz", "x", "z")


def send_quarters(quarters):
    return [swap(array, SECOND[name]) for array, name in zip(quarters, DEALT)]


def send_round(array):
    return [swap(array, FIRST[name]) for name in ROUND]


def share(array, first, second, *others):
    near = swap(array, FIRST[first])
    far = swap(after(both(array, near), *others), FIRST[second])
    size = array.shape[0]
    by = {first: (near, 0, zero), second: (far, 0, zero)}
    return [(array, 0, zero), by["x"], by["z"], (far, size, zero)]


def send_dealt(dealt, others):
    across, over_x, over_z, own = dealt
    across = swap(across, FIRST["xz"])
    over_x = swap(over_x, FIRST["x"])
    over_z = swap(over_z, FIRST["z"])
    return [(array, 0, zero) for array in (own, over_x, over_z, across)]


def shards(
    block_input,
    segment_ids,
    ln1_gain,
    ln1_bias,
    w_qkv,
    b_query,
    b_value,
    w_out,
    b_out,
    ln2_gain,
    ln2_bias,
    w_fc,
    b_fc,
    w_proj,
    b_proj,
    cotangent,
):
    MADE.clear()
    device = lax.axis_index("group") * 64 + lax.axis_index("replica")
    table = lax.dynamic_slice(jnp.asarray(numbers()), (device, 0), (1, NUMBERS)).reshape(NUMBERS)
    c = table[C]

    first, out_part, fc_part = pack(
        table, block_input, w_out, w_fc,
        (ln1_gain, ln1_bias, b_query, b_value, b_out, ln2_gain, ln2_bias, b_proj, b_fc),
    )
    first_other = swap(first, FIRST["g"])
    fc_near = swap(after(fc_part, first), FIRST["g"])
    cotangent_both = both(cotangent, swap(after(cotangent, first), CORE))
    cotangent_x = swap(cotangent_both, FIRST["x"])
    proj_parts = [cut(after(w_proj, first), c * 1024 + 512 * k, 512, 0) for k in range(2)]
    qkv_part = cut(after(w_qkv, first), c * 256, 256, 0)
    part_mine, part_theirs = project(
        after(table, cotangent_both, proj_parts, qkv_part), first, first_other, ln1_gain, ln1_bias, w_qkv
    )
    part_theirs = swap(part_theirs, FIRST["g"])
    full, fc_bias, normed_one = spread(after(table, part_mine, fc_near, cotangent_x), first, first_other)
    fc_z = swap(after(fc_near, part_mine), FIRST["z"])
    out_near = swap(after(out_part, part_mine), FIRST["g"])
    normed_sibling = swap(normed_one, CORE)
    fc_pair = both(fc_near, fc_z)
    fc_x = swap(fc_pair, FIRST["x"])
    fc_quarters = [fc_near, fc_z, fc_x]
    normed_ones = both(normed_one, normed_sibling)
    cotangent_pair = both(cotangent_both, cotangent_x)
    cotangent_z = swap(after(cotangent_pair, fc_z), FIRST["z"])

    projected, mixture = mix(after(table, normed_ones), part_mine, part_theirs, full, segment_ids)
    proj_first = swap(after(proj_parts[0], part_theirs), FIRST["g"])
    out_far = swap(after(out_near, mixture), CORE)
    side, residual = settle(
        after(table, cotangent_z), mixture, block_input, full, w_out, out_near, out_far
    )
    normed_ones_z = swap(after(normed_ones, cotangent_z), FIRST["z"])
    side_theirs = swap(side, CORE)
    normed_twos = both(side[:, :D], side_theirs[:, :D])
    mixtures = both(side[:, D:], side_theirs[:, D:])
    hidden, slope = expand(after(table, normed_ones_z), normed_twos, w_fc, fc_quarters, fc_bias)
    proj_second = swap(after(proj_parts[1], proj_first), FIRST["g"])
    normed_twos_x = swap(normed_twos, FIRST["x"])
    mixtures_z = swap(after(mixtures, normed_ones_z), FIRST["z"])
    normed_ones_x = swap(both(normed_ones, normed_ones_z), FIRST["x"])

    grad_pre, fc_sums = hidden_back(
        after(table, normed_twos_x, mixtures_z), cotangent_both, slope, w_proj, (proj_first, proj_second)
    )
    qkv_near = swap(after(qkv_part, grad_pre), FIRST["g"])
    normed_twos_z = swap(both(normed_twos, normed_twos_x), FIRST["z"])
    back_mine, back_theirs = normed_back(after(table, normed_ones_x), grad_pre, w_fc, fc_quarters)
    back_theirs = swap(back_theirs, CORE)
    feed_dealt = deal_feed(after(table, back_mine), hidden, grad_pre)
    feeds = send_dealt(feed_dealt, None)
    mixtures_x = swap(after(both(mixtures, mixtures_z), normed_ones_x), FIRST["x"])

    def pieces_of(own, x, z, last):
        found = [(own, 0, zero), (x, 0, zero), (z, 0, zero)]
        return found + [(x, BOTH, zero) if last == "x" else (z, BOTH, zero)]

    grad_residual, dealt, sums = attend_back(
        after(table, feed_dealt, normed_twos_z), back_mine, back_theirs, residual, cotangent, full,
        projected, segment_ids, w_out, out_near, out_far,
    )
    dealt_theirs = swap(lax.dynamic_index_in_dim(dealt, 1 - c, 0, False), CORE)
    attention_dealt = deal_attention(table, dealt, dealt_theirs)
    attention_grads = send_dealt(attention_dealt, None)
    qkv_far = swap(after(qkv_near, attention_dealt), CORE)
    feed_pieces = [
        pieces_of(normed_twos, normed_twos_x, normed_twos_z, "z"),
        feeds,
        feeds,
        pieces_of(cotangent_both, cotangent_x, cotangent_z, "z"),
    ]
    feed_out = feed_sent(after(table, attention_dealt), *feed_pieces)
    feed_received = swap(feed_out, FIRST["g"])
    input_grad, sums = input_back(
        after(table, feed_out), dealt, w_qkv, qkv_near, qkv_far, block_input, grad_residual, full, sums, fc_sums
    )

    attention_pieces = [
        pieces_of(normed_ones, normed_ones_x, normed_ones_z, "x"),
        pieces_of(mixtures, mixtures_x, mixtures_z, "x"),
        attention_grads,
    ]
    out = attention_sent(after(table, sums), *attention_pieces, sums)
    received = swap(out, FIRST["g"])
    *feed, feed_kept = feed_total(after(table, out), *feed_pieces, feed_received)
    feed = send_quarters(feed)
    sent, kept, sums = attention_total(after(table, feed_kept), *attention_pieces, received, sums)
    received = swap(sent, SECOND["x"])
    feed = add_up(after(table, kept), feed_kept, feed)
    feed_far = swap(feed, FAR)
    sent, kept, sums = add_split(after(table, feed), kept, received, sums)
    received = swap(sent, SECOND["z"])
    feed = add_up(after(table, kept), feed, [feed_far])
    feed_others = [swap(feed, SECOND[name]) for name in DEALT]
    low = add_low(after(table, feed), kept, received, sums)
    far = swap(low, FAR)
    feed = place_quarters(after(table, low), feed, feed_others)
    feed_z = swap(feed, FIRST["z"])
    feed_x = swap(feed, FIRST["x"])
    low, sums = add_far(after(table, feed), low, far, EXTRA)
    low = place(table, VZ, low, swap(low, SECOND["z"]))
    other = swap(low, SECOND["x"])
    feed_xz = swap(after(feed_z, low), FIRST["x"])
    attention = place(table, VX, low, other, sums)
    attentions = [attention, *send_round(attention)]
    output_mine, output_theirs = contract(after(table, attention), hidden, w_proj, (proj_first, proj_second))
    result = (residual + (output_mine + swap(output_theirs, CORE) + full[7:8])).astype(bf16)
    feeds = [feed, feed_z, feed_x, feed_xz]
    feeds += [swap(after(array, attention), CORE) for array in feeds]
    fc_grad, proj_grad = unpack_feed(after(table, result), feeds)
    attentions = attentions + [swap(array, CORE) for array in attentions]
    qkv_grad, out_grad, *vectors = unpack_attention(after(table, fc_grad), attentions)
    return (
        result,
        input_grad,
        vectors[0],
        vectors[1],
        qkv_grad,
        vectors[2],
        vectors[3],
        out_grad,
        vectors[4],
        vectors[5],
        vectors[6],
        fc_grad,
        vectors[8],
        proj_grad,
        vectors[7],
    )


def solution(mesh):
    rows = P(("group", "replica"), None)
    vector = P("group")
    matrix = P("group", None)
    vectors_in = (vector, vector, matrix, vector, vector, matrix, vector, vector, vector, matrix, vector, matrix, vector)
    return jax.shard_map(
        shards,
        mesh=mesh,
        in_specs=(rows, rows) + vectors_in + (rows,),
        out_specs=(rows, rows) + vectors_in,
        check_vma=False,
    )
```

```python
import math

import jax
import jax.numpy as jnp
import numpy as np
from jax import lax
from jax.experimental import pallas as pl
from jax.experimental.pallas import tpu as pltpu
from jax.sharding import PartitionSpec as P

D = 1024
HEADS = 16
BATCH = 8
HEAD_DIM = 64
ROWS = 128
BOTH = 2 * ROWS
EXTRA = 16

norm_epsilon = 1e-05
masked_score = -1e30
gelu_factor = 0.7978845608028654
score_scale = 1.0 / math.sqrt(HEAD_DIM)

f32 = jnp.float32
bf16 = jnp.bfloat16
AXES = ("group", "replica")
MIB = 2**20


def flat(g, yh, x, z, c):
    return (((g * 2 + yh) * 4 + x) * 4 + z) * 2 + c


def at(y, x, z, c):
    return flat(y % 2, y // 2, x, z, c)


def everywhere():
    return [(g, yh, x, z, c) for g in range(2) for yh in range(2) for x in range(4) for z in range(4) for c in range(2)]


def exchange(move):
    return [(flat(g, yh, x, z, c), move(2 * yh + g, x, z, c)) for g, yh, x, z, c in everywhere()]


FIRST = {
    "g": exchange(lambda y, x, z, c: at(y ^ (1, 3)[c], x, z, c)),
    "x": exchange(lambda y, x, z, c: at(y, x ^ (1, 3)[c], z, c)),
    "z": exchange(lambda y, x, z, c: at(y, x, z ^ (1, 3)[c], c)),
    "xz": exchange(lambda y, x, z, c: at(y, x ^ (1, 3)[c], z ^ (1, 3)[c], c)),
}
SECOND = {
    "x": exchange(lambda y, x, z, c: at(y, x ^ (3, 1)[c], z, c)),
    "z": exchange(lambda y, x, z, c: at(y, x, z ^ (3, 1)[c], c)),
    "xz": exchange(lambda y, x, z, c: at(y, x ^ (3, 1)[c], z ^ (3, 1)[c], c)),
}
FAR = exchange(lambda y, x, z, c: at(y ^ 2, x, z, c))
CORE = exchange(lambda y, x, z, c: at(y, x, z, c ^ 1))


def swap(array, pairs):
    return lax.ppermute(array, AXES, pairs)


def after(value, *others):
    return lax.optimization_barrier((value, others))[0]


G, C, UX, UZ, VX, VZ = range(6)
PIECE = 6
QUARTER = 9
NUMBERS = 16


def numbers():
    rows = []
    for g, yh, x, z, c in everywhere():
        xs = ((x % 2) ^ (x // 2), x // 2)
        zs = ((z % 2) ^ (z // 2), z // 2)
        ux, vx, uz, vz = xs[c], xs[1 - c], zs[c], zs[1 - c]
        base = (1 - g) * 512
        row = [g, c, ux, uz, vx, vz, g * 512, base + c * 256, base + (1 - c) * 256]
        row += [base + ((ux ^ rx) * 2 + (uz ^ rz)) * 128 for rx in range(2) for rz in range(2)]
        rows.append(row + [0] * (NUMBERS - len(row)))
    return np.array(rows, np.int32)


def cost(us):
    return pl.CostEstimate(flops=0, bytes_accessed=int(us * 3.69e6), transcendentals=0)


def shape(dims, dtype):
    return jax.ShapeDtypeStruct(dims, dtype)


def dot(left, right):
    return jnp.dot(left, right, preferred_element_type=f32)


def rows_dot(left, right):
    return lax.dot_general(left, right, (((0,), (0,)), ((), ())), preferred_element_type=f32)


def dot_rows(left, right):
    return lax.dot_general(left, right, (((1,), (1,)), ((), ())), preferred_element_type=f32)


def span(start, size):
    return pl.ds(pl.multiple_of(start, size), size)


def norm_parts(values):
    center = jnp.mean(values, axis=-1, keepdims=True)
    centered = values - center
    variance = jnp.mean(centered * centered, axis=-1, keepdims=True)
    scale = lax.rsqrt(variance + norm_epsilon)
    return centered * scale, scale


def norm_back(normal, scale, grad):
    return scale * (
        grad
        - jnp.mean(grad, axis=-1, keepdims=True)
        - normal * jnp.mean(grad * normal, axis=-1, keepdims=True)
    )


def over(values):
    return jnp.sum(values, axis=0, keepdims=True)


MADE = []


def stepped(body, steps, table, operands, in_specs, outputs, out_specs, estimate, scratch=(), limit=32, near=False):
    operands = [
        pltpu.with_memory_space_constraint(array, pltpu.HBM)
        if not near and array.size >= 32768 and not any(array is made for made in MADE)
        else array
        for array in operands
    ]
    results = pl.pallas_call(
        body,
        grid_spec=pltpu.PrefetchScalarGridSpec(
            num_scalar_prefetch=1,
            grid=(steps,),
            in_specs=in_specs,
            out_specs=out_specs,
            scratch_shapes=list(scratch),
        ),
        out_shape=outputs,
        compiler_params=pltpu.CompilerParams(vmem_limit_bytes=limit * MIB),
        cost_estimate=estimate,
    )(table, *operands)
    MADE.extend(jax.tree.leaves(results))
    return results


def block(dims, place):
    return pl.BlockSpec(dims, place)


def fixed(dims, row=0, column=0):
    place = (row, column) if len(dims) == 2 else (0,) * len(dims)
    return pl.BlockSpec(dims, lambda j, t: place)


FIRST_ROWS = 256 + ROWS + EXTRA


def pack(table, inputs, w_out, w_fc, vectors):
    def body(t, in_ref, out_ref, low_ref, high_ref, *refs):
        first, fc_part = refs[9:]
        first[:256, :] = out_ref[...]
        first[256:384, :] = in_ref[...]
        first[384:, :] = jnp.zeros((EXTRA, D), bf16)
        for k in range(8):
            first[384 + k // 2 : 385 + k // 2, 512 * (k % 2) : 512 * (k % 2) + 512] = refs[k][...].reshape(1, 512)
        for k in range(2):
            first[388 + k : 389 + k, :] = refs[8][pl.ds(1024 * k, 1024)].reshape(1, 1024)
        fc_part[:, :1024] = low_ref[...]
        fc_part[:, 1024:] = high_ref[...]

    outputs = [shape((FIRST_ROWS, D), bf16), shape((128, 2048), bf16)]
    return stepped(
        body,
        1,
        table,
        (inputs, w_out, w_fc, w_fc, *vectors),
        [
            fixed((ROWS, D)),
            block((256, D), lambda j, t: (t[C], 0)),
            block((128, 1024), lambda j, t: (t[UX] * 2 + t[UZ], t[C])),
            block((128, 1024), lambda j, t: (t[UX] * 2 + t[UZ], 2 + t[C])),
        ]
        + [pl.BlockSpec(v.shape, lambda j, t: (0,)) for v in vectors],
        outputs,
        [fixed(o.shape) for o in outputs],
        cost(3.6),
        limit=60,
    )


def spread(table, own, other):
    def body(t, own_ref, other_ref, full_ref, bias_ref):
        first = t[G] == 0
        mine = own_ref[...].astype(f32)[:8]
        theirs = other_ref[...].astype(f32)[:8]
        low = jnp.where(first, mine, theirs)
        high = jnp.where(first, theirs, mine)
        for k in range(8):
            half = slice(512 * (k % 2), 512 * (k % 2) + 512)
            full_ref[k : k + 1, :512] = low[k // 2 : k // 2 + 1, half]
            full_ref[k : k + 1, 512:] = high[k // 2 : k // 2 + 1, half]
        second = t[C] == 1
        bias_ref[:, :1024] = jnp.where(second, low[5:6], low[4:5])
        bias_ref[:, 1024:] = jnp.where(second, high[5:6], high[4:5])

    tail = fixed((EXTRA, D), 384 // EXTRA)
    return stepped(
        body,
        1,
        table,
        (own, other),
        [tail, tail],
        [shape((8, D), f32), shape((1, 2048), f32)],
        [fixed((8, D)), fixed((1, 2048))],
        cost(1),
    )


def project(table, own, other, gain, shift, w_qkv):
    width = 512

    def body(t, own_ref, other_ref, gain_ref, shift_ref, w_ref, mine_ref, theirs_ref, normed_ref):
        @pl.when(pl.program_id(0) == 0)
        def _():
            half = span(t[PIECE], 512)
            scale = gain_ref[...].astype(f32).reshape(1, 512)
            offset = shift_ref[...].astype(f32).reshape(1, 512)
            for k, ref in enumerate((own_ref, other_ref)):
                values = ref[...].astype(f32)
                center = jnp.mean(values, axis=-1, keepdims=True)
                centered = values - center
                variance = jnp.mean(centered * centered, axis=-1, keepdims=True)
                part = (ref[:, half].astype(f32) - center) * lax.rsqrt(variance + norm_epsilon)
                normed_ref[k * ROWS : (k + 1) * ROWS, :] = (part * scale + offset).astype(bf16)

        total = dot(normed_ref[...], w_ref[...])
        mine_ref[...] = total[:ROWS]
        theirs_ref[...] = total[ROWS:].astype(bf16)

    step = lambda j, t: (0, j)
    vector = pl.BlockSpec((512,), lambda j, t: (0,))
    return stepped(
        body,
        6,
        table,
        (own, other, gain, shift, w_qkv),
        [fixed((ROWS, D), 2), fixed((ROWS, D), 2), vector, vector, block((512, width), step)],
        [shape((ROWS, 3 * D), f32), shape((ROWS, 3 * D), bf16)],
        [block((ROWS, width), step), block((ROWS, width), step)],
        cost(8),
        [pltpu.VMEM((BOTH, 512), bf16)],
    )


def admitted(segments_ref):
    across = jnp.broadcast_to(segments_ref[...], (ROWS, ROWS))
    down = across.T
    row = lax.broadcasted_iota(jnp.int32, (ROWS, ROWS), 0)
    column = lax.broadcasted_iota(jnp.int32, (ROWS, ROWS), 1)
    return (row >= column) & (across == down)


def cut_heads(ref, first, heads):
    return [ref[:, first + head * HEAD_DIM : first + (head + 1) * HEAD_DIM] for head in heads]


def head_probs(projected_ref, heads, allowed):
    queries, keys, values = (cut_heads(projected_ref, k * D, heads) for k in range(3))
    scores = [jnp.where(allowed, dot_rows(q, k) * score_scale, masked_score) for q, k in zip(queries, keys)]
    weights = [jnp.exp(x - jnp.max(x, axis=-1, keepdims=True)) for x in scores]
    return queries, keys, values, [x / jnp.sum(x, axis=-1, keepdims=True) for x in weights]


def mix(table, mine, theirs, full, segments):
    def body(t, mine_ref, theirs_ref, full_ref, seg_ref, p_ref, mixture_ref):
        for k, row in ((0, 2), (1, None), (2, 3)):
            columns = slice(k * D, (k + 1) * D)
            total = mine_ref[:, columns] + theirs_ref[:, columns].astype(f32)
            if row is not None:
                total += full_ref[row : row + 1, :]
            p_ref[:, columns] = total.astype(bf16)
        allowed = admitted(seg_ref)
        _, _, values, probs = head_probs(p_ref, range(HEADS), allowed)
        outputs = [dot(p.astype(bf16), v).astype(bf16) for p, v in zip(probs, values)]
        for head, output in enumerate(outputs):
            mixture_ref[:, head * HEAD_DIM : (head + 1) * HEAD_DIM] = output

    return stepped(
        body,
        1,
        table,
        (mine, theirs, full, segments),
        [fixed((ROWS, 3 * D)), fixed((ROWS, 3 * D)), fixed((8, D)), fixed((1, ROWS))],
        [shape((ROWS, 3 * D), bf16), shape((ROWS, D), bf16)],
        [fixed((ROWS, 3 * D)), fixed((ROWS, D))],
        cost(8.1),
    )


def settle(table, mixture, inputs, full, w_out, near, far):
    def body(t, mixture_ref, in_ref, full_ref, own, a, b, side_ref, residual_ref):
        total = dot(mixture_ref[:, span(t[PIECE], 512)], own[...])
        for k, ref in enumerate((a, b)):
            total += dot(mixture_ref[:, span(t[PIECE + 1 + k], 256)], ref[...])
        residual = in_ref[...].astype(f32) + (total + full_ref[4:5, :])
        residual_ref[...] = residual
        normal, _ = norm_parts(residual)
        side_ref[:, :D] = (normal * full_ref[5:6, :] + full_ref[6:7, :]).astype(bf16)
        side_ref[:, D:] = mixture_ref[...]

    return stepped(
        body,
        1,
        table,
        (mixture, inputs, full, w_out, near, far),
        [fixed((ROWS, D)), fixed((ROWS, D)), fixed((8, D)), fixed((512, D)), fixed((256, D)), fixed((256, D))],
        [shape((ROWS, 2 * D), bf16), shape((ROWS, D), f32)],
        [fixed((ROWS, 2 * D)), fixed((ROWS, D))],
        cost(3),
    )


def feed_forward(table, side, early, w_fc, quarters, bias, w_proj, others, full):
    def units(j, t):
        return jnp.where(j % 4 < 2, t[G], 1 - t[G]) * 2 + j % 2

    def body(t, *refs):
        side_ref, early_refs, own_fc, pieces_fc = refs[0], refs[1:5], refs[5], refs[6:10]
        bias_ref, low_ref, high_ref, own_proj, first_proj, second_proj, full_ref = refs[10:17]
        hidden_ref, grad_ref, sums_ref, back_mine, back_theirs, out_mine, out_theirs, normed_ref, slope_ref = refs[17:]
        j = pl.program_id(0)
        k = j % 4
        columns = span(units(j, t) * 512, 512)

        @pl.when(j < 4)
        def _():
            here = span(k * 512, 512)
            values = dot(side_ref[:, span(t[PIECE], 512)], own_fc[...])
            for i, ref in enumerate(pieces_fc):
                values += dot(side_ref[:, span(t[QUARTER + i], 128)], ref[:, here])
            values += bias_ref[:, here]
            square = values * values
            inner = jnp.tanh(gelu_factor * values * (1.0 + 0.044715 * square))
            outer = 0.5 * (1.0 + inner)
            hidden_ref[:, here] = (values * outer).astype(bf16)
            slope_ref[:, here] = outer + values * outer * (1.0 - inner) * gelu_factor * (1.0 + 3.0 * 0.044715 * square)

        def with_proj(use):
            for ref, wanted in ((own_proj, k < 2), (first_proj, k == 2), (second_proj, k == 3)):

                @pl.when(wanted)
                def _():
                    use(ref[...])

        @pl.when((j >= 4) & (j < 8))
        def _():
            def use(weights):
                grad = (dot_rows(early_refs[0][:, :D], weights) * slope_ref[:, columns]).astype(bf16)
                grad_ref[:, columns] = grad
                sums_ref[:, columns] = over(grad.astype(f32))

            with_proj(use)

        @pl.when((j >= 8) & (j < 12))
        def _():
            def use(low, high, first, size):
                total = dot_rows(grad_ref[:, :1024], low) + dot_rows(grad_ref[:, 1024:], high)
                back_mine[:, span(first, size)] = total[:ROWS]
                back_theirs[:, span(first, size)] = total[ROWS:]

            @pl.when(k < 2)
            def _():
                use(low_ref[...], high_ref[...], t[G] * 512 + k * 256, 256)

            for step in (2, 3):

                @pl.when(k == step)
                def _():
                    for i in (2 * step - 4, 2 * step - 3):
                        use(pieces_fc[i][:, :1024], pieces_fc[i][:, 1024:], t[QUARTER + i], 128)

        @pl.when((j >= 12) & (j < 16))
        def _():
            def use(weights):
                total = dot(hidden_ref[:, columns], weights)

                @pl.when(k == 0)
                def _():
                    out_mine[...] = total[:ROWS]
                    out_theirs[...] = total[ROWS:]

                @pl.when(k > 0)
                def _():
                    out_mine[...] += total[:ROWS]
                    out_theirs[...] += total[ROWS:]

            with_proj(use)

        for i, ref in enumerate(early_refs):

            @pl.when(j == 16 + i)
            def _():
                normal, _ = norm_parts(ref[:, D:].astype(f32))
                normed_ref[...] = (normal * full_ref[0:1, :] + full_ref[1:2, :]).astype(bf16)

    def back_rows(j):
        return jnp.clip(j - 8, 0, 1)

    def proj_rows(j, t):
        return (t[C] * 2 + jnp.where((j == 4) | (j < 4) | (j == 12), 0, 1), 0)

    square = fixed((ROWS, D))
    return stepped(
        body,
        20,
        table,
        (side, *early, w_fc, *quarters, bias, w_fc, w_fc, w_proj, *others, full),
        [fixed((BOTH, D))]
        + [fixed((BOTH, 2 * D))] * 4
        + [block((512, 512), lambda j, t: (0, jnp.minimum(j, 3) // 2 * 4 + t[C] * 2 + jnp.minimum(j, 3) % 2))]
        + [fixed((128, 2048), row) for row in (0, 0, 0, 1)]
        + [fixed((1, 2048))]
        + [block((256, 1024), lambda j, t: (back_rows(j), t[C])), block((256, 1024), lambda j, t: (back_rows(j), 2 + t[C]))]
        + [block((512, D), proj_rows), fixed((512, D)), fixed((512, D)), fixed((8, D))],
        [shape((BOTH, 2048), bf16), shape((BOTH, 2048), bf16), shape((1, 2048), f32)]
        + [shape((ROWS, D), f32)] * 4
        + [shape((4 * BOTH, D), bf16)],
        [fixed((BOTH, 2048)), fixed((BOTH, 2048)), fixed((1, 2048)), square, square, square, square]
        + [block((BOTH, D), lambda j, t: (jnp.clip(j - 16, 0, 3), 0))],
        cost(23),
        [pltpu.VMEM((BOTH, 2048), f32)],
        limit=48,
    )


def attend_back(table, mine, theirs, residual, cotangent, full, projected, segments, w_out, near, far):
    def body(
        t, mine_ref, theirs_ref, res_ref, cot_ref, full_ref, p_ref, seg_ref, own, a, b,
        grad_ref, dealt_ref, sums_ref, mix_ref,
    ):
        normal, scale = norm_parts(res_ref[...])
        grad_normed = mine_ref[...] + theirs_ref[...]
        grad_output = cot_ref[...].astype(f32)
        grad = grad_output + norm_back(normal, scale, grad_normed * full_ref[5:6, :])
        grad_ref[...] = grad
        low = grad.astype(bf16)
        for k in range(8):
            dealt_ref[k // 4, :, 512 * (k % 4) + 384 : 512 * (k % 4) + 512] = low[:, 128 * k : 128 * (k + 1)]
        sums_ref[0:1, :] = over(grad)
        sums_ref[1:2, :] = over(grad_normed * normal)
        sums_ref[2:3, :] = over(grad_normed)
        sums_ref[3:4, :] = over(grad_output)
        sums_ref[4:, :] = jnp.zeros((4, D), f32)
        mix_ref[:, span(t[PIECE], 512)] = dot_rows(low, own[...]).astype(bf16)
        for k, ref in enumerate((a, b)):
            mix_ref[:, span(t[PIECE + 1 + k], 256)] = dot_rows(low, ref[...]).astype(bf16)
        allowed = admitted(seg_ref)

        def store(number, values):
            column = 512 * (number % 24 // 6) + HEAD_DIM * (number % 6)
            dealt_ref[number // 24, :, column : column + HEAD_DIM] = values.astype(bf16)

        for first in range(0, HEADS, BATCH):
            heads = range(first, first + BATCH)
            queries, keys, values, probs = head_probs(p_ref, heads, allowed)
            grad_mix = cut_heads(mix_ref, 0, heads)
            grad_probs = [dot_rows(g, v) for g, v in zip(grad_mix, values)]
            centres = [jnp.sum(p * g, axis=-1, keepdims=True) for p, g in zip(probs, grad_probs)]
            grad_scores = [(p * (g - x)).astype(bf16) for p, g, x in zip(probs, grad_probs, centres)]
            found = (
                [dot(g, k) * score_scale for g, k in zip(grad_scores, keys)],
                [rows_dot(g, q) * score_scale for g, q in zip(grad_scores, queries)],
                [rows_dot(p.astype(bf16), g) for p, g in zip(probs, grad_mix)],
            )
            for kind, results in enumerate(found):
                for head, result in zip(heads, results):
                    store(kind * HEADS + head, result)

    square = fixed((ROWS, D))
    return stepped(
        body,
        1,
        table,
        (mine, theirs, residual, cotangent, full, projected, segments, w_out, near, far),
        [square] * 4 + [fixed((8, D)), fixed((ROWS, 3 * D)), fixed((1, ROWS))]
        + [fixed((512, D)), fixed((256, D)), fixed((256, D))],
        [shape((ROWS, D), f32), shape((2, ROWS, 2048), bf16), shape((8, D), f32)],
        [square, fixed((2, ROWS, 2048)), fixed((8, D))],
        cost(11.5),
        [pltpu.VMEM((ROWS, D), bf16)],
    )


def input_back(table, dealt, w_qkv, near, far, inputs, grad_residual, full, sums, fc_sums):
    width = 384

    def body(t, grad_ref, own, a, b, in_ref, res_ref, full_ref, early_ref, fc_ref, out_ref, sums_ref, total_ref, bias_ref):
        j = pl.program_id(0)
        grad = grad_ref[0, :, :width]

        @pl.when(j == 0)
        def _():
            total_ref[...] = jnp.zeros((ROWS, D), f32)

        offset = 0
        for ref in (own, a, b):
            size = ref.shape[0]
            total_ref[:, offset : offset + size] += dot_rows(grad, ref[...])
            offset += size
        bias_ref[:, span(j * width, width)] = over(grad.astype(f32))

        @pl.when(j == 7)
        def _():
            offset = 0
            for k, size in enumerate((512, 256, 256)):
                out_ref[:, span(t[PIECE + k], size)] = total_ref[:, offset : offset + size]
                offset += size
            grad_normed = out_ref[...]
            normal, scale = norm_parts(in_ref[...].astype(f32))
            gain_sums = over(grad_normed * normal)
            shift_sums = over(grad_normed)
            out_ref[...] = res_ref[...] + norm_back(normal, scale, grad_normed * full_ref[0:1, :])
            row = lax.broadcasted_iota(jnp.int32, (4, 512), 0)
            for g in range(2):
                half = slice(512 * g, 512 * (g + 1))
                sums_ref[16 * g : 16 * g + 1, :] = gain_sums[:, half]
                sums_ref[16 * g + 1 : 16 * g + 2, :] = shift_sums[:, half]
                sums_ref[16 * g + 2 : 16 * g + 3, :] = bias_ref[:, 512 * g : 512 * (g + 1)]
                sums_ref[16 * g + 3 : 16 * g + 4, :] = bias_ref[:, 2048 + 512 * g : 2048 + 512 * (g + 1)]
                sums_ref[16 * g + 4 : 16 * g + 8, :] = early_ref[0:4, half]
                units = [fc_ref[:, 1024 * g + 512 * (k % 2) : 1024 * g + 512 * (k % 2) + 512] for k in range(4)]
                sums_ref[16 * g + 8 : 16 * g + 12, :] = jnp.where(row // 2 == t[C], jnp.concatenate(units, 0), 0.0)
                sums_ref[16 * g + 12 : 16 * g + 16, :] = jnp.zeros((4, 512), f32)

    step = lambda j, t: (0, j)
    return stepped(
        body,
        8,
        table,
        (dealt, w_qkv, near, far, inputs, grad_residual, full, sums, fc_sums),
        [pl.BlockSpec((1, ROWS, 512), lambda j, t: (j // 4, 0, j % 4)), block((512, width), step)]
        + [block((256, width), step)] * 2
        + [fixed((ROWS, D)), fixed((ROWS, D)), fixed((8, D)), fixed((8, D)), fixed((1, 2048))],
        [shape((ROWS, D), f32), shape((2 * EXTRA, 512), f32)],
        [fixed((ROWS, D)), fixed((2 * EXTRA, 512))],
        cost(9.2),
        [pltpu.VMEM((ROWS, D), f32), pltpu.VMEM((1, 3 * D), f32)],
    )


def piece_specs(pieces, width, number):
    specs, operands = [], []
    for array, row, column in pieces:
        specs.append(
            pl.BlockSpec(
                (BOTH, width),
                lambda j, t, row=row, column=column: (row(t) if callable(row) else row, column + number(j, t)),
            )
        )
        operands.append(array)
    return specs, operands


def sum_dots(lefts, rights, columns=slice(None)):
    total = rows_dot(lefts[0][...], rights[0][:, columns])
    for left, right in zip(lefts[1:], rights[1:]):
        total += rows_dot(left[...], right[:, columns])
    return total


def deal_feed(table, hidden, grad_pre):
    def body(t, hidden_ref, grad_ref, *outs):
        for j, out in enumerate(outs):
            away = 3 - j
            bx, bz = (away // 2) ^ t[UX], (away % 2) ^ t[UZ]
            for g in range(2):
                out[:, 256 * g : 256 * (g + 1)] = hidden_ref[:, span(g * 1024 + (bx * 2 + bz) * 256, 256)]
            out[:, 512:] = grad_ref[:, span((bx * 2 + bz) * 512, 512)]

    return stepped(
        body, 1, table, (hidden, grad_pre), [fixed((BOTH, 2048))] * 2, [shape((BOTH, D), bf16)] * 4,
        [fixed((BOTH, D))] * 4, cost(0.8), near=True,
    )


def deal_attention(table, mine, theirs):
    def body(t, mine_ref, theirs_ref, *outs):
        for j, out in enumerate(outs):
            away = 3 - j
            columns = span((((away // 2) ^ t[UX]) * 2 + ((away % 2) ^ t[UZ])) * 512, 512)
            out[:ROWS, :] = mine_ref[0, :, columns]
            out[ROWS:, :] = theirs_ref[:, columns]

    return stepped(
        body, 1, table, (mine, theirs),
        [pl.BlockSpec((1, ROWS, 2048), lambda j, t: (t[C], 0, 0)), fixed((ROWS, 2048))],
        [shape((BOTH, 512), bf16)] * 4, [fixed((BOTH, 512))] * 4, cost(0.7), near=True,
    )


def quarter(j, t):
    away = 3 - j
    return ((away // 2) ^ t[VX]) * 2 + ((away % 2) ^ t[VZ])


def half_rows(j, t):
    return jnp.where(j == 0, 1 - t[VX], t[VX])


def feed_specs(normeds, grads, hiddens, cotangents, rows, width, features, units, columns):
    specs, operands = [], []
    for pieces, size, number in (
        (normeds, rows, features),
        (grads, 512, lambda j, t: 1),
        (hiddens, 256, units),
        (cotangents, width, columns),
    ):
        more, arrays = piece_specs(pieces, size, number)
        specs += more
        operands += arrays
    return specs, operands


def feed_sent(table, normeds, grads, hiddens, cotangents):
    specs, operands = feed_specs(
        normeds, grads, hiddens, cotangents, 256, 512,
        lambda j, t: (1 - t[G]) * 2 + j, lambda j, t: 1 - t[G], lambda j, t: j,
    )

    def body(t, *refs):
        out = refs[-1]
        out[:, :512] = sum_dots(refs[:4], refs[4:8]).astype(bf16)
        units = sum_dots(refs[8:12], refs[12:16]).astype(bf16)
        for q in range(2):
            rows, columns = slice(128 * q, 128 * (q + 1)), slice(256 * q, 256 * (q + 1))
            out[rows, 512:768] = units[:128, columns]
            out[rows, 768:] = units[128:, columns]

    return stepped(
        body, 2, table, operands, specs, shape((512, D), bf16), block((256, D), lambda j, t: (j, 0)), cost(4.3),
    )


def feed_total(table, normeds, grads, hiddens, cotangents, received):
    specs, operands = feed_specs(
        normeds, grads, hiddens, cotangents, 128, 256,
        lambda j, t: t[G] * 4 + quarter(j, t), lambda j, t: t[G], quarter,
    )

    def body(t, *refs):
        received_ref = refs[16]
        outs = refs[17:]
        j = pl.program_id(0)
        got = received_ref[...].astype(f32)
        left = sum_dots(refs[:4], refs[4:8]) + got[:, :512]
        right = sum_dots(refs[8:12], refs[12:16])
        top = right[:128] + got[:, 512:768]
        low = right[128:] + got[:, 768:]
        for k, out in enumerate(outs):

            @pl.when(j == k)
            def _():
                out[:, :512] = left.astype(out.dtype)
                out[:, 512:768] = top.astype(out.dtype)
                out[:, 768:] = low.astype(out.dtype)

    return stepped(
        body,
        4,
        table,
        operands + [received],
        specs + [block((128, D), lambda j, t: (quarter(j, t), 0))],
        [shape((128, D), bf16)] * 3 + [shape((128, D), f32)],
        [fixed((128, D))] * 4,
        cost(5),
    )


def attention_sent(table, normeds, mixtures, grads, sums):
    specs, operands = [], []
    for pieces in (normeds, mixtures):
        more, arrays = piece_specs(pieces, 512, lambda j, t: 1 - t[G])
        specs += more
        operands += arrays
    more, arrays = piece_specs(grads, 512, lambda j, t: 0)

    def body(t, *refs):
        sums_ref, out_ref = refs[12:]
        out_ref[:512, :384] = sum_dots(refs[:4], refs[8:12], slice(0, 384)).astype(bf16)
        out_ref[:512, 384:] = sum_dots(refs[4:8], refs[8:12], slice(384, 512)).astype(bf16)
        out_ref[512:, :] = sums_ref[...].astype(bf16)

    return stepped(
        body,
        1,
        table,
        operands + arrays + [sums],
        specs + more + [block((EXTRA, 512), lambda j, t: (1 - t[G], 0))],
        shape((512 + EXTRA, 512), bf16),
        fixed((512 + EXTRA, 512)),
        cost(3.3),
    )


def attention_total(table, normeds, mixtures, grads, received, sums):
    specs, operands = [], []
    for pieces in (normeds, mixtures):
        more, arrays = piece_specs(pieces, 256, lambda j, t: t[G] * 2 + half_rows(j, t))
        specs += more
        operands += arrays
    more, arrays = piece_specs(grads, 512, lambda j, t: 0)

    def body(t, *refs):
        received_ref, tail_ref, sums_ref, sent_ref, kept_ref, total_ref = refs[12:]
        j = pl.program_id(0)
        got = received_ref[...].astype(f32)
        left = sum_dots(refs[:4], refs[8:12], slice(0, 384)) + got[:, :384]
        right = sum_dots(refs[4:8], refs[8:12], slice(384, 512)) + got[:, 384:]

        @pl.when(j == 0)
        def _():
            sent_ref[:256, :384] = left.astype(bf16)
            sent_ref[:256, 384:] = right.astype(bf16)
            total = sums_ref[...] + tail_ref[...].astype(f32)
            total_ref[...] = total
            sent_ref[256:, :] = total.astype(bf16)

        @pl.when(j == 1)
        def _():
            kept_ref[:, :384] = left
            kept_ref[:, 384:] = right

    return stepped(
        body,
        2,
        table,
        operands + arrays + [received, received, sums],
        specs
        + more
        + [
            block((256, 512), lambda j, t: (half_rows(j, t), 0)),
            fixed((EXTRA, 512), 512 // EXTRA),
            block((EXTRA, 512), lambda j, t: (t[G], 0)),
        ],
        [shape((256 + EXTRA, 512), bf16), shape((256, 512), f32), shape((EXTRA, 512), f32)],
        [fixed((256 + EXTRA, 512)), fixed((256, 512)), fixed((EXTRA, 512))],
        cost(3.9),
    )


def add_up(table, kept, received):
    def body(t, kept_ref, *refs):
        total = kept_ref[...].astype(f32)
        for ref in refs[:-1]:
            total += ref[...].astype(f32)
        refs[-1][...] = total.astype(bf16)

    operands = [kept, *received]
    return stepped(
        body, 1, table, operands, [fixed(a.shape) for a in operands], shape(kept.shape, bf16), fixed(kept.shape),
        cost(0.7),
        near=True,
    )


def place_quarters(table, mine, others):
    width = mine.shape[1]
    extra = mine.shape[0] - 128

    def body(t, *refs):
        out = refs[-1]
        for j, ref in enumerate(refs[:-1]):
            out[span(quarter(j, t) * 128, 128), :] = ref[:128, :]
        if extra:
            out[512:, :] = refs[3][128:, :]

    operands = [*others, mine]
    return stepped(
        body, 1, table, operands, [fixed(a.shape) for a in operands], shape((512 + extra, width), bf16),
        fixed((512 + extra, width)), cost(0.7),
        near=True,
    )


def add_split(table, kept, received, sums):
    rows, width = kept.shape
    half, extra = rows // 2, received.shape[0] - rows

    def body(t, kept_ref, received_ref, *refs):
        sent_ref, left_ref = refs[-3:-1] if extra else refs
        for bit, out in ((1 - t[VZ], sent_ref), (t[VZ], left_ref)):
            lines = span(bit * half, half)
            total = kept_ref[lines, :] + received_ref[lines, :].astype(f32)
            out[:half, :] = total.astype(out.dtype)
        if extra:
            total = refs[0][...] + received_ref[rows:, :].astype(f32)
            refs[-1][...] = total
            sent_ref[half:, :] = total.astype(bf16)

    outputs = [shape((half + extra, width), bf16), shape((half, width), f32)]
    if extra:
        outputs.append(shape((extra, width), f32))
    operands = [kept, received] + ([sums] if extra else [])
    return stepped(
        body, 1, table, operands, [fixed(a.shape) for a in operands], outputs, [fixed(o.shape) for o in outputs],
        cost(0.7),
        near=True,
    )


def add_low(table, kept, received, sums):
    rows, width = kept.shape
    extra = received.shape[0] - rows

    def body(t, kept_ref, received_ref, *refs):
        out = refs[-1]
        out[:rows, :] = (kept_ref[...] + received_ref[:rows, :].astype(f32)).astype(bf16)
        if extra:
            out[rows:, :] = (refs[0][...] + received_ref[rows:, :].astype(f32)).astype(bf16)

    operands = [kept, received] + ([sums] if extra else [])
    return stepped(
        body, 1, table, operands, [fixed(a.shape) for a in operands], shape(received.shape, bf16),
        fixed(received.shape), cost(0.6),
        near=True,
    )


def add_far(table, low, received, extra):
    rows, width = low.shape[0] - extra, low.shape[1]

    def body(t, low_ref, received_ref, *outs):
        total = low_ref[...].astype(f32) + received_ref[...].astype(f32)
        outs[0][...] = total[:rows].astype(bf16)
        if extra:
            outs[1][...] = total[rows:].astype(bf16)

    outputs = [shape((rows, width), bf16)] + ([shape((extra, width), bf16)] if extra else [])
    return stepped(
        body, 1, table, (low, received), [fixed(low.shape)] * 2, outputs, [fixed(o.shape) for o in outputs],
        cost(0.6),
        near=True,
    )


def place(table, bit, mine, other, sums=None):
    rows, width = mine.shape
    extra = 0 if sums is None else EXTRA

    def body(t, mine_ref, other_ref, *refs):
        out = refs[-1]
        out[span(t[bit] * rows, rows), :] = mine_ref[...]
        out[span((1 - t[bit]) * rows, rows), :] = other_ref[...]
        if extra:
            out[2 * rows :, :] = refs[0][...]

    operands = [mine, other] + ([sums] if extra else [])
    return stepped(
        body, 1, table, operands, [fixed(a.shape) for a in operands], shape((2 * rows + extra, width), bf16),
        fixed((2 * rows + extra, width)), cost(0.6),
        near=True,
    )


def targets(t):
    found = []
    for k in range(8):
        core = t[C] if k < 4 else 1 - t[C]
        ux, uz = (t[UX], t[UZ]) if k < 4 else (t[VX], t[VZ])
        found.append((core, ((k // 2 % 2) ^ ux) * 2 + ((k % 2) ^ uz)))
    return found


def unpack_feed(table, arrays):
    def body(t, *refs):
        fc_ref, proj_ref = refs[8:]
        rows = span(pl.program_id(0) * 128, 128)
        for ref, (core, number) in zip(refs, targets(t)):
            fc_ref[:, span((number // 2) * 2048 + core * 1024 + (number % 2) * 512, 512)] = ref[rows, :512].astype(f32)
            proj_ref[core * 4 + number, :128, :] = ref[rows, 512:768].astype(f32)
            proj_ref[core * 4 + number, 128:, :] = ref[rows, 768:].astype(f32)

    fc_grad, proj_grad = stepped(
        body,
        4,
        table,
        arrays,
        [pl.BlockSpec(memory_space=pltpu.VMEM)] * 8,
        [shape((512, 4096), f32), shape((8, 256, D), f32)],
        [block((128, 4096), lambda j, t: (j, 0)), pl.BlockSpec((8, 256, 256), lambda j, t: (0, 0, j))],
        cost(7),
        near=True,
    )
    return fc_grad, proj_grad.reshape(2048, D)


def unpack_attention(table, arrays):
    def body(t, *refs):
        arrays, qkv_ref, out_ref, vectors = refs[:8], refs[8], refs[9], refs[10:]
        rows = span(pl.program_id(0) * 128, 128)
        for ref, (core, number) in zip(arrays, targets(t)):
            qkv_ref[:, span((core * 4 + number) * 384, 384)] = ref[rows, :384].astype(f32)
            out_ref[:, span((core * 4 + number) * 128, 128)] = ref[rows, 384:].astype(f32)

        @pl.when(pl.program_id(0) == 0)
        def _():
            sums = arrays[0][512:, :].astype(f32)
            for ref in arrays[1:]:
                sums += ref[512:, :].astype(f32)
            for k in range(8):
                vectors[k][...] = sums[k : k + 1, :].reshape(512)
            for k in range(4):
                vectors[8][pl.ds(512 * k, 512)] = sums[8 + k : 9 + k, :].reshape(512)

    vector = pl.BlockSpec((512,), lambda j, t: (0,))
    return stepped(
        body,
        4,
        table,
        arrays,
        [pl.BlockSpec(memory_space=pltpu.VMEM)] * 8,
        [shape((512, 3 * D), f32), shape((512, D), f32)] + [shape((512,), f32)] * 8 + [shape((2048,), f32)],
        [block((128, 3 * D), lambda j, t: (j, 0)), block((128, D), lambda j, t: (j, 0))]
        + [vector] * 8
        + [pl.BlockSpec((2048,), lambda j, t: (0,))],
        cost(6),
        near=True,
    )


def cut(array, start, size, axis):
    return lax.dynamic_slice_in_dim(array, start, size, axis)


def both(upper, lower):
    return jnp.concatenate([upper, lower], 0)


def zero(t):
    return 0


ROUND = ("z", "x", "xz")
DEALT = ("xz", "x", "z")


def send_quarters(quarters):
    return [swap(array, SECOND[name]) for array, name in zip(quarters, DEALT)]


def send_round(array):
    return [swap(array, FIRST[name]) for name in ROUND]


def share(array):
    across = swap(array, FIRST["xz"])
    return [swap(array, FIRST["x"]), swap(array, FIRST["z"]), across]


def arrays_of(found):
    return [piece[0] for piece in found]


def send_dealt(dealt):
    across, over_x, over_z, own = dealt
    across = swap(across, FIRST["xz"])
    over_x = swap(over_x, FIRST["x"])
    over_z = swap(over_z, FIRST["z"])
    return [(array, 0, 0) for array in (own, over_x, over_z, across)]


def shards(
    block_input,
    segment_ids,
    ln1_gain,
    ln1_bias,
    w_qkv,
    b_query,
    b_value,
    w_out,
    b_out,
    ln2_gain,
    ln2_bias,
    w_fc,
    b_fc,
    w_proj,
    b_proj,
    cotangent,
):
    MADE.clear()
    device = lax.axis_index("group") * 64 + lax.axis_index("replica")
    table = lax.dynamic_slice(jnp.asarray(numbers()), (device, 0), (1, NUMBERS)).reshape(NUMBERS)
    c = table[C]

    first, fc_part = pack(
        table, block_input, w_out, w_fc,
        (ln1_gain, ln1_bias, b_query, b_value, b_out, ln2_gain, ln2_bias, b_proj, b_fc),
    )
    early = jnp.concatenate([cotangent, block_input], 1)
    early = both(early, swap(early, CORE))
    earlies = [early, *share(early)]
    out_near = swap(first, FIRST["g"])
    fc_near = swap(after(fc_part, first), FIRST["g"])
    proj_parts = [cut(after(w_proj, first), c * 1024 + 512 * k, 512, 0) for k in range(2)]
    qkv_part = cut(after(w_qkv, first), c * 256, 256, 0)
    part_mine, part_theirs = project(
        after(table, early, proj_parts, qkv_part), first, out_near, ln1_gain, ln1_bias, w_qkv
    )
    part_theirs = swap(part_theirs, FIRST["g"])
    out_far = swap(after(out_near, part_mine), CORE)
    full, fc_bias = spread(after(table, part_mine, out_far, fc_near), first, out_near)
    fc_z = swap(after(fc_near, part_mine), FIRST["z"])
    fc_pair = both(fc_near, fc_z)
    fc_x = swap(fc_pair, FIRST["x"])
    fc_quarters = [fc_near, fc_z, fc_x, fc_x]

    projected, mixture = mix(after(table, fc_pair), part_mine, part_theirs, full, segment_ids)
    proj_first = swap(after(proj_parts[0], part_theirs), FIRST["g"])
    side, residual = settle(after(table, earlies, fc_x, proj_first), mixture, block_input, full, w_out, out_near, out_far)
    proj_second = swap(after(proj_parts[1], part_theirs), FIRST["g"])
    side = both(after(side, proj_second), swap(side, CORE))
    sides = [side, *share(side)]
    qkv_near = swap(after(qkv_part, proj_first), FIRST["g"])

    hidden, grad_pre, fc_sums, back_mine, back_theirs, output_mine, output_theirs, normed_ones = feed_forward(
        table, side, earlies, w_fc, fc_quarters, fc_bias, w_proj, (proj_first, proj_second), full
    )
    back_theirs = swap(back_theirs, CORE)
    feed_dealt = deal_feed(after(table, sides, qkv_near), hidden, grad_pre)
    feeds = send_dealt(feed_dealt)

    grad_residual, dealt, sums = attend_back(
        after(table, feed_dealt), back_mine, back_theirs, residual, cotangent, full,
        projected, segment_ids, w_out, out_near, out_far,
    )
    result = (residual + (output_mine + swap(output_theirs, CORE) + full[7:8])).astype(bf16)
    dealt_theirs = swap(lax.dynamic_index_in_dim(dealt, 1 - c, 0, False), CORE)
    attention_dealt = deal_attention(after(table, arrays_of(feeds)), dealt, dealt_theirs)
    attention_grads = send_dealt(attention_dealt)
    qkv_far = swap(after(qkv_near, attention_dealt), CORE)
    feed_pieces = [
        [(array, 0, 0) for array in sides],
        feeds,
        feeds,
        [(array, 0, 0) for array in earlies],
    ]
    feed_out = feed_sent(after(table, attention_dealt), *feed_pieces)
    feed_received = swap(feed_out, FIRST["g"])
    input_grad, sums = input_back(
        after(table, feed_out), dealt, w_qkv, qkv_near, qkv_far, block_input, grad_residual, full, sums, fc_sums
    )

    normed_pieces = [(normed_ones, row, 0) for row in range(4)]
    out = attention_sent(
        after(table, sums), normed_pieces, [(array, 0, 2) for array in sides], attention_grads, sums
    )
    received = swap(out, FIRST["g"])
    *feed, feed_kept = feed_total(after(table, out), *feed_pieces, feed_received)
    feed = send_quarters(feed)
    sent, kept, sums = attention_total(
        after(table, feed_kept), normed_pieces, [(array, 0, 4) for array in sides], attention_grads, received, sums
    )
    received = swap(sent, SECOND["x"])
    feed = add_up(after(table, kept), feed_kept, feed)
    feed_far = swap(feed, FAR)
    sent, kept, sums = add_split(after(table, feed), kept, received, sums)
    received = swap(sent, SECOND["z"])
    feed = add_up(after(table, kept), feed, [feed_far])
    feed_others = [swap(feed, SECOND[name]) for name in DEALT]
    low = add_low(after(table, feed), kept, received, sums)
    far = swap(low, FAR)
    feed = place_quarters(after(table, low), feed, feed_others)
    feed_z = swap(feed, FIRST["z"])
    feed_x = swap(feed, FIRST["x"])
    low, sums = add_far(after(table, feed), low, far, EXTRA)
    low = place(table, VZ, low, swap(low, SECOND["z"]))
    other = swap(low, SECOND["x"])
    feed_xz = swap(after(feed_z, low), FIRST["x"])
    attention = place(table, VX, low, other, sums)
    attentions = [attention, *send_round(attention)]
    feeds = [feed, feed_z, feed_x, feed_xz]
    feeds += [swap(after(array, attention), CORE) for array in feeds]
    fc_grad, proj_grad = unpack_feed(after(table, attention), feeds)
    attentions = attentions + [swap(array, CORE) for array in attentions]
    qkv_grad, out_grad, *vectors = unpack_attention(after(table, fc_grad), attentions)
    return (
        result,
        input_grad,
        vectors[0],
        vectors[1],
        qkv_grad,
        vectors[2],
        vectors[3],
        out_grad,
        vectors[4],
        vectors[5],
        vectors[6],
        fc_grad,
        vectors[8],
        proj_grad,
        vectors[7],
    )


def solution(mesh):
    rows = P(("group", "replica"), None)
    vector = P("group")
    matrix = P("group", None)
    vectors_in = (vector, vector, matrix, vector, vector, matrix, vector, vector, vector, matrix, vector, matrix, vector)
    return jax.shard_map(
        shards,
        mesh=mesh,
        in_specs=(rows, rows) + vectors_in + (rows,),
        out_specs=(rows, rows) + vectors_in,
        check_vma=False,
    )
```

```python
import math

import jax
import jax.numpy as jnp
import numpy as np
from jax import lax
from jax.experimental import pallas as pl
from jax.experimental.pallas import tpu as pltpu
from jax.sharding import PartitionSpec as P

D = 1024
HEADS = 16
BATCH = 8
HEAD_DIM = 64
ROWS = 128
BOTH = 2 * ROWS
EXTRA = 16

norm_epsilon = 1e-05
masked_score = -1e30
gelu_factor = 0.7978845608028654
score_scale = 1.0 / math.sqrt(HEAD_DIM)

f32 = jnp.float32
bf16 = jnp.bfloat16
AXES = ("group", "replica")
MIB = 2**20


def flat(g, yh, x, z, c):
    return (((g * 2 + yh) * 4 + x) * 4 + z) * 2 + c


def at(y, x, z, c):
    return flat(y % 2, y // 2, x, z, c)


def everywhere():
    return [(g, yh, x, z, c) for g in range(2) for yh in range(2) for x in range(4) for z in range(4) for c in range(2)]


def exchange(move):
    return [(flat(g, yh, x, z, c), move(2 * yh + g, x, z, c)) for g, yh, x, z, c in everywhere()]


FIRST = {
    "g": exchange(lambda y, x, z, c: at(y ^ (1, 3)[c], x, z, c)),
    "x": exchange(lambda y, x, z, c: at(y, x ^ (1, 3)[c], z, c)),
    "z": exchange(lambda y, x, z, c: at(y, x, z ^ (1, 3)[c], c)),
    "xz": exchange(lambda y, x, z, c: at(y, x ^ (1, 3)[c], z ^ (1, 3)[c], c)),
}
SECOND = {
    "x": exchange(lambda y, x, z, c: at(y, x ^ (3, 1)[c], z, c)),
    "z": exchange(lambda y, x, z, c: at(y, x, z ^ (3, 1)[c], c)),
    "xz": exchange(lambda y, x, z, c: at(y, x ^ (3, 1)[c], z ^ (3, 1)[c], c)),
}
FAR = exchange(lambda y, x, z, c: at(y ^ 2, x, z, c))
CORE = exchange(lambda y, x, z, c: at(y, x, z, c ^ 1))


def swap(array, pairs):
    return lax.ppermute(array, AXES, pairs)


def after(value, *others):
    return lax.optimization_barrier((value, others))[0]


G, C, UX, UZ, VX, VZ = range(6)
PIECE = 6
QUARTER = 9
NUMBERS = 16


def numbers():
    rows = []
    for g, yh, x, z, c in everywhere():
        xs = ((x % 2) ^ (x // 2), x // 2)
        zs = ((z % 2) ^ (z // 2), z // 2)
        ux, vx, uz, vz = xs[c], xs[1 - c], zs[c], zs[1 - c]
        base = (1 - g) * 512
        row = [g, c, ux, uz, vx, vz, g * 512, base + c * 256, base + (1 - c) * 256]
        row += [base + ((ux ^ rx) * 2 + (uz ^ rz)) * 128 for rx in range(2) for rz in range(2)]
        rows.append(row + [0] * (NUMBERS - len(row)))
    return np.array(rows, np.int32)


def cost(us):
    return pl.CostEstimate(flops=0, bytes_accessed=int(us * 3.69e6), transcendentals=0)


def shape(dims, dtype):
    return jax.ShapeDtypeStruct(dims, dtype)


def dot(left, right):
    return jnp.dot(left, right, preferred_element_type=f32)


def rows_dot(left, right):
    return lax.dot_general(left, right, (((0,), (0,)), ((), ())), preferred_element_type=f32)


def dot_rows(left, right):
    return lax.dot_general(left, right, (((1,), (1,)), ((), ())), preferred_element_type=f32)


def span(start, size):
    return pl.ds(pl.multiple_of(start, size), size)


def norm_parts(values):
    center = jnp.mean(values, axis=-1, keepdims=True)
    centered = values - center
    variance = jnp.mean(centered * centered, axis=-1, keepdims=True)
    scale = lax.rsqrt(variance + norm_epsilon)
    return centered * scale, scale


def norm_back(normal, scale, grad):
    return scale * (
        grad
        - jnp.mean(grad, axis=-1, keepdims=True)
        - normal * jnp.mean(grad * normal, axis=-1, keepdims=True)
    )


def over(values):
    return jnp.sum(values, axis=0, keepdims=True)


MADE = []


def stepped(body, steps, table, operands, in_specs, outputs, out_specs, estimate, scratch=(), limit=32, near=False):
    operands = [
        pltpu.with_memory_space_constraint(array, pltpu.HBM)
        if not near and array.size >= 32768 and not any(array is made for made in MADE)
        else array
        for array in operands
    ]
    results = pl.pallas_call(
        body,
        grid_spec=pltpu.PrefetchScalarGridSpec(
            num_scalar_prefetch=1,
            grid=(steps,),
            in_specs=in_specs,
            out_specs=out_specs,
            scratch_shapes=list(scratch),
        ),
        out_shape=outputs,
        compiler_params=pltpu.CompilerParams(vmem_limit_bytes=limit * MIB),
        cost_estimate=estimate,
    )(table, *operands)
    MADE.extend(jax.tree.leaves(results))
    return results


def block(dims, place):
    return pl.BlockSpec(dims, place)


def fixed(dims, row=0, column=0):
    place = (row, column) if len(dims) == 2 else (0,) * len(dims)
    return pl.BlockSpec(dims, lambda j, t: place)


FIRST_ROWS = 256 + ROWS + EXTRA


def pack(table, inputs, w_out, w_fc, vectors):
    def body(t, in_ref, out_ref, low_ref, high_ref, *refs):
        first, fc_part = refs[9:]
        first[:256, :] = out_ref[...]
        first[256:384, :] = in_ref[...]
        first[384:, :] = jnp.zeros((EXTRA, D), bf16)
        for k in range(8):
            first[384 + k // 2 : 385 + k // 2, 512 * (k % 2) : 512 * (k % 2) + 512] = refs[k][...].reshape(1, 512)
        for k in range(2):
            first[388 + k : 389 + k, :] = refs[8][pl.ds(1024 * k, 1024)].reshape(1, 1024)
        fc_part[:, :1024] = low_ref[...]
        fc_part[:, 1024:] = high_ref[...]

    outputs = [shape((FIRST_ROWS, D), bf16), shape((128, 2048), bf16)]
    return stepped(
        body,
        1,
        table,
        (inputs, w_out, w_fc, w_fc, *vectors),
        [
            fixed((ROWS, D)),
            block((256, D), lambda j, t: (t[C], 0)),
            block((128, 1024), lambda j, t: (t[UX] * 2 + t[UZ], t[C])),
            block((128, 1024), lambda j, t: (t[UX] * 2 + t[UZ], 2 + t[C])),
        ]
        + [pl.BlockSpec(v.shape, lambda j, t: (0,)) for v in vectors],
        outputs,
        [fixed(o.shape) for o in outputs],
        cost(3.6),
        limit=60,
    )


def spread(table, own, other):
    def body(t, own_ref, other_ref, full_ref, bias_ref):
        first = t[G] == 0
        mine = own_ref[...].astype(f32)[:8]
        theirs = other_ref[...].astype(f32)[:8]
        low = jnp.where(first, mine, theirs)
        high = jnp.where(first, theirs, mine)
        for k in range(8):
            half = slice(512 * (k % 2), 512 * (k % 2) + 512)
            full_ref[k : k + 1, :512] = low[k // 2 : k // 2 + 1, half]
            full_ref[k : k + 1, 512:] = high[k // 2 : k // 2 + 1, half]
        second = t[C] == 1
        bias_ref[:, :1024] = jnp.where(second, low[5:6], low[4:5])
        bias_ref[:, 1024:] = jnp.where(second, high[5:6], high[4:5])

    tail = fixed((EXTRA, D), 384 // EXTRA)
    return stepped(
        body,
        1,
        table,
        (own, other),
        [tail, tail],
        [shape((8, D), f32), shape((1, 2048), f32)],
        [fixed((8, D)), fixed((1, 2048))],
        cost(1),
    )


def project(table, own, other, gain, shift, w_qkv):
    width = 512

    def body(t, own_ref, other_ref, gain_ref, shift_ref, w_ref, mine_ref, theirs_ref, normed_ref):
        @pl.when(pl.program_id(0) == 0)
        def _():
            half = span(t[PIECE], 512)
            scale = gain_ref[...].astype(f32).reshape(1, 512)
            offset = shift_ref[...].astype(f32).reshape(1, 512)
            for k, ref in enumerate((own_ref, other_ref)):
                values = ref[...].astype(f32)
                center = jnp.mean(values, axis=-1, keepdims=True)
                centered = values - center
                variance = jnp.mean(centered * centered, axis=-1, keepdims=True)
                part = (ref[:, half].astype(f32) - center) * lax.rsqrt(variance + norm_epsilon)
                normed_ref[k * ROWS : (k + 1) * ROWS, :] = (part * scale + offset).astype(bf16)

        total = dot(normed_ref[...], w_ref[...])
        mine_ref[...] = total[:ROWS]
        theirs_ref[...] = total[ROWS:].astype(bf16)

    step = lambda j, t: (0, j)
    vector = pl.BlockSpec((512,), lambda j, t: (0,))
    return stepped(
        body,
        6,
        table,
        (own, other, gain, shift, w_qkv),
        [fixed((ROWS, D), 2), fixed((ROWS, D), 2), vector, vector, block((512, width), step)],
        [shape((ROWS, 3 * D), f32), shape((ROWS, 3 * D), bf16)],
        [block((ROWS, width), step), block((ROWS, width), step)],
        cost(8),
        [pltpu.VMEM((BOTH, 512), bf16)],
    )


def admitted(segments_ref):
    across = jnp.broadcast_to(segments_ref[...], (ROWS, ROWS))
    down = across.T
    row = lax.broadcasted_iota(jnp.int32, (ROWS, ROWS), 0)
    column = lax.broadcasted_iota(jnp.int32, (ROWS, ROWS), 1)
    return (row >= column) & (across == down)


def cut_heads(ref, first, heads):
    return [ref[:, first + head * HEAD_DIM : first + (head + 1) * HEAD_DIM] for head in heads]


def head_probs(projected_ref, heads, allowed):
    queries, keys, values = (cut_heads(projected_ref, k * D, heads) for k in range(3))
    scores = [jnp.where(allowed, dot_rows(q, k) * score_scale, masked_score) for q, k in zip(queries, keys)]
    weights = [jnp.exp(x - jnp.max(x, axis=-1, keepdims=True)) for x in scores]
    return queries, keys, values, [x / jnp.sum(x, axis=-1, keepdims=True) for x in weights]


def mix(table, mine, theirs, full, segments):
    def body(t, mine_ref, theirs_ref, full_ref, seg_ref, p_ref, mixture_ref):
        for k, row in ((0, 2), (1, None), (2, 3)):
            columns = slice(k * D, (k + 1) * D)
            total = mine_ref[:, columns] + theirs_ref[:, columns].astype(f32)
            if row is not None:
                total += full_ref[row : row + 1, :]
            p_ref[:, columns] = total.astype(bf16)
        allowed = admitted(seg_ref)
        _, _, values, probs = head_probs(p_ref, range(HEADS), allowed)
        outputs = [dot(p.astype(bf16), v).astype(bf16) for p, v in zip(probs, values)]
        for head, output in enumerate(outputs):
            mixture_ref[:, head * HEAD_DIM : (head + 1) * HEAD_DIM] = output

    return stepped(
        body,
        1,
        table,
        (mine, theirs, full, segments),
        [fixed((ROWS, 3 * D)), fixed((ROWS, 3 * D)), fixed((8, D)), fixed((1, ROWS))],
        [shape((ROWS, 3 * D), bf16), shape((ROWS, D), bf16)],
        [fixed((ROWS, 3 * D)), fixed((ROWS, D))],
        cost(8.1),
    )


def settle(table, mixture, inputs, full, w_out, near, far):
    def body(t, mixture_ref, in_ref, full_ref, own, a, b, side_ref, residual_ref):
        total = dot(mixture_ref[:, span(t[PIECE], 512)], own[...])
        for k, ref in enumerate((a, b)):
            total += dot(mixture_ref[:, span(t[PIECE + 1 + k], 256)], ref[...])
        residual = in_ref[...].astype(f32) + (total + full_ref[4:5, :])
        residual_ref[...] = residual
        normal, _ = norm_parts(residual)
        side_ref[:, :D] = (normal * full_ref[5:6, :] + full_ref[6:7, :]).astype(bf16)
        side_ref[:, D:] = mixture_ref[...]

    return stepped(
        body,
        1,
        table,
        (mixture, inputs, full, w_out, near, far),
        [fixed((ROWS, D)), fixed((ROWS, D)), fixed((8, D)), fixed((512, D)), fixed((256, D)), fixed((256, D))],
        [shape((ROWS, 2 * D), bf16), shape((ROWS, D), f32)],
        [fixed((ROWS, 2 * D)), fixed((ROWS, D))],
        cost(3),
    )


def feed_forward(table, side, early, w_fc, fc_others, bias, w_proj, proj_others):
    def body(t, side_ref, cot_ref, bias_ref, w_fc, near_fc, z_fc, x_fc, w_proj, first_proj, second_proj, *refs):
        hidden_ref, grad_ref, sums_ref, back_mine, back_theirs, out_mine, out_theirs = refs[:7]
        fc_own, fc_rest, proj_own, proj_rest, rest_ref, slope_ref, sems = refs[7:]
        low, high = span(t[C] * 1024, 1024), span(2048 + t[C] * 1024, 1024)
        copies = [
            (w_fc.at[:, low], fc_own.at[:, :1024]),
            (w_fc.at[:, high], fc_own.at[:, 1024:]),
            (near_fc, fc_rest.at[:128]),
            (z_fc, fc_rest.at[128:256]),
            (x_fc, fc_rest.at[256:]),
            (w_proj.at[low], proj_own),
            (first_proj, proj_rest.at[:512]),
            (second_proj, proj_rest.at[512:]),
        ]
        copies = [pltpu.make_async_copy(src, dst, sems.at[k]) for k, (src, dst) in enumerate(copies)]
        for copy in copies:
            copy.start()
        for i in range(4):
            rest_ref[:, 128 * i : 128 * (i + 1)] = side_ref[:, span(t[QUARTER + i], 128)]
        own = side_ref[:, span(t[PIECE], 512)]
        for copy in copies[:5]:
            copy.wait()
        for n in range(4):
            here = slice(512 * n, 512 * (n + 1))
            values = dot(own, fc_own[:, here]) + dot(rest_ref[...], fc_rest[:, here]) + bias_ref[:, here]
            square = values * values
            inner = jnp.tanh(gelu_factor * values * (1.0 + 0.044715 * square))
            outer = 0.5 * (1.0 + inner)
            hidden_ref[:, here] = (values * outer).astype(bf16)
            slope_ref[:, here] = outer + values * outer * (1.0 - inner) * gelu_factor * (1.0 + 3.0 * 0.044715 * square)
        for copy in copies[5:]:
            copy.wait()
        for group, weights in ((t[G], proj_own), (1 - t[G], proj_rest)):
            for n in range(2):
                columns = span(group * 1024 + n * 512, 512)
                grad = (dot_rows(cot_ref[...], weights[512 * n : 512 * (n + 1), :]) * slope_ref[:, columns]).astype(bf16)
                grad_ref[:, columns] = grad
                sums_ref[:, columns] = over(grad.astype(f32))
        total = dot_rows(grad_ref[...], fc_own[...])
        back_mine[:, span(t[PIECE], 512)] = total[:ROWS]
        back_theirs[:, span(t[PIECE], 512)] = total[ROWS:]
        total = dot_rows(grad_ref[...], fc_rest[...])
        for i in range(4):
            back_mine[:, span(t[QUARTER + i], 128)] = total[:ROWS, 128 * i : 128 * (i + 1)]
            back_theirs[:, span(t[QUARTER + i], 128)] = total[ROWS:, 128 * i : 128 * (i + 1)]
        for n in range(2):
            here = slice(512 * n, 512 * (n + 1))
            total = dot(hidden_ref[:, span(t[G] * 1024, 1024)], proj_own[:, here])
            total += dot(hidden_ref[:, span((1 - t[G]) * 1024, 1024)], proj_rest[:, here])
            out_mine[:, here] = total[:ROWS]
            out_theirs[:, here] = total[ROWS:]

    anywhere = pl.BlockSpec(memory_space=pl.ANY)
    square = fixed((ROWS, D))
    return stepped(
        body,
        1,
        table,
        (side, early, bias, w_fc, *fc_others, w_proj, *proj_others),
        [fixed((BOTH, D)), fixed((BOTH, D)), fixed((1, 2048))] + [anywhere] * 7,
        [shape((BOTH, 2048), bf16), shape((BOTH, 2048), bf16), shape((1, 2048), f32)] + [shape((ROWS, D), f32)] * 4,
        [fixed((BOTH, 2048)), fixed((BOTH, 2048)), fixed((1, 2048)), square, square, square, square],
        cost(12),
        [pltpu.VMEM((512, 2048), bf16)] * 2
        + [pltpu.VMEM((1024, D), bf16)] * 2
        + [pltpu.VMEM((BOTH, 512), bf16), pltpu.VMEM((BOTH, 2048), f32), pltpu.SemaphoreType.DMA((8,))],
        limit=48,
    )


def first_norms(table, pieces, full):
    def body(t, *refs):
        full_ref, normed_ref = refs[4:]
        for i, ref in enumerate(refs[:4]):
            normal, _ = norm_parts(ref[...].astype(f32))
            normed_ref[i * BOTH : (i + 1) * BOTH, :] = (normal * full_ref[0:1, :] + full_ref[1:2, :]).astype(bf16)

    return stepped(
        body, 1, table, (*pieces, full), [fixed((BOTH, D), 0, 1)] * 4 + [fixed((8, D))],
        shape((4 * BOTH, D), bf16), fixed((4 * BOTH, D)), cost(4),
    )


def attend_back(table, mine, theirs, residual, cotangent, full, projected, segments, w_out, near, far):
    def body(
        t, mine_ref, theirs_ref, res_ref, cot_ref, full_ref, p_ref, seg_ref, own, a, b,
        grad_ref, dealt_ref, sums_ref, mix_ref,
    ):
        normal, scale = norm_parts(res_ref[...])
        grad_normed = mine_ref[...] + theirs_ref[...]
        grad_output = cot_ref[...].astype(f32)
        grad = grad_output + norm_back(normal, scale, grad_normed * full_ref[5:6, :])
        grad_ref[...] = grad
        low = grad.astype(bf16)
        for k in range(8):
            dealt_ref[k // 4, :, 512 * (k % 4) + 384 : 512 * (k % 4) + 512] = low[:, 128 * k : 128 * (k + 1)]
        sums_ref[0:1, :] = over(grad)
        sums_ref[1:2, :] = over(grad_normed * normal)
        sums_ref[2:3, :] = over(grad_normed)
        sums_ref[3:4, :] = over(grad_output)
        sums_ref[4:, :] = jnp.zeros((4, D), f32)
        mix_ref[:, span(t[PIECE], 512)] = dot_rows(low, own[...]).astype(bf16)
        for k, ref in enumerate((a, b)):
            mix_ref[:, span(t[PIECE + 1 + k], 256)] = dot_rows(low, ref[...]).astype(bf16)
        allowed = admitted(seg_ref)

        def store(number, values):
            column = 512 * (number % 24 // 6) + HEAD_DIM * (number % 6)
            dealt_ref[number // 24, :, column : column + HEAD_DIM] = values.astype(bf16)

        for first in range(0, HEADS, BATCH):
            heads = range(first, first + BATCH)
            queries, keys, values, probs = head_probs(p_ref, heads, allowed)
            grad_mix = cut_heads(mix_ref, 0, heads)
            grad_probs = [dot_rows(g, v) for g, v in zip(grad_mix, values)]
            centres = [jnp.sum(p * g, axis=-1, keepdims=True) for p, g in zip(probs, grad_probs)]
            grad_scores = [(p * (g - x)).astype(bf16) for p, g, x in zip(probs, grad_probs, centres)]
            found = (
                [dot(g, k) * score_scale for g, k in zip(grad_scores, keys)],
                [rows_dot(g, q) * score_scale for g, q in zip(grad_scores, queries)],
                [rows_dot(p.astype(bf16), g) for p, g in zip(probs, grad_mix)],
            )
            for kind, results in enumerate(found):
                for head, result in zip(heads, results):
                    store(kind * HEADS + head, result)

    square = fixed((ROWS, D))
    return stepped(
        body,
        1,
        table,
        (mine, theirs, residual, cotangent, full, projected, segments, w_out, near, far),
        [square] * 4 + [fixed((8, D)), fixed((ROWS, 3 * D)), fixed((1, ROWS))]
        + [fixed((512, D)), fixed((256, D)), fixed((256, D))],
        [shape((ROWS, D), f32), shape((2, ROWS, 2048), bf16), shape((8, D), f32)],
        [square, fixed((2, ROWS, 2048)), fixed((8, D))],
        cost(11.5),
        [pltpu.VMEM((ROWS, D), bf16)],
    )


def input_back(table, dealt, w_qkv, near, far, inputs, grad_residual, full, sums, fc_sums):
    width = 384

    def body(t, grad_ref, own, a, b, in_ref, res_ref, full_ref, early_ref, fc_ref, out_ref, sums_ref, total_ref, bias_ref):
        j = pl.program_id(0)
        grad = grad_ref[0, :, :width]

        @pl.when(j == 0)
        def _():
            total_ref[...] = jnp.zeros((ROWS, D), f32)

        offset = 0
        for ref in (own, a, b):
            size = ref.shape[0]
            total_ref[:, offset : offset + size] += dot_rows(grad, ref[...])
            offset += size
        bias_ref[:, span(j * width, width)] = over(grad.astype(f32))

        @pl.when(j == 7)
        def _():
            offset = 0
            for k, size in enumerate((512, 256, 256)):
                out_ref[:, span(t[PIECE + k], size)] = total_ref[:, offset : offset + size]
                offset += size
            grad_normed = out_ref[...]
            normal, scale = norm_parts(in_ref[...].astype(f32))
            gain_sums = over(grad_normed * normal)
            shift_sums = over(grad_normed)
            out_ref[...] = res_ref[...] + norm_back(normal, scale, grad_normed * full_ref[0:1, :])
            row = lax.broadcasted_iota(jnp.int32, (4, 512), 0)
            for g in range(2):
                half = slice(512 * g, 512 * (g + 1))
                sums_ref[16 * g : 16 * g + 1, :] = gain_sums[:, half]
                sums_ref[16 * g + 1 : 16 * g + 2, :] = shift_sums[:, half]
                sums_ref[16 * g + 2 : 16 * g + 3, :] = bias_ref[:, 512 * g : 512 * (g + 1)]
                sums_ref[16 * g + 3 : 16 * g + 4, :] = bias_ref[:, 2048 + 512 * g : 2048 + 512 * (g + 1)]
                sums_ref[16 * g + 4 : 16 * g + 8, :] = early_ref[0:4, half]
                units = [fc_ref[:, 1024 * g + 512 * (k % 2) : 1024 * g + 512 * (k % 2) + 512] for k in range(4)]
                sums_ref[16 * g + 8 : 16 * g + 12, :] = jnp.where(row // 2 == t[C], jnp.concatenate(units, 0), 0.0)
                sums_ref[16 * g + 12 : 16 * g + 16, :] = jnp.zeros((4, 512), f32)

    step = lambda j, t: (0, j)
    return stepped(
        body,
        8,
        table,
        (dealt, w_qkv, near, far, inputs, grad_residual, full, sums, fc_sums),
        [pl.BlockSpec((1, ROWS, 512), lambda j, t: (j // 4, 0, j % 4)), block((512, width), step)]
        + [block((256, width), step)] * 2
        + [fixed((ROWS, D)), fixed((ROWS, D)), fixed((8, D)), fixed((8, D)), fixed((1, 2048))],
        [shape((ROWS, D), f32), shape((2 * EXTRA, 512), f32)],
        [fixed((ROWS, D)), fixed((2 * EXTRA, 512))],
        cost(9.2),
        [pltpu.VMEM((ROWS, D), f32), pltpu.VMEM((1, 3 * D), f32)],
    )


def piece_specs(pieces, width, number):
    specs, operands = [], []
    for array, row, column in pieces:
        specs.append(
            pl.BlockSpec(
                (BOTH, width),
                lambda j, t, row=row, column=column: (row(t) if callable(row) else row, column + number(j, t)),
            )
        )
        operands.append(array)
    return specs, operands


def sum_dots(lefts, rights, columns=slice(None)):
    total = rows_dot(lefts[0][...], rights[0][:, columns])
    for left, right in zip(lefts[1:], rights[1:]):
        total += rows_dot(left[...], right[:, columns])
    return total


def deal_feed(table, hidden, grad_pre):
    def body(t, hidden_ref, grad_ref, *outs):
        for j, out in enumerate(outs):
            away = 3 - j
            bx, bz = (away // 2) ^ t[UX], (away % 2) ^ t[UZ]
            for g in range(2):
                out[:, 256 * g : 256 * (g + 1)] = hidden_ref[:, span(g * 1024 + (bx * 2 + bz) * 256, 256)]
            out[:, 512:] = grad_ref[:, span((bx * 2 + bz) * 512, 512)]

    return stepped(
        body, 1, table, (hidden, grad_pre), [fixed((BOTH, 2048))] * 2, [shape((BOTH, D), bf16)] * 4,
        [fixed((BOTH, D))] * 4, cost(0.8), near=True,
    )


def deal_attention(table, mine, theirs, mixtures):
    def body(t, mine_ref, theirs_ref, mix_ref, *outs):
        for j, out in enumerate(outs):
            away = 3 - j
            columns = span((((away // 2) ^ t[UX]) * 2 + ((away % 2) ^ t[UZ])) * 512, 512)
            out[:ROWS, :512] = mine_ref[0, :, columns]
            out[ROWS:, :512] = theirs_ref[:, columns]
            out[:, 512:] = mix_ref[...]

    return stepped(
        body, 1, table, (mine, theirs, mixtures),
        [pl.BlockSpec((1, ROWS, 2048), lambda j, t: (t[C], 0, 0)), fixed((ROWS, 2048)), fixed((BOTH, D))],
        [shape((BOTH, 512 + D), bf16)] * 4, [fixed((BOTH, 512 + D))] * 4, cost(1), near=True,
    )


def quarter(j, t):
    away = 3 - j
    return ((away // 2) ^ t[VX]) * 2 + ((away % 2) ^ t[VZ])


def half_rows(j, t):
    return jnp.where(j == 0, 1 - t[VX], t[VX])


def feed_specs(normeds, grads, hiddens, cotangents, rows, width, features, units, columns):
    specs, operands = [], []
    for pieces, size, number in (
        (normeds, rows, features),
        (grads, 512, lambda j, t: 1),
        (hiddens, 256, units),
        (cotangents, width, columns),
    ):
        more, arrays = piece_specs(pieces, size, number)
        specs += more
        operands += arrays
    return specs, operands


def feed_sent(table, normeds, grads, hiddens, cotangents):
    specs, operands = feed_specs(
        normeds, grads, hiddens, cotangents, 256, 512,
        lambda j, t: (1 - t[G]) * 2 + j, lambda j, t: 1 - t[G], lambda j, t: j,
    )

    def body(t, *refs):
        out = refs[-1]
        out[:, :512] = sum_dots(refs[:4], refs[4:8]).astype(bf16)
        units = sum_dots(refs[8:12], refs[12:16]).astype(bf16)
        for q in range(2):
            rows, columns = slice(128 * q, 128 * (q + 1)), slice(256 * q, 256 * (q + 1))
            out[rows, 512:768] = units[:128, columns]
            out[rows, 768:] = units[128:, columns]

    return stepped(
        body, 2, table, operands, specs, shape((512, D), bf16), block((256, D), lambda j, t: (j, 0)), cost(4.3),
    )


def feed_total(table, normeds, grads, hiddens, cotangents, received):
    specs, operands = feed_specs(
        normeds, grads, hiddens, cotangents, 128, 256,
        lambda j, t: t[G] * 4 + quarter(j, t), lambda j, t: t[G], quarter,
    )

    def body(t, *refs):
        received_ref = refs[16]
        outs = refs[17:]
        j = pl.program_id(0)
        got = received_ref[...].astype(f32)
        left = sum_dots(refs[:4], refs[4:8]) + got[:, :512]
        right = sum_dots(refs[8:12], refs[12:16])
        top = right[:128] + got[:, 512:768]
        low = right[128:] + got[:, 768:]
        for k, out in enumerate(outs):

            @pl.when(j == k)
            def _():
                out[:, :512] = left.astype(out.dtype)
                out[:, 512:768] = top.astype(out.dtype)
                out[:, 768:] = low.astype(out.dtype)

    return stepped(
        body,
        4,
        table,
        operands + [received],
        specs + [block((128, D), lambda j, t: (quarter(j, t), 0))],
        [shape((128, D), bf16)] * 3 + [shape((128, D), f32)],
        [fixed((128, D))] * 4,
        cost(5),
    )


def attention_sent(table, normeds, mixtures, grads, sums):
    specs, operands = [], []
    for pieces in (normeds, mixtures):
        more, arrays = piece_specs(pieces, 512, lambda j, t: 1 - t[G])
        specs += more
        operands += arrays
    more, arrays = piece_specs(grads, 512, lambda j, t: 0)

    def body(t, *refs):
        sums_ref, out_ref = refs[12:]
        out_ref[:512, :384] = sum_dots(refs[:4], refs[8:12], slice(0, 384)).astype(bf16)
        out_ref[:512, 384:] = sum_dots(refs[4:8], refs[8:12], slice(384, 512)).astype(bf16)
        out_ref[512:, :] = sums_ref[...].astype(bf16)

    return stepped(
        body,
        1,
        table,
        operands + arrays + [sums],
        specs + more + [block((EXTRA, 512), lambda j, t: (1 - t[G], 0))],
        shape((512 + EXTRA, 512), bf16),
        fixed((512 + EXTRA, 512)),
        cost(3.3),
    )


def attention_total(table, normeds, mixtures, grads, received, sums):
    specs, operands = [], []
    for pieces in (normeds, mixtures):
        more, arrays = piece_specs(pieces, 256, lambda j, t: t[G] * 2 + half_rows(j, t))
        specs += more
        operands += arrays
    more, arrays = piece_specs(grads, 512, lambda j, t: 0)

    def body(t, *refs):
        received_ref, tail_ref, sums_ref, sent_ref, kept_ref, total_ref = refs[12:]
        j = pl.program_id(0)
        got = received_ref[...].astype(f32)
        left = sum_dots(refs[:4], refs[8:12], slice(0, 384)) + got[:, :384]
        right = sum_dots(refs[4:8], refs[8:12], slice(384, 512)) + got[:, 384:]

        @pl.when(j == 0)
        def _():
            sent_ref[:256, :384] = left.astype(bf16)
            sent_ref[:256, 384:] = right.astype(bf16)
            total = sums_ref[...] + tail_ref[...].astype(f32)
            total_ref[...] = total
            sent_ref[256:, :] = total.astype(bf16)

        @pl.when(j == 1)
        def _():
            kept_ref[:, :384] = left
            kept_ref[:, 384:] = right

    return stepped(
        body,
        2,
        table,
        operands + arrays + [received, received, sums],
        specs
        + more
        + [
            block((256, 512), lambda j, t: (half_rows(j, t), 0)),
            fixed((EXTRA, 512), 512 // EXTRA),
            block((EXTRA, 512), lambda j, t: (t[G], 0)),
        ],
        [shape((256 + EXTRA, 512), bf16), shape((256, 512), f32), shape((EXTRA, 512), f32)],
        [fixed((256 + EXTRA, 512)), fixed((256, 512)), fixed((EXTRA, 512))],
        cost(3.9),
    )


def add_up(table, kept, received):
    def body(t, kept_ref, *refs):
        total = kept_ref[...].astype(f32)
        for ref in refs[:-1]:
            total += ref[...].astype(f32)
        refs[-1][...] = total.astype(bf16)

    operands = [kept, *received]
    return stepped(
        body, 1, table, operands, [fixed(a.shape) for a in operands], shape(kept.shape, bf16), fixed(kept.shape),
        cost(0.7),
        near=True,
    )


def place_quarters(table, mine, others):
    width = mine.shape[1]
    extra = mine.shape[0] - 128

    def body(t, *refs):
        out = refs[-1]
        for j, ref in enumerate(refs[:-1]):
            out[span(quarter(j, t) * 128, 128), :] = ref[:128, :]
        if extra:
            out[512:, :] = refs[3][128:, :]

    operands = [*others, mine]
    return stepped(
        body, 1, table, operands, [fixed(a.shape) for a in operands], shape((512 + extra, width), bf16),
        fixed((512 + extra, width)), cost(0.7),
        near=True,
    )


def add_split(table, kept, received, sums):
    rows, width = kept.shape
    half, extra = rows // 2, received.shape[0] - rows

    def body(t, kept_ref, received_ref, *refs):
        sent_ref, left_ref = refs[-3:-1] if extra else refs
        for bit, out in ((1 - t[VZ], sent_ref), (t[VZ], left_ref)):
            lines = span(bit * half, half)
            total = kept_ref[lines, :] + received_ref[lines, :].astype(f32)
            out[:half, :] = total.astype(out.dtype)
        if extra:
            total = refs[0][...] + received_ref[rows:, :].astype(f32)
            refs[-1][...] = total
            sent_ref[half:, :] = total.astype(bf16)

    outputs = [shape((half + extra, width), bf16), shape((half, width), f32)]
    if extra:
        outputs.append(shape((extra, width), f32))
    operands = [kept, received] + ([sums] if extra else [])
    return stepped(
        body, 1, table, operands, [fixed(a.shape) for a in operands], outputs, [fixed(o.shape) for o in outputs],
        cost(0.7),
        near=True,
    )


def add_low(table, kept, received, sums):
    rows, width = kept.shape
    extra = received.shape[0] - rows

    def body(t, kept_ref, received_ref, *refs):
        out = refs[-1]
        out[:rows, :] = (kept_ref[...] + received_ref[:rows, :].astype(f32)).astype(bf16)
        if extra:
            out[rows:, :] = (refs[0][...] + received_ref[rows:, :].astype(f32)).astype(bf16)

    operands = [kept, received] + ([sums] if extra else [])
    return stepped(
        body, 1, table, operands, [fixed(a.shape) for a in operands], shape(received.shape, bf16),
        fixed(received.shape), cost(0.6),
        near=True,
    )


def add_far(table, low, received, extra):
    rows, width = low.shape[0] - extra, low.shape[1]

    def body(t, low_ref, received_ref, *outs):
        total = low_ref[...].astype(f32) + received_ref[...].astype(f32)
        outs[0][...] = total[:rows].astype(bf16)
        if extra:
            outs[1][...] = total[rows:].astype(bf16)

    outputs = [shape((rows, width), bf16)] + ([shape((extra, width), bf16)] if extra else [])
    return stepped(
        body, 1, table, (low, received), [fixed(low.shape)] * 2, outputs, [fixed(o.shape) for o in outputs],
        cost(0.6),
        near=True,
    )


def place(table, bit, mine, other, sums=None):
    rows, width = mine.shape
    extra = 0 if sums is None else EXTRA

    def body(t, mine_ref, other_ref, *refs):
        out = refs[-1]
        out[span(t[bit] * rows, rows), :] = mine_ref[...]
        out[span((1 - t[bit]) * rows, rows), :] = other_ref[...]
        if extra:
            out[2 * rows :, :] = refs[0][...]

    operands = [mine, other] + ([sums] if extra else [])
    return stepped(
        body, 1, table, operands, [fixed(a.shape) for a in operands], shape((2 * rows + extra, width), bf16),
        fixed((2 * rows + extra, width)), cost(0.6),
        near=True,
    )


def targets(t):
    found = []
    for k in range(8):
        core = t[C] if k < 4 else 1 - t[C]
        ux, uz = (t[UX], t[UZ]) if k < 4 else (t[VX], t[VZ])
        found.append((core, ((k // 2 % 2) ^ ux) * 2 + ((k % 2) ^ uz)))
    return found


def unpack_feed(table, arrays):
    def body(t, *refs):
        fc_ref, proj_ref = refs[8:]
        rows = span(pl.program_id(0) * 128, 128)
        for ref, (core, number) in zip(refs, targets(t)):
            fc_ref[:, span((number // 2) * 2048 + core * 1024 + (number % 2) * 512, 512)] = ref[rows, :512].astype(f32)
            proj_ref[core * 4 + number, :128, :] = ref[rows, 512:768].astype(f32)
            proj_ref[core * 4 + number, 128:, :] = ref[rows, 768:].astype(f32)

    fc_grad, proj_grad = stepped(
        body,
        4,
        table,
        arrays,
        [pl.BlockSpec(memory_space=pltpu.VMEM)] * 8,
        [shape((512, 4096), f32), shape((8, 256, D), f32)],
        [block((128, 4096), lambda j, t: (j, 0)), pl.BlockSpec((8, 256, 256), lambda j, t: (0, 0, j))],
        cost(7),
        near=True,
    )
    return fc_grad, proj_grad.reshape(2048, D)


def unpack_attention(table, arrays):
    def body(t, *refs):
        arrays, qkv_ref, out_ref, vectors = refs[:8], refs[8], refs[9], refs[10:]
        rows = span(pl.program_id(0) * 128, 128)
        for ref, (core, number) in zip(arrays, targets(t)):
            qkv_ref[:, span((core * 4 + number) * 384, 384)] = ref[rows, :384].astype(f32)
            out_ref[:, span((core * 4 + number) * 128, 128)] = ref[rows, 384:].astype(f32)

        @pl.when(pl.program_id(0) == 0)
        def _():
            sums = arrays[0][512:, :].astype(f32)
            for ref in arrays[1:]:
                sums += ref[512:, :].astype(f32)
            for k in range(8):
                vectors[k][...] = sums[k : k + 1, :].reshape(512)
            for k in range(4):
                vectors[8][pl.ds(512 * k, 512)] = sums[8 + k : 9 + k, :].reshape(512)

    vector = pl.BlockSpec((512,), lambda j, t: (0,))
    return stepped(
        body,
        4,
        table,
        arrays,
        [pl.BlockSpec(memory_space=pltpu.VMEM)] * 8,
        [shape((512, 3 * D), f32), shape((512, D), f32)] + [shape((512,), f32)] * 8 + [shape((2048,), f32)],
        [block((128, 3 * D), lambda j, t: (j, 0)), block((128, D), lambda j, t: (j, 0))]
        + [vector] * 8
        + [pl.BlockSpec((2048,), lambda j, t: (0,))],
        cost(6),
        near=True,
    )


def cut(array, start, size, axis):
    return lax.dynamic_slice_in_dim(array, start, size, axis)


def both(upper, lower):
    return jnp.concatenate([upper, lower], 0)


def zero(t):
    return 0


ROUND = ("z", "x", "xz")
DEALT = ("xz", "x", "z")


def send_quarters(quarters):
    return [swap(array, SECOND[name]) for array, name in zip(quarters, DEALT)]


def send_round(array):
    return [swap(array, FIRST[name]) for name in ROUND]


def share(array):
    across = swap(array, FIRST["xz"])
    return [swap(array, FIRST["x"]), swap(array, FIRST["z"]), across]


def arrays_of(found):
    return [piece[0] for piece in found]


def send_dealt(dealt):
    across, over_x, over_z, own = dealt
    across = swap(across, FIRST["xz"])
    over_x = swap(over_x, FIRST["x"])
    over_z = swap(over_z, FIRST["z"])
    return [(array, 0, 0) for array in (own, over_x, over_z, across)]


def shards(
    block_input,
    segment_ids,
    ln1_gain,
    ln1_bias,
    w_qkv,
    b_query,
    b_value,
    w_out,
    b_out,
    ln2_gain,
    ln2_bias,
    w_fc,
    b_fc,
    w_proj,
    b_proj,
    cotangent,
):
    MADE.clear()
    device = lax.axis_index("group") * 64 + lax.axis_index("replica")
    table = lax.dynamic_slice(jnp.asarray(numbers()), (device, 0), (1, NUMBERS)).reshape(NUMBERS)
    c = table[C]

    first, fc_part = pack(
        table, block_input, w_out, w_fc,
        (ln1_gain, ln1_bias, b_query, b_value, b_out, ln2_gain, ln2_bias, b_proj, b_fc),
    )
    early = jnp.concatenate([cotangent, block_input], 1)
    early = both(early, swap(early, CORE))
    earlies = [early, *share(early)]
    out_near = swap(first, FIRST["g"])
    fc_near = swap(after(fc_part, first), FIRST["g"])
    proj_parts = [cut(after(w_proj, first), c * 1024 + 512 * k, 512, 0) for k in range(2)]
    qkv_part = cut(after(w_qkv, first), c * 256, 256, 0)
    part_mine, part_theirs = project(
        after(table, early, proj_parts, qkv_part, fc_near), first, out_near, ln1_gain, ln1_bias, w_qkv
    )
    part_theirs = swap(part_theirs, FIRST["g"])
    out_far = swap(after(out_near, part_mine), CORE)
    full, fc_bias = spread(after(table, part_mine, out_far, fc_near), first, out_near)
    fc_z = swap(after(fc_near, part_mine), FIRST["z"])
    fc_pair = both(fc_near, fc_z)
    fc_x = swap(fc_pair, FIRST["x"])
    fc_others = [fc_near, fc_z, fc_x]

    projected, mixture = mix(after(table, fc_pair), part_mine, part_theirs, full, segment_ids)
    proj_first = swap(after(proj_parts[0], part_theirs), FIRST["g"])
    side, residual = settle(after(table, earlies, fc_x, proj_first), mixture, block_input, full, w_out, out_near, out_far)
    proj_second = swap(after(proj_parts[1], part_theirs), FIRST["g"])
    side_theirs = swap(side, CORE)
    side = after(side, proj_second)
    normed_twos = both(side[:, :D], side_theirs[:, :D])
    mixtures = both(side[:, D:], side_theirs[:, D:])
    sides = [normed_twos, *share(normed_twos)]
    qkv_near = swap(after(qkv_part, proj_first), FIRST["g"])

    hidden, grad_pre, fc_sums, back_mine, back_theirs, output_mine, output_theirs = feed_forward(
        table, normed_twos, early, w_fc, fc_others, fc_bias, w_proj, (proj_first, proj_second)
    )
    back_theirs = swap(back_theirs, CORE)
    feed_dealt = deal_feed(after(table, sides, qkv_near), hidden, grad_pre)
    feeds = send_dealt(feed_dealt)
    normed_ones = first_norms(after(table, feed_dealt), earlies, full)

    grad_residual, dealt, sums = attend_back(
        after(table, normed_ones), back_mine, back_theirs, residual, cotangent, full,
        projected, segment_ids, w_out, out_near, out_far,
    )
    result = (residual + (output_mine + swap(output_theirs, CORE) + full[7:8])).astype(bf16)
    dealt_theirs = swap(lax.dynamic_index_in_dim(dealt, 1 - c, 0, False), CORE)
    attention_dealt = deal_attention(after(table, arrays_of(feeds)), dealt, dealt_theirs, mixtures)
    attention_grads = send_dealt(attention_dealt)
    qkv_far = swap(after(qkv_near, attention_dealt), CORE)
    feed_pieces = [
        [(array, 0, 0) for array in sides],
        feeds,
        feeds,
        [(array, 0, 0) for array in earlies],
    ]
    feed_out = feed_sent(after(table, attention_dealt), *feed_pieces)
    feed_received = swap(feed_out, FIRST["g"])
    input_grad, sums = input_back(
        after(table, feed_out), dealt, w_qkv, qkv_near, qkv_far, block_input, grad_residual, full, sums, fc_sums
    )

    normed_pieces = [(normed_ones, row, 0) for row in range(4)]
    out = attention_sent(
        after(table, sums), normed_pieces, [(array, 0, 1) for array, _, _ in attention_grads], attention_grads, sums
    )
    received = swap(out, FIRST["g"])
    *feed, feed_kept = feed_total(after(table, out), *feed_pieces, feed_received)
    feed = send_quarters(feed)
    sent, kept, sums = attention_total(
        after(table, feed_kept), normed_pieces, [(array, 0, 2) for array, _, _ in attention_grads], attention_grads, received, sums
    )
    received = swap(sent, SECOND["x"])
    feed = add_up(after(table, kept), feed_kept, feed)
    feed_far = swap(feed, FAR)
    sent, kept, sums = add_split(after(table, feed), kept, received, sums)
    received = swap(sent, SECOND["z"])
    feed = add_up(after(table, kept), feed, [feed_far])
    feed_others = [swap(feed, SECOND[name]) for name in DEALT]
    low = add_low(after(table, feed), kept, received, sums)
    far = swap(low, FAR)
    feed = place_quarters(after(table, low), feed, feed_others)
    feed_z = swap(feed, FIRST["z"])
    feed_x = swap(feed, FIRST["x"])
    low, sums = add_far(after(table, feed), low, far, EXTRA)
    low = place(table, VZ, low, swap(low, SECOND["z"]))
    other = swap(low, SECOND["x"])
    feed_xz = swap(after(feed_z, low), FIRST["x"])
    attention = place(table, VX, low, other, sums)
    attentions = [attention, *send_round(attention)]
    feeds = [feed, feed_z, feed_x, feed_xz]
    feeds += [swap(after(array, attention), CORE) for array in feeds]
    fc_grad, proj_grad = unpack_feed(after(table, attention), feeds)
    attentions = attentions + [swap(array, CORE) for array in attentions]
    qkv_grad, out_grad, *vectors = unpack_attention(after(table, fc_grad), attentions)
    return (
        result,
        input_grad,
        vectors[0],
        vectors[1],
        qkv_grad,
        vectors[2],
        vectors[3],
        out_grad,
        vectors[4],
        vectors[5],
        vectors[6],
        fc_grad,
        vectors[8],
        proj_grad,
        vectors[7],
    )


def solution(mesh):
    rows = P(("group", "replica"), None)
    vector = P("group")
    matrix = P("group", None)
    vectors_in = (vector, vector, matrix, vector, vector, matrix, vector, vector, vector, matrix, vector, matrix, vector)
    return jax.shard_map(
        shards,
        mesh=mesh,
        in_specs=(rows, rows) + vectors_in + (rows,),
        out_specs=(rows, rows) + vectors_in,
        check_vma=False,
    )
```

```python
import math

import jax
import jax.numpy as jnp
import numpy as np
from jax import lax
from jax.experimental import pallas as pl
from jax.experimental.pallas import tpu as pltpu
from jax.sharding import PartitionSpec as P

D = 1024
HEADS = 16
BATCH = 8
HEAD_DIM = 64
ROWS = 128
BOTH = 2 * ROWS
EXTRA = 16

norm_epsilon = 1e-05
masked_score = -1e30
gelu_factor = 0.7978845608028654
score_scale = 1.0 / math.sqrt(HEAD_DIM)

f32 = jnp.float32
bf16 = jnp.bfloat16
AXES = ("group", "replica")
MIB = 2**20


def flat(g, yh, x, z, c):
    return (((g * 2 + yh) * 4 + x) * 4 + z) * 2 + c


def at(y, x, z, c):
    return flat(y % 2, y // 2, x, z, c)


def everywhere():
    return [(g, yh, x, z, c) for g in range(2) for yh in range(2) for x in range(4) for z in range(4) for c in range(2)]


def exchange(move):
    return [(flat(g, yh, x, z, c), move(2 * yh + g, x, z, c)) for g, yh, x, z, c in everywhere()]


FIRST = {
    "g": exchange(lambda y, x, z, c: at(y ^ (1, 3)[c], x, z, c)),
    "x": exchange(lambda y, x, z, c: at(y, x ^ (1, 3)[c], z, c)),
    "z": exchange(lambda y, x, z, c: at(y, x, z ^ (1, 3)[c], c)),
    "xz": exchange(lambda y, x, z, c: at(y, x ^ (1, 3)[c], z ^ (1, 3)[c], c)),
}
SECOND = {
    "x": exchange(lambda y, x, z, c: at(y, x ^ (3, 1)[c], z, c)),
    "z": exchange(lambda y, x, z, c: at(y, x, z ^ (3, 1)[c], c)),
    "xz": exchange(lambda y, x, z, c: at(y, x ^ (3, 1)[c], z ^ (3, 1)[c], c)),
}
FAR = exchange(lambda y, x, z, c: at(y ^ 2, x, z, c))
CORE = exchange(lambda y, x, z, c: at(y, x, z, c ^ 1))


def swap(array, pairs):
    return lax.ppermute(array, AXES, pairs)


def after(value, *others):
    return lax.optimization_barrier((value, others))[0]


G, C, UX, UZ, VX, VZ = range(6)
PIECE = 6
QUARTER = 9
NUMBERS = 16


def numbers():
    rows = []
    for g, yh, x, z, c in everywhere():
        xs = ((x % 2) ^ (x // 2), x // 2)
        zs = ((z % 2) ^ (z // 2), z // 2)
        ux, vx, uz, vz = xs[c], xs[1 - c], zs[c], zs[1 - c]
        base = (1 - g) * 512
        row = [g, c, ux, uz, vx, vz, g * 512, base + c * 256, base + (1 - c) * 256]
        row += [base + ((ux ^ rx) * 2 + (uz ^ rz)) * 128 for rx in range(2) for rz in range(2)]
        rows.append(row + [0] * (NUMBERS - len(row)))
    return np.array(rows, np.int32)


def cost(us):
    return pl.CostEstimate(flops=0, bytes_accessed=int(us * 3.69e6), transcendentals=0)


def shape(dims, dtype):
    return jax.ShapeDtypeStruct(dims, dtype)


def dot(left, right):
    return jnp.dot(left, right, preferred_element_type=f32)


def rows_dot(left, right):
    return lax.dot_general(left, right, (((0,), (0,)), ((), ())), preferred_element_type=f32)


def dot_rows(left, right):
    return lax.dot_general(left, right, (((1,), (1,)), ((), ())), preferred_element_type=f32)


def span(start, size):
    return pl.ds(pl.multiple_of(start, size), size)


def norm_parts(values):
    center = jnp.mean(values, axis=-1, keepdims=True)
    centered = values - center
    variance = jnp.mean(centered * centered, axis=-1, keepdims=True)
    scale = lax.rsqrt(variance + norm_epsilon)
    return centered * scale, scale


def norm_back(normal, scale, grad):
    return scale * (
        grad
        - jnp.mean(grad, axis=-1, keepdims=True)
        - normal * jnp.mean(grad * normal, axis=-1, keepdims=True)
    )


def over(values):
    return jnp.sum(values, axis=0, keepdims=True)


MADE = []


def stepped(body, steps, table, operands, in_specs, outputs, out_specs, estimate, scratch=(), limit=32, near=False):
    operands = [
        pltpu.with_memory_space_constraint(array, pltpu.HBM)
        if not near and array.size >= 32768 and not any(array is made for made in MADE)
        else array
        for array in operands
    ]
    results = pl.pallas_call(
        body,
        grid_spec=pltpu.PrefetchScalarGridSpec(
            num_scalar_prefetch=1,
            grid=(steps,),
            in_specs=in_specs,
            out_specs=out_specs,
            scratch_shapes=list(scratch),
        ),
        out_shape=outputs,
        compiler_params=pltpu.CompilerParams(vmem_limit_bytes=limit * MIB),
        cost_estimate=estimate,
    )(table, *operands)
    MADE.extend(jax.tree.leaves(results))
    return results


def block(dims, place):
    return pl.BlockSpec(dims, place)


def fixed(dims, row=0, column=0):
    place = (row, column) if len(dims) == 2 else (0,) * len(dims)
    return pl.BlockSpec(dims, lambda j, t: place)


FIRST_ROWS = 256 + ROWS + EXTRA


def pack(table, inputs, w_out, w_fc, vectors):
    def body(t, in_ref, out_ref, low_ref, high_ref, *refs):
        first, fc_part = refs[9:]
        first[:256, :] = out_ref[...]
        first[256:384, :] = in_ref[...]
        rows = [
            jnp.concatenate([refs[k + n][...].astype(f32).reshape(1, 512) for n in range(2)], 1) for k in range(0, 8, 2)
        ]
        rows += [refs[8][pl.ds(1024 * k, 1024)].astype(f32).reshape(1, 1024) for k in range(2)]
        first[384:, :] = jnp.concatenate([*rows, jnp.zeros((EXTRA - 6, D), f32)], 0).astype(bf16)
        fc_part[:, :1024] = low_ref[...]
        fc_part[:, 1024:] = high_ref[...]

    outputs = [shape((FIRST_ROWS, D), bf16), shape((128, 2048), bf16)]
    return stepped(
        body,
        1,
        table,
        (inputs, w_out, w_fc, w_fc, *vectors),
        [
            fixed((ROWS, D)),
            block((256, D), lambda j, t: (t[C], 0)),
            block((128, 1024), lambda j, t: (t[UX] * 2 + t[UZ], t[C])),
            block((128, 1024), lambda j, t: (t[UX] * 2 + t[UZ], 2 + t[C])),
        ]
        + [pl.BlockSpec(v.shape, lambda j, t: (0,)) for v in vectors],
        outputs,
        [fixed(o.shape) for o in outputs],
        cost(3.6),
        limit=60,
    )


def spread(table, own, other):
    def body(t, own_ref, other_ref, full_ref, bias_ref):
        first = t[G] == 0
        mine = own_ref[...].astype(f32)[:8]
        theirs = other_ref[...].astype(f32)[:8]
        low = jnp.where(first, mine, theirs)
        high = jnp.where(first, theirs, mine)
        for k in range(8):
            half = slice(512 * (k % 2), 512 * (k % 2) + 512)
            full_ref[k : k + 1, :512] = low[k // 2 : k // 2 + 1, half]
            full_ref[k : k + 1, 512:] = high[k // 2 : k // 2 + 1, half]
        second = t[C] == 1
        bias_ref[:, :1024] = jnp.where(second, low[5:6], low[4:5])
        bias_ref[:, 1024:] = jnp.where(second, high[5:6], high[4:5])

    tail = fixed((EXTRA, D), 384 // EXTRA)
    return stepped(
        body,
        1,
        table,
        (own, other),
        [tail, tail],
        [shape((8, D), f32), shape((1, 2048), f32)],
        [fixed((8, D)), fixed((1, 2048))],
        cost(1),
    )


def project(table, own, other, gain, shift, w_qkv):
    width = 512

    def body(t, own_ref, other_ref, gain_ref, shift_ref, w_ref, mine_ref, theirs_ref, normed_ref):
        @pl.when(pl.program_id(0) == 0)
        def _():
            half = span(t[PIECE], 512)
            scale = gain_ref[...].astype(f32).reshape(1, 512)
            offset = shift_ref[...].astype(f32).reshape(1, 512)
            for k, ref in enumerate((own_ref, other_ref)):
                values = ref[...].astype(f32)
                center = jnp.mean(values, axis=-1, keepdims=True)
                centered = values - center
                variance = jnp.mean(centered * centered, axis=-1, keepdims=True)
                part = (ref[:, half].astype(f32) - center) * lax.rsqrt(variance + norm_epsilon)
                normed_ref[k * ROWS : (k + 1) * ROWS, :] = (part * scale + offset).astype(bf16)

        total = dot(normed_ref[...], w_ref[...])
        mine_ref[...] = total[:ROWS]
        theirs_ref[...] = total[ROWS:].astype(bf16)

    step = lambda j, t: (0, j)
    vector = pl.BlockSpec((512,), lambda j, t: (0,))
    return stepped(
        body,
        6,
        table,
        (own, other, gain, shift, w_qkv),
        [fixed((ROWS, D), 2), fixed((ROWS, D), 2), vector, vector, block((512, width), step)],
        [shape((ROWS, 3 * D), f32), shape((ROWS, 3 * D), bf16)],
        [block((ROWS, width), step), block((ROWS, width), step)],
        cost(8),
        [pltpu.VMEM((BOTH, 512), bf16)],
    )


def admitted(segments_ref):
    across = jnp.broadcast_to(segments_ref[...], (ROWS, ROWS))
    down = across.T
    row = lax.broadcasted_iota(jnp.int32, (ROWS, ROWS), 0)
    column = lax.broadcasted_iota(jnp.int32, (ROWS, ROWS), 1)
    return (row >= column) & (across == down)


def cut_heads(ref, first, heads):
    return [ref[:, first + head * HEAD_DIM : first + (head + 1) * HEAD_DIM] for head in heads]


def head_probs(projected_ref, heads, allowed):
    queries, keys, values = (cut_heads(projected_ref, k * D, heads) for k in range(3))
    scores = [jnp.where(allowed, dot_rows(q, k) * score_scale, masked_score) for q, k in zip(queries, keys)]
    weights = [jnp.exp(x - jnp.max(x, axis=-1, keepdims=True)) for x in scores]
    return queries, keys, values, [x / jnp.sum(x, axis=-1, keepdims=True) for x in weights]


def mix(table, mine, theirs, full, segments):
    def body(t, mine_ref, theirs_ref, full_ref, seg_ref, p_ref, mixture_ref):
        for k, row in ((0, 2), (1, None), (2, 3)):
            columns = slice(k * D, (k + 1) * D)
            total = mine_ref[:, columns] + theirs_ref[:, columns].astype(f32)
            if row is not None:
                total += full_ref[row : row + 1, :]
            p_ref[:, columns] = total.astype(bf16)
        allowed = admitted(seg_ref)
        _, _, values, probs = head_probs(p_ref, range(HEADS), allowed)
        outputs = [dot(p.astype(bf16), v).astype(bf16) for p, v in zip(probs, values)]
        for head, output in enumerate(outputs):
            mixture_ref[:, head * HEAD_DIM : (head + 1) * HEAD_DIM] = output

    return stepped(
        body,
        1,
        table,
        (mine, theirs, full, segments),
        [fixed((ROWS, 3 * D)), fixed((ROWS, 3 * D)), fixed((8, D)), fixed((1, ROWS))],
        [shape((ROWS, 3 * D), bf16), shape((ROWS, D), bf16)],
        [fixed((ROWS, 3 * D)), fixed((ROWS, D))],
        cost(8.1),
    )


def settle(table, mixture, inputs, full, w_out, near, far):
    def body(t, mixture_ref, in_ref, full_ref, own, a, b, side_ref, residual_ref):
        total = dot(mixture_ref[:, span(t[PIECE], 512)], own[...])
        for k, ref in enumerate((a, b)):
            total += dot(mixture_ref[:, span(t[PIECE + 1 + k], 256)], ref[...])
        residual = in_ref[...].astype(f32) + (total + full_ref[4:5, :])
        residual_ref[...] = residual
        normal, _ = norm_parts(residual)
        side_ref[:, :D] = (normal * full_ref[5:6, :] + full_ref[6:7, :]).astype(bf16)
        side_ref[:, D:] = mixture_ref[...]

    return stepped(
        body,
        1,
        table,
        (mixture, inputs, full, w_out, near, far),
        [fixed((ROWS, D)), fixed((ROWS, D)), fixed((8, D)), fixed((512, D)), fixed((256, D)), fixed((256, D))],
        [shape((ROWS, 2 * D), bf16), shape((ROWS, D), f32)],
        [fixed((ROWS, 2 * D)), fixed((ROWS, D))],
        cost(3),
    )


def feed_forward(table, side, early, w_fc, fc_others, bias, w_proj, proj_others):
    def body(t, side_ref, cot_ref, bias_ref, w_fc, near_fc, z_fc, x_fc, w_proj, first_proj, second_proj, *refs):
        hidden_ref, grad_ref, sums_ref, back_mine, back_theirs, out_mine, out_theirs = refs[:7]
        fc_own, fc_rest, proj_own, proj_rest, rest_ref, slope_ref, sems = refs[7:]
        low, high = span(t[C] * 1024, 1024), span(2048 + t[C] * 1024, 1024)
        copies = [
            (w_fc.at[:, low], fc_own.at[:, :1024]),
            (w_fc.at[:, high], fc_own.at[:, 1024:]),
            (near_fc, fc_rest.at[:128]),
            (z_fc, fc_rest.at[128:256]),
            (x_fc, fc_rest.at[256:]),
            (w_proj.at[low], proj_own),
            (first_proj, proj_rest.at[:512]),
            (second_proj, proj_rest.at[512:]),
        ]
        copies = [pltpu.make_async_copy(src, dst, sems.at[k]) for k, (src, dst) in enumerate(copies)]
        for copy in copies:
            copy.start()
        for i in range(4):
            rest_ref[:, 128 * i : 128 * (i + 1)] = side_ref[:, span(t[QUARTER + i], 128)]
        own = side_ref[:, span(t[PIECE], 512)]
        for copy in copies[:5]:
            copy.wait()
        for n in range(4):
            here = slice(512 * n, 512 * (n + 1))
            values = dot(own, fc_own[:, here]) + dot(rest_ref[...], fc_rest[:, here]) + bias_ref[:, here]
            square = values * values
            inner = jnp.tanh(gelu_factor * values * (1.0 + 0.044715 * square))
            outer = 0.5 * (1.0 + inner)
            hidden_ref[:, here] = (values * outer).astype(bf16)
            slope_ref[:, here] = outer + values * outer * (1.0 - inner) * gelu_factor * (1.0 + 3.0 * 0.044715 * square)
        for copy in copies[5:]:
            copy.wait()
        for group, weights in ((t[G], proj_own), (1 - t[G], proj_rest)):
            for n in range(2):
                columns = span(group * 1024 + n * 512, 512)
                grad = (dot_rows(cot_ref[...], weights[512 * n : 512 * (n + 1), :]) * slope_ref[:, columns]).astype(bf16)
                grad_ref[:, columns] = grad
                sums_ref[:, columns] = over(grad.astype(f32))
        total = dot_rows(grad_ref[...], fc_own[...])
        back_mine[:, span(t[PIECE], 512)] = total[:ROWS]
        back_theirs[:, span(t[PIECE], 512)] = total[ROWS:]
        total = dot_rows(grad_ref[...], fc_rest[...])
        for i in range(4):
            back_mine[:, span(t[QUARTER + i], 128)] = total[:ROWS, 128 * i : 128 * (i + 1)]
            back_theirs[:, span(t[QUARTER + i], 128)] = total[ROWS:, 128 * i : 128 * (i + 1)]
        for n in range(2):
            here = slice(512 * n, 512 * (n + 1))
            total = dot(hidden_ref[:, span(t[G] * 1024, 1024)], proj_own[:, here])
            total += dot(hidden_ref[:, span((1 - t[G]) * 1024, 1024)], proj_rest[:, here])
            out_mine[:, here] = total[:ROWS]
            out_theirs[:, here] = total[ROWS:]

    anywhere = pl.BlockSpec(memory_space=pl.ANY)
    square = fixed((ROWS, D))
    return stepped(
        body,
        1,
        table,
        (side, early, bias, w_fc, *fc_others, w_proj, *proj_others),
        [fixed((BOTH, D)), fixed((BOTH, D)), fixed((1, 2048))] + [anywhere] * 7,
        [shape((BOTH, 2048), bf16), shape((BOTH, 2048), bf16), shape((1, 2048), f32)] + [shape((ROWS, D), f32)] * 4,
        [fixed((BOTH, 2048)), fixed((BOTH, 2048)), fixed((1, 2048)), square, square, square, square],
        cost(12),
        [pltpu.VMEM((512, 2048), bf16)] * 2
        + [pltpu.VMEM((1024, D), bf16)] * 2
        + [pltpu.VMEM((BOTH, 512), bf16), pltpu.VMEM((BOTH, 2048), f32), pltpu.SemaphoreType.DMA((8,))],
        limit=48,
    )


def first_norms(table, pieces, full):
    def body(t, *refs):
        full_ref, normed_ref = refs[4:]
        for i, ref in enumerate(refs[:4]):
            normal, _ = norm_parts(ref[...].astype(f32))
            normed_ref[i * BOTH : (i + 1) * BOTH, :] = (normal * full_ref[0:1, :] + full_ref[1:2, :]).astype(bf16)

    return stepped(
        body, 1, table, (*pieces, full), [fixed((BOTH, D), 0, 1)] * 4 + [fixed((8, D))],
        shape((4 * BOTH, D), bf16), fixed((4 * BOTH, D)), cost(4),
    )


def attend_back(table, mine, theirs, residual, cotangent, full, projected, segments, w_out, near, far):
    def body(
        t, mine_ref, theirs_ref, res_ref, cot_ref, full_ref, p_ref, seg_ref, own, a, b,
        grad_ref, dealt_ref, sums_ref, mix_ref,
    ):
        normal, scale = norm_parts(res_ref[...])
        grad_normed = mine_ref[...] + theirs_ref[...]
        grad_output = cot_ref[...].astype(f32)
        grad = grad_output + norm_back(normal, scale, grad_normed * full_ref[5:6, :])
        grad_ref[...] = grad
        low = grad.astype(bf16)
        for k in range(8):
            dealt_ref[k // 4, :, 512 * (k % 4) + 384 : 512 * (k % 4) + 512] = low[:, 128 * k : 128 * (k + 1)]
        sums_ref[0:1, :] = over(grad)
        sums_ref[1:2, :] = over(grad_normed * normal)
        sums_ref[2:3, :] = over(grad_normed)
        sums_ref[3:4, :] = over(grad_output)
        sums_ref[4:, :] = jnp.zeros((4, D), f32)
        mix_ref[:, span(t[PIECE], 512)] = dot_rows(low, own[...]).astype(bf16)
        for k, ref in enumerate((a, b)):
            mix_ref[:, span(t[PIECE + 1 + k], 256)] = dot_rows(low, ref[...]).astype(bf16)
        allowed = admitted(seg_ref)

        def store(number, values):
            column = 512 * (number % 24 // 6) + HEAD_DIM * (number % 6)
            dealt_ref[number // 24, :, column : column + HEAD_DIM] = values.astype(bf16)

        for first in range(0, HEADS, BATCH):
            heads = range(first, first + BATCH)
            queries, keys, values, probs = head_probs(p_ref, heads, allowed)
            grad_mix = cut_heads(mix_ref, 0, heads)
            grad_probs = [dot_rows(g, v) for g, v in zip(grad_mix, values)]
            centres = [jnp.sum(p * g, axis=-1, keepdims=True) for p, g in zip(probs, grad_probs)]
            grad_scores = [(p * (g - x)).astype(bf16) for p, g, x in zip(probs, grad_probs, centres)]
            found = (
                [dot(g, k) * score_scale for g, k in zip(grad_scores, keys)],
                [rows_dot(g, q) * score_scale for g, q in zip(grad_scores, queries)],
                [rows_dot(p.astype(bf16), g) for p, g in zip(probs, grad_mix)],
            )
            for kind, results in enumerate(found):
                for head, result in zip(heads, results):
                    store(kind * HEADS + head, result)

    square = fixed((ROWS, D))
    return stepped(
        body,
        1,
        table,
        (mine, theirs, residual, cotangent, full, projected, segments, w_out, near, far),
        [square] * 4 + [fixed((8, D)), fixed((ROWS, 3 * D)), fixed((1, ROWS))]
        + [fixed((512, D)), fixed((256, D)), fixed((256, D))],
        [shape((ROWS, D), f32), shape((2, ROWS, 2048), bf16), shape((8, D), f32)],
        [square, fixed((2, ROWS, 2048)), fixed((8, D))],
        cost(11.5),
        [pltpu.VMEM((ROWS, D), bf16)],
    )


def input_back(table, dealt, w_qkv, near, far, inputs, grad_residual, full, sums, fc_sums):
    width = 384

    def body(t, grad_ref, own, a, b, in_ref, res_ref, full_ref, early_ref, fc_ref, out_ref, sums_ref, total_ref, bias_ref):
        j = pl.program_id(0)
        grad = grad_ref[0, :, :width]

        @pl.when(j == 0)
        def _():
            total_ref[...] = jnp.zeros((ROWS, D), f32)

        offset = 0
        for ref in (own, a, b):
            size = ref.shape[0]
            total_ref[:, offset : offset + size] += dot_rows(grad, ref[...])
            offset += size
        bias_ref[:, span(j * width, width)] = over(grad.astype(f32))

        @pl.when(j == 7)
        def _():
            offset = 0
            for k, size in enumerate((512, 256, 256)):
                out_ref[:, span(t[PIECE + k], size)] = total_ref[:, offset : offset + size]
                offset += size
            grad_normed = out_ref[...]
            normal, scale = norm_parts(in_ref[...].astype(f32))
            gain_sums = over(grad_normed * normal)
            shift_sums = over(grad_normed)
            out_ref[...] = res_ref[...] + norm_back(normal, scale, grad_normed * full_ref[0:1, :])
            row = lax.broadcasted_iota(jnp.int32, (4, 512), 0)
            for g in range(2):
                half = slice(512 * g, 512 * (g + 1))
                sums_ref[16 * g : 16 * g + 1, :] = gain_sums[:, half]
                sums_ref[16 * g + 1 : 16 * g + 2, :] = shift_sums[:, half]
                sums_ref[16 * g + 2 : 16 * g + 3, :] = bias_ref[:, 512 * g : 512 * (g + 1)]
                sums_ref[16 * g + 3 : 16 * g + 4, :] = bias_ref[:, 2048 + 512 * g : 2048 + 512 * (g + 1)]
                sums_ref[16 * g + 4 : 16 * g + 8, :] = early_ref[0:4, half]
                units = [fc_ref[:, 1024 * g + 512 * (k % 2) : 1024 * g + 512 * (k % 2) + 512] for k in range(4)]
                sums_ref[16 * g + 8 : 16 * g + 12, :] = jnp.where(row // 2 == t[C], jnp.concatenate(units, 0), 0.0)
                sums_ref[16 * g + 12 : 16 * g + 16, :] = jnp.zeros((4, 512), f32)

    step = lambda j, t: (0, j)
    return stepped(
        body,
        8,
        table,
        (dealt, w_qkv, near, far, inputs, grad_residual, full, sums, fc_sums),
        [pl.BlockSpec((1, ROWS, 512), lambda j, t: (j // 4, 0, j % 4)), block((512, width), step)]
        + [block((256, width), step)] * 2
        + [fixed((ROWS, D)), fixed((ROWS, D)), fixed((8, D)), fixed((8, D)), fixed((1, 2048))],
        [shape((ROWS, D), f32), shape((2 * EXTRA, 512), f32)],
        [fixed((ROWS, D)), fixed((2 * EXTRA, 512))],
        cost(9.2),
        [pltpu.VMEM((ROWS, D), f32), pltpu.VMEM((1, 3 * D), f32)],
    )


def piece_specs(pieces, width, number):
    specs, operands = [], []
    for array, row, column in pieces:
        specs.append(
            pl.BlockSpec(
                (BOTH, width),
                lambda j, t, row=row, column=column: (row(t) if callable(row) else row, column + number(j, t)),
            )
        )
        operands.append(array)
    return specs, operands


def sum_dots(lefts, rights, columns=slice(None)):
    total = rows_dot(lefts[0][...], rights[0][:, columns])
    for left, right in zip(lefts[1:], rights[1:]):
        total += rows_dot(left[...], right[:, columns])
    return total


def deal_feed(table, hidden, grad_pre):
    def body(t, hidden_ref, grad_ref, *outs):
        for j, out in enumerate(outs):
            away = 3 - j
            bx, bz = (away // 2) ^ t[UX], (away % 2) ^ t[UZ]
            for g in range(2):
                out[:, 256 * g : 256 * (g + 1)] = hidden_ref[:, span(g * 1024 + (bx * 2 + bz) * 256, 256)]
            out[:, 512:] = grad_ref[:, span((bx * 2 + bz) * 512, 512)]

    return stepped(
        body, 1, table, (hidden, grad_pre), [fixed((BOTH, 2048))] * 2, [shape((BOTH, D), bf16)] * 4,
        [fixed((BOTH, D))] * 4, cost(0.8), near=True,
    )


def deal_attention(table, mine, theirs, mixtures):
    def body(t, mine_ref, theirs_ref, mix_ref, *outs):
        for j, out in enumerate(outs):
            away = 3 - j
            columns = span((((away // 2) ^ t[UX]) * 2 + ((away % 2) ^ t[UZ])) * 512, 512)
            out[:ROWS, :512] = mine_ref[0, :, columns]
            out[ROWS:, :512] = theirs_ref[:, columns]
            out[:, 512:] = mix_ref[...]

    return stepped(
        body, 1, table, (mine, theirs, mixtures),
        [pl.BlockSpec((1, ROWS, 2048), lambda j, t: (t[C], 0, 0)), fixed((ROWS, 2048)), fixed((BOTH, D))],
        [shape((BOTH, 512 + D), bf16)] * 4, [fixed((BOTH, 512 + D))] * 4, cost(1), near=True,
    )


def quarter(j, t):
    away = 3 - j
    return ((away // 2) ^ t[VX]) * 2 + ((away % 2) ^ t[VZ])


def half_rows(j, t):
    return jnp.where(j == 0, 1 - t[VX], t[VX])


def feed_specs(normeds, grads, hiddens, cotangents, rows, width, features, units, columns):
    specs, operands = [], []
    for pieces, size, number in (
        (normeds, rows, features),
        (grads, 512, lambda j, t: 1),
        (hiddens, 256, units),
        (cotangents, width, columns),
    ):
        more, arrays = piece_specs(pieces, size, number)
        specs += more
        operands += arrays
    return specs, operands


def feed_sent(table, normeds, grads, hiddens, cotangents):
    specs, operands = feed_specs(
        normeds, grads, hiddens, cotangents, 256, 512,
        lambda j, t: (1 - t[G]) * 2 + j, lambda j, t: 1 - t[G], lambda j, t: j,
    )

    def body(t, *refs):
        out = refs[-1]
        out[:, :512] = sum_dots(refs[:4], refs[4:8]).astype(bf16)
        units = sum_dots(refs[8:12], refs[12:16]).astype(bf16)
        for q in range(2):
            rows, columns = slice(128 * q, 128 * (q + 1)), slice(256 * q, 256 * (q + 1))
            out[rows, 512:768] = units[:128, columns]
            out[rows, 768:] = units[128:, columns]

    return stepped(
        body, 2, table, operands, specs, shape((512, D), bf16), block((256, D), lambda j, t: (j, 0)), cost(4.3),
    )


def feed_total(table, normeds, grads, hiddens, cotangents, received):
    specs, operands = feed_specs(
        normeds, grads, hiddens, cotangents, 128, 256,
        lambda j, t: t[G] * 4 + quarter(j, t), lambda j, t: t[G], quarter,
    )

    def body(t, *refs):
        received_ref = refs[16]
        outs = refs[17:]
        j = pl.program_id(0)
        got = received_ref[...].astype(f32)
        left = sum_dots(refs[:4], refs[4:8]) + got[:, :512]
        right = sum_dots(refs[8:12], refs[12:16])
        top = right[:128] + got[:, 512:768]
        low = right[128:] + got[:, 768:]
        for k, out in enumerate(outs):

            @pl.when(j == k)
            def _():
                out[:, :512] = left.astype(out.dtype)
                out[:, 512:768] = top.astype(out.dtype)
                out[:, 768:] = low.astype(out.dtype)

    return stepped(
        body,
        4,
        table,
        operands + [received],
        specs + [block((128, D), lambda j, t: (quarter(j, t), 0))],
        [shape((128, D), bf16)] * 3 + [shape((128, D), f32)],
        [fixed((128, D))] * 4,
        cost(5),
    )


def attention_sent(table, normeds, mixtures, grads, sums):
    specs, operands = [], []
    for pieces in (normeds, mixtures):
        more, arrays = piece_specs(pieces, 512, lambda j, t: 1 - t[G])
        specs += more
        operands += arrays
    more, arrays = piece_specs(grads, 512, lambda j, t: 0)

    def body(t, *refs):
        sums_ref, out_ref = refs[12:]
        out_ref[:512, :384] = sum_dots(refs[:4], refs[8:12], slice(0, 384)).astype(bf16)
        out_ref[:512, 384:] = sum_dots(refs[4:8], refs[8:12], slice(384, 512)).astype(bf16)
        out_ref[512:, :] = sums_ref[...].astype(bf16)

    return stepped(
        body,
        1,
        table,
        operands + arrays + [sums],
        specs + more + [block((EXTRA, 512), lambda j, t: (1 - t[G], 0))],
        shape((512 + EXTRA, 512), bf16),
        fixed((512 + EXTRA, 512)),
        cost(3.3),
    )


def attention_total(table, normeds, mixtures, grads, received, sums):
    specs, operands = [], []
    for pieces in (normeds, mixtures):
        more, arrays = piece_specs(pieces, 256, lambda j, t: t[G] * 2 + half_rows(j, t))
        specs += more
        operands += arrays
    more, arrays = piece_specs(grads, 512, lambda j, t: 0)

    def body(t, *refs):
        received_ref, tail_ref, sums_ref, sent_ref, kept_ref, total_ref = refs[12:]
        j = pl.program_id(0)
        got = received_ref[...].astype(f32)
        left = sum_dots(refs[:4], refs[8:12], slice(0, 384)) + got[:, :384]
        right = sum_dots(refs[4:8], refs[8:12], slice(384, 512)) + got[:, 384:]

        @pl.when(j == 0)
        def _():
            sent_ref[:256, :384] = left.astype(bf16)
            sent_ref[:256, 384:] = right.astype(bf16)
            total = sums_ref[...] + tail_ref[...].astype(f32)
            total_ref[...] = total
            sent_ref[256:, :] = total.astype(bf16)

        @pl.when(j == 1)
        def _():
            kept_ref[:, :384] = left
            kept_ref[:, 384:] = right

    return stepped(
        body,
        2,
        table,
        operands + arrays + [received, received, sums],
        specs
        + more
        + [
            block((256, 512), lambda j, t: (half_rows(j, t), 0)),
            fixed((EXTRA, 512), 512 // EXTRA),
            block((EXTRA, 512), lambda j, t: (t[G], 0)),
        ],
        [shape((256 + EXTRA, 512), bf16), shape((256, 512), f32), shape((EXTRA, 512), f32)],
        [fixed((256 + EXTRA, 512)), fixed((256, 512)), fixed((EXTRA, 512))],
        cost(3.9),
    )


def add_up(table, kept, received):
    def body(t, kept_ref, *refs):
        total = kept_ref[...].astype(f32)
        for ref in refs[:-1]:
            total += ref[...].astype(f32)
        refs[-1][...] = total.astype(bf16)

    operands = [kept, *received]
    return stepped(
        body, 1, table, operands, [fixed(a.shape) for a in operands], shape(kept.shape, bf16), fixed(kept.shape),
        cost(0.7),
        near=True,
    )


def place_quarters(table, mine, others):
    width = mine.shape[1]
    extra = mine.shape[0] - 128

    def body(t, *refs):
        out = refs[-1]
        for j, ref in enumerate(refs[:-1]):
            out[span(quarter(j, t) * 128, 128), :] = ref[:128, :]
        if extra:
            out[512:, :] = refs[3][128:, :]

    operands = [*others, mine]
    return stepped(
        body, 1, table, operands, [fixed(a.shape) for a in operands], shape((512 + extra, width), bf16),
        fixed((512 + extra, width)), cost(0.7),
        near=True,
    )


def add_split(table, kept, received, sums):
    rows, width = kept.shape
    half, extra = rows // 2, received.shape[0] - rows

    def body(t, kept_ref, received_ref, *refs):
        sent_ref, left_ref = refs[-3:-1] if extra else refs
        for bit, out in ((1 - t[VZ], sent_ref), (t[VZ], left_ref)):
            lines = span(bit * half, half)
            total = kept_ref[lines, :] + received_ref[lines, :].astype(f32)
            out[:half, :] = total.astype(out.dtype)
        if extra:
            total = refs[0][...] + received_ref[rows:, :].astype(f32)
            refs[-1][...] = total
            sent_ref[half:, :] = total.astype(bf16)

    outputs = [shape((half + extra, width), bf16), shape((half, width), f32)]
    if extra:
        outputs.append(shape((extra, width), f32))
    operands = [kept, received] + ([sums] if extra else [])
    return stepped(
        body, 1, table, operands, [fixed(a.shape) for a in operands], outputs, [fixed(o.shape) for o in outputs],
        cost(0.7),
        near=True,
    )


def add_low(table, kept, received, sums):
    rows, width = kept.shape
    extra = received.shape[0] - rows

    def body(t, kept_ref, received_ref, *refs):
        out = refs[-1]
        out[:rows, :] = (kept_ref[...] + received_ref[:rows, :].astype(f32)).astype(bf16)
        if extra:
            out[rows:, :] = (refs[0][...] + received_ref[rows:, :].astype(f32)).astype(bf16)

    operands = [kept, received] + ([sums] if extra else [])
    return stepped(
        body, 1, table, operands, [fixed(a.shape) for a in operands], shape(received.shape, bf16),
        fixed(received.shape), cost(0.6),
        near=True,
    )


def add_far(table, low, received, extra):
    rows, width = low.shape[0] - extra, low.shape[1]

    def body(t, low_ref, received_ref, *outs):
        total = low_ref[...].astype(f32) + received_ref[...].astype(f32)
        outs[0][...] = total[:rows].astype(bf16)
        if extra:
            outs[1][...] = total[rows:].astype(bf16)

    outputs = [shape((rows, width), bf16)] + ([shape((extra, width), bf16)] if extra else [])
    return stepped(
        body, 1, table, (low, received), [fixed(low.shape)] * 2, outputs, [fixed(o.shape) for o in outputs],
        cost(0.6),
        near=True,
    )


def place(table, bit, mine, other, sums=None):
    rows, width = mine.shape
    extra = 0 if sums is None else EXTRA

    def body(t, mine_ref, other_ref, *refs):
        out = refs[-1]
        out[span(t[bit] * rows, rows), :] = mine_ref[...]
        out[span((1 - t[bit]) * rows, rows), :] = other_ref[...]
        if extra:
            out[2 * rows :, :] = refs[0][...]

    operands = [mine, other] + ([sums] if extra else [])
    return stepped(
        body, 1, table, operands, [fixed(a.shape) for a in operands], shape((2 * rows + extra, width), bf16),
        fixed((2 * rows + extra, width)), cost(0.6),
        near=True,
    )


def targets(t):
    found = []
    for k in range(8):
        core = t[C] if k < 4 else 1 - t[C]
        ux, uz = (t[UX], t[UZ]) if k < 4 else (t[VX], t[VZ])
        found.append((core, ((k // 2 % 2) ^ ux) * 2 + ((k % 2) ^ uz)))
    return found


def unpack_feed(table, arrays):
    def body(t, *refs):
        fc_ref, proj_ref = refs[8:]
        rows = span(pl.program_id(0) * 128, 128)
        for ref, (core, number) in zip(refs, targets(t)):
            fc_ref[:, span((number // 2) * 2048 + core * 1024 + (number % 2) * 512, 512)] = ref[rows, :512].astype(f32)
            proj_ref[core * 4 + number, :128, :] = ref[rows, 512:768].astype(f32)
            proj_ref[core * 4 + number, 128:, :] = ref[rows, 768:].astype(f32)

    fc_grad, proj_grad = stepped(
        body,
        4,
        table,
        arrays,
        [pl.BlockSpec(memory_space=pltpu.VMEM)] * 8,
        [shape((512, 4096), f32), shape((8, 256, D), f32)],
        [block((128, 4096), lambda j, t: (j, 0)), pl.BlockSpec((8, 256, 256), lambda j, t: (0, 0, j))],
        cost(7),
        near=True,
    )
    return fc_grad, proj_grad.reshape(2048, D)


def unpack_attention(table, arrays):
    def body(t, *refs):
        arrays, qkv_ref, out_ref, vectors = refs[:8], refs[8], refs[9], refs[10:]
        rows = span(pl.program_id(0) * 128, 128)
        for ref, (core, number) in zip(arrays, targets(t)):
            qkv_ref[:, span((core * 4 + number) * 384, 384)] = ref[rows, :384].astype(f32)
            out_ref[:, span((core * 4 + number) * 128, 128)] = ref[rows, 384:].astype(f32)

        @pl.when(pl.program_id(0) == 0)
        def _():
            sums = arrays[0][512:, :].astype(f32)
            for ref in arrays[1:]:
                sums += ref[512:, :].astype(f32)
            for k in range(8):
                vectors[k][...] = sums[k : k + 1, :].reshape(512)
            for k in range(4):
                vectors[8][pl.ds(512 * k, 512)] = sums[8 + k : 9 + k, :].reshape(512)

    vector = pl.BlockSpec((512,), lambda j, t: (0,))
    return stepped(
        body,
        4,
        table,
        arrays,
        [pl.BlockSpec(memory_space=pltpu.VMEM)] * 8,
        [shape((512, 3 * D), f32), shape((512, D), f32)] + [shape((512,), f32)] * 8 + [shape((2048,), f32)],
        [block((128, 3 * D), lambda j, t: (j, 0)), block((128, D), lambda j, t: (j, 0))]
        + [vector] * 8
        + [pl.BlockSpec((2048,), lambda j, t: (0,))],
        cost(6),
        near=True,
    )


def cut(array, start, size, axis):
    return lax.dynamic_slice_in_dim(array, start, size, axis)


def both(upper, lower):
    return jnp.concatenate([upper, lower], 0)


def zero(t):
    return 0


ROUND = ("z", "x", "xz")
DEALT = ("xz", "x", "z")


def send_quarters(quarters):
    return [swap(array, SECOND[name]) for array, name in zip(quarters, DEALT)]


def send_round(array):
    return [swap(array, FIRST[name]) for name in ROUND]


def share(array):
    across = swap(array, FIRST["xz"])
    return [swap(array, FIRST["x"]), swap(array, FIRST["z"]), across]


def arrays_of(found):
    return [piece[0] for piece in found]


def send_dealt(dealt):
    across, over_x, over_z, own = dealt
    across = swap(across, FIRST["xz"])
    over_x = swap(over_x, FIRST["x"])
    over_z = swap(over_z, FIRST["z"])
    return [(array, 0, 0) for array in (own, over_x, over_z, across)]


def shards(
    block_input,
    segment_ids,
    ln1_gain,
    ln1_bias,
    w_qkv,
    b_query,
    b_value,
    w_out,
    b_out,
    ln2_gain,
    ln2_bias,
    w_fc,
    b_fc,
    w_proj,
    b_proj,
    cotangent,
):
    MADE.clear()
    device = lax.axis_index("group") * 64 + lax.axis_index("replica")
    table = lax.dynamic_slice(jnp.asarray(numbers()), (device, 0), (1, NUMBERS)).reshape(NUMBERS)
    c = table[C]

    first, fc_part = pack(
        table, block_input, w_out, w_fc,
        (ln1_gain, ln1_bias, b_query, b_value, b_out, ln2_gain, ln2_bias, b_proj, b_fc),
    )
    early = jnp.concatenate([cotangent, block_input], 1)
    early = both(early, swap(early, CORE))
    earlies = [early, *share(early)]
    out_near = swap(first, FIRST["g"])
    fc_near = swap(after(fc_part, first), FIRST["g"])
    proj_parts = [cut(after(w_proj, first), c * 1024 + 512 * k, 512, 0) for k in range(2)]
    qkv_part = cut(after(w_qkv, first), c * 256, 256, 0)
    part_mine, part_theirs = project(
        after(table, early, proj_parts, qkv_part, fc_near), first, out_near, ln1_gain, ln1_bias, w_qkv
    )
    part_theirs = swap(part_theirs, FIRST["g"])
    out_far = swap(after(out_near, part_mine), CORE)
    full, fc_bias = spread(after(table, part_mine, out_far, fc_near), first, out_near)
    fc_z = swap(after(fc_near, part_mine), FIRST["z"])
    fc_pair = both(fc_near, fc_z)
    fc_x = swap(fc_pair, FIRST["x"])
    fc_others = [fc_near, fc_z, fc_x]

    projected, mixture = mix(after(table, fc_pair), part_mine, part_theirs, full, segment_ids)
    proj_first = swap(after(proj_parts[0], part_theirs), FIRST["g"])
    side, residual = settle(after(table, earlies, fc_x, proj_first), mixture, block_input, full, w_out, out_near, out_far)
    proj_second = swap(after(proj_parts[1], part_theirs), FIRST["g"])
    side_theirs = swap(side, CORE)
    side = after(side, proj_second)
    normed_twos = both(side[:, :D], side_theirs[:, :D])
    mixtures = both(side[:, D:], side_theirs[:, D:])
    sides = [normed_twos, *share(normed_twos)]
    qkv_near = swap(after(qkv_part, proj_first), FIRST["g"])

    hidden, grad_pre, fc_sums, back_mine, back_theirs, output_mine, output_theirs = feed_forward(
        table, normed_twos, early, w_fc, fc_others, fc_bias, w_proj, (proj_first, proj_second)
    )
    back_theirs = swap(back_theirs, CORE)
    feed_dealt = deal_feed(after(table, sides, qkv_near), hidden, grad_pre)
    feeds = send_dealt(feed_dealt)
    normed_ones = first_norms(after(table, feed_dealt), earlies, full)

    grad_residual, dealt, sums = attend_back(
        after(table, normed_ones), back_mine, back_theirs, residual, cotangent, full,
        projected, segment_ids, w_out, out_near, out_far,
    )
    result = (residual + (output_mine + swap(output_theirs, CORE) + full[7:8])).astype(bf16)
    dealt_theirs = swap(lax.dynamic_index_in_dim(dealt, 1 - c, 0, False), CORE)
    attention_dealt = deal_attention(after(table, arrays_of(feeds)), dealt, dealt_theirs, mixtures)
    attention_grads = send_dealt(attention_dealt)
    qkv_far = swap(after(qkv_near, attention_dealt), CORE)
    feed_pieces = [
        [(array, 0, 0) for array in sides],
        feeds,
        feeds,
        [(array, 0, 0) for array in earlies],
    ]
    feed_out = feed_sent(after(table, attention_dealt), *feed_pieces)
    feed_received = swap(feed_out, FIRST["g"])
    input_grad, sums = input_back(
        after(table, feed_out), dealt, w_qkv, qkv_near, qkv_far, block_input, grad_residual, full, sums, fc_sums
    )

    normed_pieces = [(normed_ones, row, 0) for row in range(4)]
    out = attention_sent(
        after(table, sums), normed_pieces, [(array, 0, 1) for array, _, _ in attention_grads], attention_grads, sums
    )
    received = swap(out, FIRST["g"])
    *feed, feed_kept = feed_total(after(table, out), *feed_pieces, feed_received)
    feed = send_quarters(feed)
    sent, kept, sums = attention_total(
        after(table, feed_kept), normed_pieces, [(array, 0, 2) for array, _, _ in attention_grads], attention_grads, received, sums
    )
    received = swap(sent, SECOND["x"])
    feed = add_up(after(table, kept), feed_kept, feed)
    feed_far = swap(feed, FAR)
    sent, kept, sums = add_split(after(table, feed), kept, received, sums)
    received = swap(sent, SECOND["z"])
    feed = add_up(after(table, kept), feed, [feed_far])
    feed_others = [swap(feed, SECOND[name]) for name in DEALT]
    low = add_low(after(table, feed), kept, received, sums)
    far = swap(low, FAR)
    feed = place_quarters(after(table, low), feed, feed_others)
    feed_z = swap(feed, FIRST["z"])
    feed_x = swap(feed, FIRST["x"])
    low, sums = add_far(after(table, feed), low, far, EXTRA)
    low = place(table, VZ, low, swap(low, SECOND["z"]))
    other = swap(low, SECOND["x"])
    feed_xz = swap(after(feed_z, low), FIRST["x"])
    attention = place(table, VX, low, other, sums)
    attentions = [attention, *send_round(attention)]
    feeds = [feed, feed_z, feed_x, feed_xz]
    feeds += [swap(after(array, attention), CORE) for array in feeds]
    fc_grad, proj_grad = unpack_feed(after(table, attention), feeds)
    attentions = attentions + [swap(array, CORE) for array in attentions]
    qkv_grad, out_grad, *vectors = unpack_attention(after(table, fc_grad), attentions)
    return (
        result,
        input_grad,
        vectors[0],
        vectors[1],
        qkv_grad,
        vectors[2],
        vectors[3],
        out_grad,
        vectors[4],
        vectors[5],
        vectors[6],
        fc_grad,
        vectors[8],
        proj_grad,
        vectors[7],
    )


def solution(mesh):
    rows = P(("group", "replica"), None)
    vector = P("group")
    matrix = P("group", None)
    vectors_in = (vector, vector, matrix, vector, vector, matrix, vector, vector, vector, matrix, vector, matrix, vector)
    return jax.shard_map(
        shards,
        mesh=mesh,
        in_specs=(rows, rows) + vectors_in + (rows,),
        out_specs=(rows, rows) + vectors_in,
        check_vma=False,
    )
```
